32 devices in a mesh: batch: 8 (over z, y), rep: 4 (over x, core).
Axes of the slice: x: 2, y: 2, z: 4, core: 2. Of those that a mesh axis runs over, the one named last changes fastest.
Arguments:
- query_tokens: bfloat16 [256, 32, 768], P(('batch', 'rep')), may hold values from -6 to 6
- passage_tokens: bfloat16 [256, 224, 768], P(('batch', 'rep')), may hold values from -6 to 6
- query_length: int32 [256], P(('batch', 'rep')), may hold values from 8 to 32
- passage_length: int32 [256], P(('batch', 'rep')), may hold values from 56 to 224
- clusters: int32 [256], replicated, may hold values from 0 to 1999
- positives: int32 [256], P(('batch', 'rep')), may hold values from 0 to 255, each once
- w_query: bfloat16 [768, 768], replicated, may hold values from -0.21875 to 0.21875
- b_query: bfloat16 [768], replicated, may hold values from -3 to 3
- w_key: bfloat16 [768, 768], replicated, may hold values from -0.21875 to 0.21875
- w_value: bfloat16 [768, 768], replicated, may hold values from -0.21875 to 0.21875
- b_value: bfloat16 [768], replicated, may hold values from -1.1953125 to 1.1953125
- w_mix: bfloat16 [768, 768], replicated, may hold values from -2.5 to 2.5
- b_mix: bfloat16 [768], replicated, may hold values from -0.59765625 to 0.59765625
- gain_one: bfloat16 [768], replicated, may hold values from 0.5 to 1.5
- shift_one: bfloat16 [768], replicated, may hold values from -0.59765625 to 0.59765625
- w_inner: bfloat16 [768, 3072], replicated, may hold values from -0.21875 to 0.21875
- b_inner: bfloat16 [3072], replicated, may hold values from -1.1953125 to 1.1953125
- w_outer: bfloat16 [3072, 768], replicated, may hold values from -0.109375 to 0.109375
- b_outer: bfloat16 [768], replicated, may hold values from -0.59765625 to 0.59765625
- gain_two: bfloat16 [768], replicated, may hold values from 0.5 to 1.5
- shift_two: bfloat16 [768], replicated, may hold values from -0.59765625 to 0.59765625
Outputs:
- query_out: bfloat16 [256, 32, 768], P(('batch', 'rep'))
- passage_out: bfloat16 [256, 224, 768], P(('batch', 'rep'))
- mean_loss: float32 [], replicated
- query_grad: float32 [256, 32, 768], P(('batch', 'rep'))
- passage_grad: float32 [256, 224, 768], P(('batch', 'rep'))
- grad_w_query: float32 [768, 768], P('batch')
- grad_b_query: float32 [768], P('batch')
- grad_w_key: float32 [768, 768], P('batch')
- grad_w_value: float32 [768, 768], P('batch')
- grad_b_value: float32 [768], P('batch')
- grad_w_mix: float32 [768, 768], P('batch')
- grad_b_mix: float32 [768], P('batch')
- grad_gain_one: float32 [768], P('batch')
- grad_shift_one: float32 [768], P('batch')
- grad_w_inner: float32 [768, 3072], P('batch')
- grad_b_inner: float32 [3072], P('batch')
- grad_w_outer: float32 [3072, 768], P('batch')
- grad_b_outer: float32 [768], P('batch')
- grad_gain_two: float32 [768], P('batch')
- grad_shift_two: float32 [768], P('batch')
The draws below stay inside these ranges and needn't reach their ends.
Inputs may be any that keep to these rules, and one draw needn't show every extreme that they name: `positives`: each passage is the positive of exactly one query.
All inputs are finite; a program needn't handle non-finite values.
Results may differ from the reference program's by a relative error of at most 0.023.
Values may be sent and summed in bfloat16 or wider, within the bound.
No kernel may reach another device: no remote copies, remote signals or barrier semaphores. Data moves between devices by JAX's collectives and lax.ppermute only.
A program may use at most 192 MiB of HBM per device.

```python
import math
import jax
import jax.numpy as jnp
import numpy as np
from jax import lax

D = 768
HEADS = 12
HEAD = 64
FF = 3072
QLEN = 32
PLEN = 224
CLUSTERS = 2000
PAIRS = 256


def set_ends(result, own_key, low, largest):
    shape = result.shape
    index_at = [jax.random.randint(jax.random.fold_in(own_key, axis), (), 0, shape[axis]) for axis in range(len(shape))]
    result = result.at[tuple(index_at)].set(low)
    longest = shape.index(max(shape))
    index_at[longest] = (index_at[longest] + 1) % shape[longest]
    return result.at[tuple(index_at)].set(largest)


def spiked(array, key, source, target, shards_of, factor):
    owner, partner = [(jnp.arange(array.shape[dim]) // (array.shape[dim] // shards_of)).reshape([-1 if axis == dim else 1 for axis in range(array.ndim)]) for dim in (source, target)]
    chosen = jax.random.permutation(key, shards_of)[partner]
    strong = (owner == chosen) | (owner == (partner + shards_of // 2) % shards_of)
    return jnp.where(strong, factor * array, array)


def steps_of(rng, shape, cuts, least, top_value):
    loudness = 1.0
    for axis_at, parts in cuts:
        steps = jax.random.uniform(jax.random.fold_in(jax.random.fold_in(rng, 6), axis_at), (parts,), jnp.float32, least / len(cuts), top_value / len(cuts))
        loudness = loudness * jnp.repeat(jnp.exp(steps), shape[axis_at] // parts).reshape((-1,) + (1,) * (len(shape) - 1 - axis_at))
    return loudness


def cumulative_ranks(amount, skew):
    weights = [(1 << 20) // math.isqrt(rank ** skew) + 1 for rank in range(1, amount + 1)]
    scale = 1 + sum(weights) // (1 << 30)
    return np.cumsum(np.array([max(1, weight // scale) for weight in weights]))


def ranked_ids(key, dims, count, slope):
    listing = cumulative_ranks(count, slope)
    ticket = jax.random.randint(jax.random.fold_in(key, 1), dims, 0, int(listing[count - 1]))
    grade = jnp.searchsorted(jnp.asarray(listing, jnp.int32), ticket, side="right")
    return jax.random.permutation(jax.random.fold_in(key, 2), count)[grade].astype(jnp.int32)


def centred(rng, dims, width, limit, shards=(), held_as=jnp.bfloat16):
    gain = steps_of(rng, dims, shards, -0.22, 0.18) if shards else 1.0
    drawn = jax.random.normal(rng, dims, jnp.float32) * width * gain
    return jnp.minimum(jnp.maximum(drawn, -limit), limit).astype(held_as)


def bell_draw_with(rng, extent, width, reach, shards, heavy, kind=jnp.bfloat16):
    values = width * jax.random.normal(rng, extent, jnp.float32)
    if shards:
        values = values * steps_of(rng, extent, shards, -0.22, 0.18)
    return jnp.clip(spiked(values, jax.random.fold_in(rng, 3), *heavy), -reach, reach).astype(kind)


def setup_inputs(seed: int = 0) -> dict:
    key_of = jax.random.split(jax.random.key(seed), 22)
    return {
        "query_tokens": bell_draw_with(key_of[0], (PAIRS, QLEN, D), 1.0, 6.0, ((0, 32),), (0, 2, 32, 2.75)),
        "passage_tokens": bell_draw_with(key_of[1], (PAIRS, PLEN, D), 1.0, 6.0, ((0, 32),), (0, 2, 32, 2.75)),
        "query_length": set_ends(jax.random.randint(key_of[2], (PAIRS,), QLEN // 4, QLEN + 1), jax.random.fold_in(key_of[2], 1), QLEN // 4, QLEN).astype(jnp.int32),
        "passage_length": set_ends(jax.random.randint(key_of[3], (PAIRS,), PLEN // 4, PLEN + 1), jax.random.fold_in(key_of[3], 1), PLEN // 4, PLEN).astype(jnp.int32),
        "clusters": set_ends(ranked_ids(key_of[4], (PAIRS,), CLUSTERS, 2), jax.random.fold_in(key_of[4], 3), 0, CLUSTERS - 1).astype(jnp.int32),
        "positives": jax.random.permutation(key_of[5], PAIRS).astype(jnp.int32),
        "w_query": centred(key_of[6], (D, D), D ** -0.5, 0.21875),
        "b_query": centred(key_of[7], (D,), 0.5, 3.0),
        "w_key": centred(key_of[8], (D, D), D ** -0.5, 0.21875),
        "w_value": centred(key_of[9], (D, D), D ** -0.5, 0.21875),
        "b_value": centred(key_of[10], (D,), 0.2, 1.1953125),
        "w_mix": centred(key_of[11], (D, D), (D // 128) ** -0.5, 2.5),
        "b_mix": centred(key_of[12], (D,), 0.1, 0.59765625),
        "gain_one": jnp.clip(1.0 + 0.1 * jax.random.normal(key_of[13], (D,), jnp.float32), 0.5, 1.5).astype(jnp.bfloat16),
        "shift_one": centred(key_of[14], (D,), 0.1, 0.59765625),
        "w_inner": centred(key_of[15], (D, FF), D ** -0.5, 0.21875),
        "b_inner": centred(key_of[16], (FF,), 0.2, 1.1953125),
        "w_outer": centred(key_of[17], (FF, D), FF ** -0.5, 0.109375),
        "b_outer": centred(key_of[18], (D,), 0.1, 0.59765625),
        "gain_two": jnp.clip(1.0 + 0.1 * jax.random.normal(key_of[19], (D,), jnp.float32), 0.5, 1.5).astype(jnp.bfloat16),
        "shift_two": centred(key_of[20], (D,), 0.1, 0.59765625),
    }


@jax.custom_vjp
def low(v):
    return lax.optimization_barrier(v.astype(jnp.bfloat16)).astype(jnp.float32)

@jax.custom_vjp
def low_back(v):
    return v

def low_keep(v):
    return (low(v), None)

def low_pass(kept, grad):
    return (grad,)

def back_keep(v):
    return (v, None)

def back_low(kept, grad):
    return (low(grad),)
low.defvjp(low_keep, low_pass)
low_back.defvjp(back_keep, back_low)
highest = lax.Precision.HIGHEST

def rounded(values):
    return low(low_back(values))

def project(values, weight):
    return jnp.einsum('...d,de->...e', values, weight, precision=highest)

def normalize(values, gain_vec, shift_vec):
    center = values - lax.optimization_barrier(jnp.mean(values, axis=-1, keepdims=True))
    spread = lax.rsqrt(lax.optimization_barrier(jnp.mean(center * center, axis=-1, keepdims=True)) + 1e-12)
    return center * spread * gain_vec + shift_vec

def encoder_layer(inputs, lengths, params):
    w_query, b_query, w_key, w_value, b_value, w_mix, b_mix, gain_one, shift_one, w_inner, b_inner, w_outer, b_outer, gain_two, shift_two = params
    seq_count, seq_length, feat_width = inputs.shape
    head_shape = (seq_count, seq_length, HEADS, HEAD)
    queries = rounded(project(inputs, w_query) + b_query).reshape(head_shape)
    key_heads = rounded(project(inputs, w_key)).reshape(head_shape)
    values = rounded(project(inputs, w_value) + b_value).reshape(head_shape)
    scores = low_back(jnp.einsum('bqhe,bkhe->bhqk', queries, key_heads, precision=highest) * HEAD ** (-0.5))
    valid = lax.broadcasted_iota(jnp.int32, (seq_count, 1, 1, seq_length), 3) < lengths.reshape(seq_count, 1, 1, 1)
    attn_probs = jax.nn.softmax(jnp.where(valid, scores, -1e+30), axis=-1)
    mixed_heads = rounded(jnp.einsum('bhqk,bkhe->bqhe', low(attn_probs), values, precision=highest).reshape(seq_count, seq_length, feat_width))
    attended = low_back(project(mixed_heads, w_mix) + b_mix)
    first_norm = normalize(inputs + attended, gain_one, shift_one)
    inner_pre = low_back(project(low(first_norm), w_inner) + b_inner)
    hidden = low(jax.nn.gelu(inner_pre, approximate=False))
    outer_pre = low_back(project(hidden, w_outer) + b_outer)
    return normalize(first_norm + outer_pre, gain_two, shift_two)

def reference(query_tokens, passage_tokens, query_length, passage_length, clusters, positives, w_query, b_query, w_key, w_value, b_value, w_mix, b_mix, gain_one, shift_one, w_inner, b_inner, w_outer, b_outer, gain_two, shift_two):
    params = tuple((weight.astype(jnp.float32) for weight in (w_query, b_query, w_key, w_value, b_value, w_mix, b_mix, gain_one, shift_one, w_inner, b_inner, w_outer, b_outer, gain_two, shift_two)))
    block_pairs = 16
    groups = PAIRS // block_pairs

    def run_block(params_in, piece_set):
        query_block, passage_block, query_len_block, passage_len_block = piece_set
        return (encoder_layer(query_block, query_len_block, params_in), encoder_layer(passage_block, passage_len_block, params_in))
    checked = jax.checkpoint(run_block)

    def forward(params_in, query_inputs, passage_inputs):
        piece_sets = (query_inputs.reshape(groups, block_pairs, QLEN, D), passage_inputs.reshape(groups, block_pairs, PLEN, D), query_length.reshape(groups, block_pairs), passage_length.reshape(groups, block_pairs))

        def scan_step(carry_in, piece_set):
            return (carry_in, checked(params_in, piece_set))
        _, (query_result, passage_result) = lax.scan(scan_step, 0, piece_sets)
        query_result = query_result.reshape(PAIRS, QLEN, D)
        passage_result = passage_result.reshape(PAIRS, PLEN, D)
        cls_query = low(query_result[:, 0])
        cls_passage = low(passage_result[:, 0])
        pair_scores = low_back(jnp.dot(cls_query, cls_passage.T, precision=highest) * (2.0 * D ** (-0.5)))
        column = lax.broadcasted_iota(jnp.int32, (PAIRS, PAIRS), 1)
        chosen = column == positives[:, None]
        counted = (clusters[None, :] != clusters[:, None]) | chosen
        log_total = jax.nn.logsumexp(jnp.where(counted, pair_scores, -1e+30), axis=1)
        picked = lax.optimization_barrier(jnp.sum(jnp.where(chosen, pair_scores, 0.0), axis=1))
        return (jnp.sum(log_total - picked), (query_result, passage_result))
    query_inputs = query_tokens.astype(jnp.float32)
    passage_inputs = passage_tokens.astype(jnp.float32)
    total_loss, pullback, (query_result, passage_result) = jax.vjp(forward, params, query_inputs, passage_inputs, has_aux=True)
    param_grads, query_grad, passage_grad = pullback(jnp.ones_like(total_loss))
    grad_w_query, grad_b_query, grad_w_key, grad_w_value, grad_b_value, grad_w_mix, grad_b_mix, grad_gain_one, grad_shift_one, grad_w_inner, grad_b_inner, grad_w_outer, grad_b_outer, grad_gain_two, grad_shift_two = param_grads
    return (query_result.astype(jnp.bfloat16), passage_result.astype(jnp.bfloat16), total_loss / PAIRS, query_grad, passage_grad, grad_w_query, grad_b_query, grad_w_key, grad_w_value, grad_b_value, grad_w_mix, grad_b_mix, grad_gain_one, grad_shift_one, grad_w_inner, grad_b_inner, grad_w_outer, grad_b_outer, grad_gain_two, grad_shift_two)
```

```python
import functools

import jax
import jax.numpy as jnp
from jax import lax
from jax.experimental import pallas as pl
from jax.experimental.pallas import tpu as pltpu
from jax.sharding import PartitionSpec as P

HEADS = 12
HEAD = 64
LANES = 128
AXES = ("batch", "rep")
BF = jnp.bfloat16
F32 = jnp.float32
MIB = 2**20
KERNEL_ROWS = 1024
B_QUERY, B_VALUE, B_MIX, GAIN_ONE, SHIFT_ONE, B_OUTER, GAIN_TWO, SHIFT_TWO = range(8)


def dot(a, b):
    return jnp.dot(a, b, preferred_element_type=F32)


def dot_nt(a, b):
    return lax.dot_general(a, b, (((1,), (1,)), ((), ())), preferred_element_type=F32)


def dot_tn(a, b):
    return lax.dot_general(a, b, (((0,), (0,)), ((), ())), preferred_element_type=F32)


def gelu(z):
    half = 0.5 * z
    return half + half * lax.erf(z * 0.5**0.5)


def gelu_slope(z):
    phi = jnp.exp(-0.5 * z * z) * 0.3989422804014327
    return 0.5 + 0.5 * lax.erf(z * 0.5**0.5) + z * phi


def center_scale(v):
    c = v - jnp.mean(v, axis=-1, keepdims=True)
    r = lax.rsqrt(jnp.mean(c * c, axis=-1, keepdims=True) + 1e-12)
    return c * r, r


def scores_of(qp, ka, own, sel):
    qa = jnp.concatenate([jnp.where(sel, qp, jnp.zeros_like(qp)), own], 1)
    return dot_nt(qa, ka)


def softened(scores):
    return jnp.exp2(scores - jnp.max(scores, axis=-1, keepdims=True)).astype(BF)


def values_of(vp, key_low):
    zero, one = jnp.zeros_like(vp), jnp.ones_like(vp)
    top = jnp.concatenate([jnp.where(key_low, vp, zero), jnp.where(key_low, one, zero)], 1)
    low = jnp.concatenate([jnp.where(key_low, zero, vp), jnp.where(key_low, zero, one)], 1)
    return jnp.concatenate([top, low], 0)


def row(pack, index):
    return pack[index : index + 1, :]


def forward_kernel(joint, start, len_ref, x_ref, pack, bi, wq, wk, wv, wm, wi, wo, *rest):
    out_ref = rest[-1]
    at_seq = start + pl.program_id(0)
    seqs, seq_rows, _ = x_ref.shape
    if joint:
        rows = keys = seqs * seq_rows
        x = x_ref[...].reshape(rows, x_ref.shape[2])
        at = lax.broadcasted_iota(jnp.int32, (rows, LANES), 0)
        lane = lax.broadcasted_iota(jnp.int32, (rows, LANES), 1)
        length = jnp.zeros((rows, LANES), jnp.int32)
        for s in range(seqs):
            length = jnp.where(lane == s, len_ref[s], length)
        off = at - lane * seq_rows
        bias = jnp.where((off >= 0) & (off < length), 0.0, -1e30).astype(BF)
        own = jnp.where((off >= 0) & (off < seq_rows), 1.0, 0.0).astype(BF)
    else:
        x = x_ref[at_seq]
        rows = seq_rows
        keys = -(-rows // LANES) * LANES
        at = lax.broadcasted_iota(jnp.int32, (keys, LANES), 0)
        lane = lax.broadcasted_iota(jnp.int32, (keys, LANES), 1)
        bias = jnp.where((lane == 0) & (at >= len_ref[at_seq]), -1e30, 0.0).astype(BF)
        own = jnp.where(
            lax.broadcasted_iota(jnp.int32, (rows, LANES), 1) == 0, 1.0, 0.0
        ).astype(BF)

    width = x.shape[1]
    wide = 2 * LANES
    groups = width // wide
    scale = HEAD**-0.5 * 1.4426950408889634
    low = lax.broadcasted_iota(jnp.int32, (rows, LANES), 1) < HEAD
    key_low = lax.broadcasted_iota(jnp.int32, (keys, LANES), 1) < HEAD

    def projected(w, g, index=None, factor=None):
        cols = slice(g * wide, (g + 1) * wide)
        v = dot(x, w[:, cols])
        if index is not None:
            v = v + row(pack, index)[:, cols]
        if factor is not None:
            v = v * factor
        v = v.astype(BF)
        if factor is not None or keys == rows:
            return v
        return jnp.concatenate([v, jnp.zeros((keys - rows, wide), BF)], 0)

    def pair_cols(p):
        return slice(p % 2 * LANES, (p % 2 + 1) * LANES)

    made = [(projected(wq, 0, B_QUERY, scale), projected(wk, 0), projected(wv, 0, B_VALUE))]

    def pair_scores(p):
        q, k, _ = made[p // 2]
        cols = pair_cols(p)
        ka = jnp.concatenate([k[:, cols], bias], 1)
        return scores_of(q[:, cols], ka, own, low), scores_of(q[:, cols], ka, own, ~low)

    ready = pair_scores(0)
    outs = []
    for p in range(HEADS // 2):
        g = p // 2
        scores = ready
        if p % 2 == 0 and g + 1 < groups:
            part = projected(wq, g + 1, B_QUERY, scale), projected(wk, g + 1)
        if p % 2 == 1 and g + 1 < groups:
            made.append(part + (projected(wv, g + 1, B_VALUE),))
        if p + 1 < HEADS // 2:
            ready = pair_scores(p + 1)
        e = jnp.concatenate([softened(v) for v in scores], 1)
        o = dot(e, values_of(made[g][2][:, pair_cols(p)], key_low))
        outs.append((o[:, :LANES] / o[:, LANES:]).astype(BF))
    mixed = jnp.concatenate(outs, 1)

    nrm, _ = center_scale(x.astype(F32) + dot(mixed, wm[...]) + row(pack, B_MIX))
    first = nrm * row(pack, GAIN_ONE) + row(pack, SHIFT_ONE)
    first_low = first.astype(BF)
    acc = first + row(pack, B_OUTER)
    for j in range(wi.shape[1] // width):
        cols = slice(j * width, (j + 1) * width)
        z = dot(first_low, wi[:, cols]) + bi[:, cols]
        acc = acc + dot(gelu(z).astype(BF), wo[cols, :])
    nrm, _ = center_scale(acc)
    out = (nrm * row(pack, GAIN_TWO) + row(pack, SHIFT_TWO)).astype(BF)
    if joint:
        out_ref[...] = out.reshape(out_ref.shape)
    else:
        out_ref[at_seq] = out


def forward(tokens, lengths, pack, bi, mats, joint, start, count, into=None):
    _, rows, width = tokens.shape
    total = count * rows
    weight_bytes = sum(m.size * 2 for m in mats)
    extra = [] if into is None else [pltpu.with_memory_space_constraint(into, pltpu.VMEM)]
    operands = [in_hbm(lengths), tokens, pack, bi, *mats] + extra
    return pl.pallas_call(
        functools.partial(forward_kernel, joint, start),
        grid=(1 if joint else count,),
        in_specs=[smem()] + [vmem()] * 9 + [anywhere()] * len(extra),
        out_specs=vmem(),
        out_shape=pltpu.VMEM(tokens.shape, BF),
        input_output_aliases={} if into is None else {len(operands) - 1: 0},
        compiler_params=params(16),
        cost_estimate=pl.CostEstimate(
            flops=int(total * weight_bytes * 1.9),
            bytes_accessed=weight_bytes + total * width * 4,
            transcendentals=total * 4096,
        ),
        name="forward_rows",
    )(*operands)


def head_of_lane(shape):
    return lax.broadcasted_iota(jnp.int32, shape, 1) // HEAD


def expand_heads(v):
    head = head_of_lane(v.shape)
    zero = jnp.zeros_like(v)
    return jnp.concatenate([jnp.where(head == h, v, zero) for h in range(HEADS)], 0)


def collapse_heads(v):
    seqs = v.shape[0] // HEADS
    out = jnp.zeros((seqs, v.shape[1]), v.dtype)
    head = head_of_lane(out.shape)
    for h in range(HEADS):
        out = jnp.where(head == h, v[h * seqs : (h + 1) * seqs], out)
    return out


PLACES = ("own", "line", "core", "y", "x", "inside", "first_off", "first_inside", "hidden_off", "hidden_inside", "pair")


def place_of(places, planes, name):
    return places[2 * planes + PLACES.index(name)]


def window_size(size):
    return size if size % LANES == 0 else 2 * LANES


def split3(v):
    hi = v.astype(BF)
    mid = (v - hi.astype(F32)).astype(BF)
    lo = (v - hi.astype(F32) - mid.astype(F32)).astype(BF)
    return hi, mid, lo


def load(pairs, sems):
    copies = [pltpu.make_async_copy(a, b, sems.at[i]) for i, (a, b) in enumerate(pairs)]
    for c in copies:
        c.start()
    return copies


def cls_kernel(places, query_len, passage_len, target, clusters, qt_h, pt_h, wq_h, wk_h, wv_h, wm_h, wi_h, wo_h, *rest):
    planes = len(rest) - 25
    vectors, (packet, probs_out, a_out, pack, bi), rest = rest[:9], rest[9:14], rest[14:]
    wq, wk, wv, wm, wi, wo, qt, pt = rest[:8]
    early = rest[8 : 8 + planes]
    px_s, pair_s, sems = rest[8 + planes :]
    copies = load(
        ((qt_h, qt), (pt_h, pt), (wq_h, wq), (wk_h, wk), (wv_h, wv), (wm_h, wm), (wi_h, wi), (wo_h, wo)),
        sems,
    )
    copies, (q_copy, p_copy) = copies[2:], copies[:2]
    for i, v in enumerate(vectors[:8]):
        pack[i : i + 1, :] = v[...].astype(F32).reshape(1, -1)
    bi[...] = vectors[8][...].astype(F32).reshape(1, -1)
    pairs, query_rows, width = qt.shape
    passage_rows = pt.shape[1]
    seqs = 2 * pairs
    at = lax.broadcasted_iota(jnp.int32, (seqs, width), 0)
    start = jnp.zeros((seqs, width), F32)
    q_copy.wait()
    p_copy.wait()
    for s in range(seqs):
        src = qt[s, 0:16, :] if s < pairs else pt[s - pairs, 0:16, :]
        start = jnp.where(at == s, src.astype(F32)[0:1, :], start)
    low_start = start.astype(BF)
    copies[0].wait()
    q0 = (dot(low_start, wq[...]) + row(pack, B_QUERY)).astype(BF)
    copies[1].wait()
    a = (dot_nt(expand_heads(q0), wk[...]) * HEAD**-0.5).astype(BF)
    a_out[...] = a
    xq = qt[...].reshape(pairs * query_rows, width)
    xp = pt[...].reshape(pairs * passage_rows, width)
    scores = jnp.concatenate([dot_nt(a, xq), dot_nt(a, xp)], 1)
    s_row = lax.broadcasted_iota(jnp.int32, (HEADS * seqs, 1), 0) % seqs
    lo = jnp.zeros((HEADS * seqs, 1), jnp.int32)
    hi = jnp.zeros((HEADS * seqs, 1), jnp.int32)
    for s in range(seqs):
        if s < pairs:
            first_at, length = s * query_rows, query_len[s]
        else:
            first_at = pairs * query_rows + (s - pairs) * passage_rows
            length = passage_len[s - pairs]
        lo = jnp.where(s_row == s, first_at, lo)
        hi = jnp.where(s_row == s, first_at + length, hi)
    column = lax.broadcasted_iota(jnp.int32, scores.shape, 1)
    scores = jnp.where((column >= lo) & (column < hi), scores, -1e30)
    e = jnp.exp(scores - jnp.max(scores, axis=-1, keepdims=True))
    probs = e / jnp.sum(e, axis=-1, keepdims=True)
    probs_out[...] = probs
    probs = probs.astype(BF)
    cut = pairs * query_rows
    px = (dot(probs[:, :cut], xq) + dot(probs[:, cut:], xp)).astype(BF)
    px_s[...] = px
    copies[2].wait()
    mixed = (collapse_heads(dot(px, wv[...])) + row(pack, B_VALUE)).astype(BF)
    pair_s[0:seqs, :] = low_start
    pair_s[seqs : 2 * seqs, :] = mixed
    heads_rows = HEADS * seqs
    for k, out in enumerate(early):
        window = pl.ds(pl.multiple_of(places[k], LANES), 2 * LANES)
        out[0:heads_rows, :] = px_s[:, window]
        out[heads_rows : heads_rows + 2 * seqs, :] = pair_s[:, window]
        for j in range(width // (2 * LANES)):
            base = heads_rows + (2 + j) * seqs
            out[base : base + seqs, :] = q0[:, j * 2 * LANES : (j + 1) * 2 * LANES]
    copies[3].wait()
    nrm, r_one = center_scale(start + dot(mixed, wm[...]) + row(pack, B_MIX))
    first = nrm * row(pack, GAIN_ONE) + row(pack, SHIFT_ONE)
    low = first.astype(BF)
    acc = first + row(pack, B_OUTER)
    copies[4].wait()
    copies[5].wait()
    for j in range(wi.shape[1] // width):
        cols = slice(j * width, (j + 1) * width)
        hidden = gelu(dot(low, wi[:, cols]) + bi[:, cols]).astype(BF)
        acc = acc + dot(hidden, wo[cols, :])
    nrm, r_two = center_scale(acc)
    packet[:, :width] = (nrm * row(pack, GAIN_TWO) + row(pack, SHIFT_TWO)).astype(BF)
    packet[:, width : 2 * width] = low
    lane = lax.broadcasted_iota(jnp.int32, (seqs, LANES), 1)
    at = lax.broadcasted_iota(jnp.int32, (seqs, LANES), 0)
    wanted = jnp.zeros((seqs, LANES), jnp.int32)
    cluster = jnp.zeros((seqs, LANES), jnp.int32)
    base = place_of(places, planes, "pair")
    for s in range(seqs):
        cluster = jnp.where(at == s, clusters[base + s % pairs], cluster)
        if s < pairs:
            wanted = jnp.where(at == s, target[s], wanted)
    extra = jnp.zeros((seqs, LANES), jnp.int32)
    for j, v in enumerate((wanted // LANES, wanted % LANES, cluster // LANES, cluster % LANES)):
        extra = jnp.where(lane == 6 + j, v, extra)
    extra = extra.astype(F32)
    for j, part in enumerate(split3(r_one) + split3(r_two)):
        extra = jnp.where(lane == j, part.astype(F32), extra)
    packet[:, 2 * width :] = extra.astype(BF)


def vmem():
    return pl.BlockSpec(memory_space=pltpu.VMEM)


def smem():
    return pl.BlockSpec(memory_space=pltpu.SMEM)


def anywhere():
    return pl.BlockSpec(memory_space=pl.ANY)


def params(mib):
    return pltpu.CompilerParams(vmem_limit_bytes=mib * MIB)


def in_hbm(v):
    return pltpu.with_memory_space_constraint(v, pltpu.HBM)


def cls_forward(places, query_length, passage_length, positives, clusters, query_tokens, passage_tokens, mats, vectors, planes):
    pairs, query_rows, width = query_tokens.shape
    seqs = 2 * pairs
    tokens = pairs * (query_rows + passage_tokens.shape[1])
    early_rows = seqs * (HEADS + 2 + width // (2 * LANES))
    outs = [
        jax.ShapeDtypeStruct((seqs, 2 * width + LANES), BF),
        pltpu.HBM((HEADS * seqs, tokens), F32),
        pltpu.HBM((HEADS * seqs, width), BF),
        jax.ShapeDtypeStruct((8, width), F32),
        jax.ShapeDtypeStruct((1, mats[4].shape[1]), F32),
    ]
    outs += [pltpu.VMEM(v.shape, v.dtype) for v in (*mats, query_tokens, passage_tokens)]
    outs += [jax.ShapeDtypeStruct((early_rows, 2 * LANES), BF)] * planes
    got = pl.pallas_call(
        cls_kernel,
        in_specs=[smem()] * 5 + [anywhere()] * 8 + [vmem()] * 9,
        out_specs=[vmem()] * len(outs),
        out_shape=outs,
        scratch_shapes=[
            pltpu.VMEM((HEADS * seqs, width), BF),
            pltpu.VMEM((2 * seqs, width), BF),
            pltpu.SemaphoreType.DMA((8,)),
        ],
        compiler_params=params(20),
        cost_estimate=pl.CostEstimate(flops=8 * 10**9, bytes_accessed=20 * 10**6, transcendentals=0),
        name="cls_forward",
    )(
        places, *[in_hbm(v) for v in (query_length, passage_length, positives, clusters)],
        in_hbm(query_tokens), in_hbm(passage_tokens), *[in_hbm(m) for m in mats], *[in_hbm(v) for v in vectors],
    )
    kept = [pltpu.with_memory_space_constraint(v, pltpu.VMEM) for v in got[5:13]]
    return got[:5], kept[:6], kept[6:], got[13:]


def place_planes_kernel(places, *refs):
    *parts, out = refs
    for k, part in enumerate(parts):
        at = places[len(parts) + k]
        out[pl.ds(at // part.shape[0], 1)] = part[...][None]


def place_planes(places, parts):
    shape = (len(parts),) + parts[0].shape
    return pl.pallas_call(
        place_planes_kernel,
        in_specs=[smem()] + [vmem()] * len(parts),
        out_specs=vmem(),
        out_shape=jax.ShapeDtypeStruct(shape, BF),
        compiler_params=params(8),
        name="place_planes",
    )(places, *parts)


def place_pair_kernel(planes, name, places, mine, got, out):
    at = place_of(places, planes, name)
    out[:, pl.ds(at, 1)] = mine[...][:, None]
    out[:, pl.ds(1 - at, 1)] = got[...][:, None]


def place_pair(places, planes, name, mine, got):
    shape = (mine.shape[0], 2) + mine.shape[1:]
    out = pl.pallas_call(
        functools.partial(place_pair_kernel, planes, name),
        in_specs=[smem()] + [vmem()] * 2,
        out_specs=vmem(),
        out_shape=jax.ShapeDtypeStruct(shape, BF),
        compiler_params=params(8),
        name="place_pair",
    )(places, mine, got)
    return out.reshape((-1,) + mine.shape[1:])


def norm_back(grad, nrm, r, gain):
    g = grad * gain
    return r * (
        g - jnp.mean(g, axis=-1, keepdims=True) - nrm * jnp.mean(g * nrm, axis=-1, keepdims=True)
    )


def back_kernel(
    planes, slice_first, places, packet_a, packet_b, pack, bi, wq, wk, wv, wm, wi, wo,
    qt, pt, probs_h, a_h, *rest,
):
    grad_wo, grad_wi, vectors, grad_bi, line_att, line_mix, dp_q, dp_p, ab_out, at_start = rest[:10]
    late = rest[10 : 10 + planes]
    probs_ref, a_ref, packet_s, mix_s, line_s, start_s, xs_s, win_s, sems = rest[10 + planes :]
    copies = load(((probs_h, probs_ref), (a_h, a_ref)), sems)
    core = place_of(places, planes, "core")
    packet_s[:, pl.ds(core, 1)] = packet_a[...][:, None]
    packet_s[:, pl.ds(1 - core, 1)] = packet_b[...][:, None]
    pairs, query_rows, width = qt.shape
    passage_rows = pt.shape[1]
    seqs = 2 * pairs
    packet = packet_s[...].reshape(-1, packet_s.shape[-1])
    rows = packet.shape[0]
    scale = 2.0 * width**-0.5

    cls = packet[:, :width]
    tail = packet[:, 2 * width :].astype(F32)
    scores = dot_nt(cls, cls) * scale
    is_query = lax.broadcasted_iota(jnp.int32, (rows, 1), 0) % seqs < pairs
    is_passage = lax.broadcasted_iota(jnp.int32, (1, rows), 1) % seqs >= pairs
    wanted = (tail[:, 6:7] * LANES + tail[:, 7:8]).astype(jnp.int32)
    column = lax.broadcasted_iota(jnp.int32, (1, rows), 1)
    chosen = (column // seqs * pairs + column % pairs == wanted) & is_passage
    across = tail.T
    cluster_row = across[8:9, :] * LANES + across[9:10, :]
    cluster_col = tail[:, 8:9] * LANES + tail[:, 9:10]
    counted = ((cluster_row != cluster_col) | chosen) & is_passage
    masked = jnp.where(counted, scores, -1e30)
    peak = jnp.max(masked, axis=1, keepdims=True)
    log_total = peak + jnp.log(jnp.sum(jnp.exp(masked - peak), axis=1, keepdims=True))
    one = jnp.where(chosen, 1.0, 0.0)
    picked = jnp.sum(one * scores, axis=1, keepdims=True)
    loss = jnp.sum(jnp.where(is_query, log_total - picked, 0.0), axis=0, keepdims=True)
    d_pair = jnp.where(is_query, jnp.exp(masked - log_total) - one, 0.0).astype(BF)
    d_cls = (dot(d_pair, cls) + dot_tn(d_pair, cls)) * scale

    first = packet[:, width : 2 * width]
    nrm_two = (cls.astype(F32) - row(pack, SHIFT_TWO)) / row(pack, GAIN_TWO)
    r_two = tail[:, 3:4] + tail[:, 4:5] + tail[:, 5:6]
    d_second = norm_back(d_cls, nrm_two, r_two, row(pack, GAIN_TWO))
    d_outer = d_second.astype(BF)
    vectors[0:1, :] = jnp.sum(d_outer.astype(F32), axis=0, keepdims=True)
    vectors[1:2, :] = jnp.sum(d_cls * nrm_two, axis=0, keepdims=True)
    vectors[2:3, :] = jnp.sum(d_cls, axis=0, keepdims=True)
    piece = grad_wi.shape[0]
    first_window = pl.ds(
        pl.multiple_of(place_of(places, planes, "first_off"), LANES), 2 * LANES
    )
    mix_s[...] = first
    first_piece = mix_s[:, first_window]
    inside = pl.ds(pl.multiple_of(place_of(places, planes, "first_inside"), 8), piece)
    d_first = d_second
    for j in range(wi.shape[1] // width):
        cols = slice(j * width, (j + 1) * width)
        inner = dot(first, wi[:, cols]) + bi[:, cols]
        d_inner = (dot_nt(d_outer, wo[cols, :]) * gelu_slope(inner)).astype(BF)
        d_first = d_first + dot_nt(d_inner, wi[:, cols])
        found = dot_tn(first_piece, d_inner)
        if slice_first:
            win_s[: 2 * LANES, :] = found
            found = win_s[inside, :]
        grad_wi[:, cols] = found
        grad_bi[:, cols] = jnp.sum(d_inner.astype(F32), axis=0, keepdims=True)
    size = grad_wo.shape[0]
    off = pl.multiple_of(place_of(places, planes, "hidden_off"), LANES)
    window = pl.ds(off, window_size(size))
    hidden = gelu(dot(first, wi[:, window]) + bi[:, window]).astype(BF)
    found = dot_tn(hidden, d_outer)
    if size != window_size(size):
        win_s[: window_size(size), :] = found
        found = win_s[pl.ds(pl.multiple_of(place_of(places, planes, "hidden_inside"), 8), size), :]
    grad_wo[...] = found
    nrm_one = (first.astype(F32) - row(pack, SHIFT_ONE)) / row(pack, GAIN_ONE)
    r_one = tail[:, 0:1] + tail[:, 1:2] + tail[:, 2:3]
    d_start = norm_back(d_first, nrm_one, r_one, row(pack, GAIN_ONE))
    vectors[3:4, :] = jnp.sum(d_first * nrm_one, axis=0, keepdims=True)
    vectors[4:5, :] = jnp.sum(d_first, axis=0, keepdims=True)
    start_s[...] = d_start
    d_attended = d_start.astype(BF)
    vectors[5:6, :] = jnp.sum(d_attended.astype(F32), axis=0, keepdims=True)
    d_mixed = dot_nt(d_attended, wm[...]).astype(BF)
    vectors[6:7, :] = jnp.sum(d_mixed.astype(F32), axis=0, keepdims=True)
    vectors[7:8, :] = jnp.broadcast_to(loss, (1, width))
    line_rows = line_att.shape[0]
    by_line = (planes, rows // line_rows, seqs, width)
    line = pl.ds(place_of(places, planes, "line"), 1)
    line_s[...] = d_attended.reshape(by_line)
    line_att[...] = line_s[:, line].reshape(line_rows, width)
    line_s[...] = d_mixed.reshape(by_line)
    line_mix[...] = line_s[:, line].reshape(line_rows, width)
    mix_s[...] = d_mixed

    own = pl.ds(pl.multiple_of(place_of(places, planes, "own"), seqs), seqs)
    own_mixed = mix_s[own, :]
    for c in copies:
        c.wait()
    bm = dot_nt(expand_heads(own_mixed), wv[...]).astype(BF)
    xq = qt[...].reshape(pairs * query_rows, width)
    xp = pt[...].reshape(pairs * passage_rows, width)
    d_probs = jnp.concatenate([dot_nt(bm, xq), dot_nt(bm, xp)], 1)
    probs = probs_ref[...]
    d_scores = (probs * (d_probs - jnp.sum(probs * d_probs, axis=-1, keepdims=True))).astype(BF)
    cut = pairs * query_rows
    xs = (dot(d_scores[:, :cut], xq) + dot(d_scores[:, cut:], xp)).astype(BF)
    xs_s[...] = xs
    d_query = (collapse_heads(dot(xs, wk[...])) * HEAD**-0.5).astype(BF)
    heads_rows = HEADS * seqs
    for k, out in enumerate(late):
        window = pl.ds(pl.multiple_of(places[k], LANES), 2 * LANES)
        out[0:heads_rows, :] = xs_s[:, window]
        for j in range(width // (2 * LANES)):
            base = heads_rows + j * seqs
            out[base : base + seqs, :] = d_query[:, j * 2 * LANES : (j + 1) * 2 * LANES]
    probs = probs.astype(BF)
    for out, cols in ((dp_q, slice(0, cut)), (dp_p, slice(cut, None))):
        out[0:heads_rows, :] = d_scores[:, cols]
        out[heads_rows:, :] = probs[:, cols]
    ab_out[0:heads_rows, :] = a_ref[...]
    ab_out[heads_rows:, :] = bm
    at_start[...] = dot_nt(d_query, wq[...]) + start_s[own, :]


def cls_backward(places, packet_a, packet_b, pack, bi, mats, query_tokens, passage_tokens, probs, a, planes, batch_count):
    pairs, query_rows, width = query_tokens.shape
    seqs = 2 * pairs
    blocks = packet_a.shape[0]
    rows = 2 * blocks * seqs
    late_rows = seqs * (HEADS + width // (2 * LANES))
    cut = pairs * query_rows
    hidden = mats[4].shape[1]
    first_rows, hidden_rows = width // batch_count, hidden // batch_count
    slice_first = first_rows % 8 == 0

    def out(shape, kind):
        return jax.ShapeDtypeStruct(shape, kind)

    outs = [
        pltpu.HBM((hidden_rows, width), F32),
        pltpu.HBM((first_rows if slice_first else 2 * LANES, hidden), F32),
        out((8, width), F32),
        out((1, hidden), F32),
        out((planes * seqs, width), BF),
        out((planes * seqs, width), BF),
        pltpu.HBM((2 * HEADS * seqs, cut), BF),
        pltpu.HBM((2 * HEADS * seqs, probs.shape[1] - cut), BF),
        pltpu.HBM((2 * HEADS * seqs, width), BF),
        out((seqs, width), F32),
    ] + [out((late_rows, 2 * LANES), BF)] * planes
    got = pl.pallas_call(
        functools.partial(back_kernel, planes, slice_first),
        in_specs=[smem()] + [vmem()] * 12 + [anywhere()] * 2,
        out_specs=[vmem()] * len(outs),
        out_shape=outs,
        scratch_shapes=[pltpu.VMEM(v.shape, v.dtype) for v in (probs, a)]
        + [
            pltpu.VMEM((blocks, 2) + packet_a.shape[1:], BF),
            pltpu.VMEM((rows, width), BF),
            pltpu.VMEM((planes, rows // (planes * seqs), seqs, width), BF),
            pltpu.VMEM((rows, width), F32),
            pltpu.VMEM((HEADS * seqs, width), BF),
            pltpu.VMEM((2 * LANES, width), F32),
            pltpu.SemaphoreType.DMA((2,)),
        ],
        compiler_params=params(34),
        cost_estimate=pl.CostEstimate(flops=16 * 10**9, bytes_accessed=25 * 10**6, transcendentals=0),
        name="cls_backward",
    )(
        places, packet_a, packet_b, pack, bi, *mats,
        query_tokens, passage_tokens, in_hbm(probs), in_hbm(a),
    )
    return got[:10], got[10:]


def plain_backward(places, packet_a, packet_b, pack, bi, mats, query_tokens, passage_tokens, probs, a, planes, batch_count):
    wq, wk, wv, wm, wi, wo = mats
    pairs, query_rows, width = query_tokens.shape
    seqs = 2 * pairs
    blocks = packet_a.shape[0]
    rows = 2 * blocks * seqs
    cut = pairs * query_rows
    hidden = wi.shape[1]

    def at(name):
        return places[2 * planes + PLACES.index(name)]

    core = at("core")
    packet = jnp.stack(
        [jnp.where(core == 0, packet_a, packet_b), jnp.where(core == 0, packet_b, packet_a)], 1
    )
    packet = packet.reshape(2 * blocks, seqs, -1)
    cls_query = packet[:, :pairs, :width].reshape(-1, width)
    cls_passage = packet[:, pairs:, :width].reshape(-1, width)
    packet = packet.reshape(rows, -1)
    tail = packet[:, 2 * width :].astype(F32)

    def sides(v):
        v = v.reshape(2 * blocks, seqs)
        return v[:, :pairs].reshape(-1), v[:, pairs:].reshape(-1)

    scale = 2.0 * width**-0.5
    scores = dot_nt(cls_query, cls_passage) * scale
    wanted = sides(tail[:, 6] * LANES + tail[:, 7])[0]
    query_cluster, passage_cluster = sides(tail[:, 8] * LANES + tail[:, 9])
    chosen = jnp.arange(scores.shape[1], dtype=F32)[None] == wanted[:, None]
    counted = (query_cluster[:, None] != passage_cluster[None]) | chosen
    masked = jnp.where(counted, scores, -1e30)
    log_total = jax.nn.logsumexp(masked, axis=1, keepdims=True)
    one = chosen.astype(F32)
    loss = jnp.sum(log_total - jnp.sum(one * scores, axis=1, keepdims=True))
    d_pair = (jnp.exp(masked - log_total) - one).astype(BF)
    d_cls = jnp.concatenate(
        [
            dot(d_pair, cls_passage).reshape(2 * blocks, pairs, width),
            dot_tn(d_pair, cls_query).reshape(2 * blocks, pairs, width),
        ],
        1,
    ).reshape(rows, width) * scale
    first = packet[:, width : 2 * width]
    nrm_two = (packet[:, :width].astype(F32) - row(pack, SHIFT_TWO)) / row(pack, GAIN_TWO)
    nrm_one = (first.astype(F32) - row(pack, SHIFT_ONE)) / row(pack, GAIN_ONE)
    d_second = norm_back(
        d_cls, nrm_two, jnp.sum(tail[:, 3:6], 1, keepdims=True), row(pack, GAIN_TWO)
    )
    d_outer = d_second.astype(BF)
    hidden_rows, first_rows = hidden // batch_count, width // batch_count
    hidden_at = at("hidden_off") + at("hidden_inside")
    first_at = at("first_off") + at("first_inside")
    wi_piece = lax.dynamic_slice_in_dim(wi, hidden_at, hidden_rows, 1)
    bi_piece = lax.dynamic_slice_in_dim(bi, hidden_at, hidden_rows, 1)

    def block(parts):
        first, d_outer = parts
        d_inner = (dot_nt(d_outer, wo) * gelu_slope(dot(first, wi) + bi)).astype(BF)
        return d_inner, dot_nt(d_inner, wi), gelu(dot(first, wi_piece) + bi_piece).astype(BF)

    size = rows // 8
    parts = first.reshape(-1, size, width), d_outer.reshape(-1, size, width)
    d_inner, more, hidden_piece = (v.reshape(rows, -1) for v in lax.map(block, parts))
    d_first = d_second + more
    first_piece = lax.dynamic_slice_in_dim(first, first_at, first_rows, 1)
    grad_wo, grad_wi = dot_tn(hidden_piece, d_outer), dot_tn(first_piece, d_inner)
    if first_rows % 8:
        grad_wi = lax.dynamic_update_slice_in_dim(
            jnp.zeros((2 * LANES, hidden), F32), grad_wi, at("first_inside"), 0
        )
    d_start = norm_back(
        d_first, nrm_one, jnp.sum(tail[:, 0:3], 1, keepdims=True), row(pack, GAIN_ONE)
    )
    d_attended = d_start.astype(BF)
    d_mixed = dot_nt(d_attended, wm).astype(BF)
    sums = (d_outer, d_cls * nrm_two, d_cls, d_first * nrm_one, d_first, d_attended, d_mixed)
    vectors = [jnp.sum(v.astype(F32), 0) for v in sums] + [jnp.full((width,), loss)]

    def line(v):
        v = v.reshape(planes, -1, seqs, width)
        return lax.dynamic_slice_in_dim(v, at("line"), 1, 1).reshape(planes * seqs, width)

    def own(v):
        return lax.dynamic_slice_in_dim(v, at("own"), seqs, 0)

    bm = dot_nt(expand_heads(own(d_mixed)), wv).astype(BF)
    xq = query_tokens.reshape(-1, width)
    xp = passage_tokens.reshape(-1, width)
    d_probs = jnp.concatenate([dot_nt(bm, xq), dot_nt(bm, xp)], 1)
    d_scores = (probs * (d_probs - jnp.sum(probs * d_probs, axis=-1, keepdims=True))).astype(BF)
    xs = (dot(d_scores[:, :cut], xq) + dot(d_scores[:, cut:], xp)).astype(BF)
    d_query = (collapse_heads(dot(xs, wk)) * HEAD**-0.5).astype(BF)
    blocks_of_query = [
        d_query[:, j : j + 2 * LANES] for j in range(0, width, 2 * LANES)
    ]
    late = [
        jnp.concatenate(
            [lax.dynamic_slice_in_dim(xs, places[k], 2 * LANES, 1)] + blocks_of_query
        )
        for k in range(planes)
    ]
    dp = jnp.concatenate([d_scores, probs.astype(BF)])
    return (
        grad_wo, grad_wi, jnp.stack(vectors), jnp.sum(d_inner.astype(F32), 0, keepdims=True),
        line(d_attended), line(d_mixed), dp[:, :cut], dp[:, cut:],
        jnp.concatenate([a, bm]), dot_nt(d_query, wq) + own(d_start),
    ), late


def tokens_kernel(base, dp, ab, at_start, near, out, far, sem):
    step = pl.program_id(0)
    copy = pltpu.make_async_copy(near, far, sem.at[0])

    @pl.when(step == 0)
    def _():
        copy.start()

    per, rows, _ = out.shape
    v = dot_tn(dp[...], ab[...])
    at = lax.broadcasted_iota(jnp.int32, v.shape, 0)
    for s in range(per):
        extra = at_start[pl.ds(base + step * per + s, 1), :]
        v = jnp.where(at == s * rows, v + extra, v)
    out[...] = v.reshape(out.shape)

    @pl.when(step == pl.num_programs(0) - 1)
    def _():
        copy.wait()


def token_grads(dp, ab, at_start, near, base, steps):
    pairs, rows, width = near.shape
    per = pairs // steps
    return pl.pallas_call(
        functools.partial(tokens_kernel, base),
        grid=(steps,),
        in_specs=[
            pl.BlockSpec((dp.shape[0], per * rows), lambda i: (0, i)),
            pl.BlockSpec(ab.shape, lambda i: (0, 0)),
            pl.BlockSpec(at_start.shape, lambda i: (0, 0)),
            anywhere(),
        ],
        out_specs=[pl.BlockSpec((per, rows, width), lambda i: (i, 0, 0)), anywhere()],
        out_shape=[pltpu.HBM((pairs, rows, width), F32), pltpu.HBM(near.shape, BF)],
        scratch_shapes=[pltpu.SemaphoreType.DMA((1,))],
        compiler_params=params(20),
        cost_estimate=pl.CostEstimate(flops=2 * 10**9, bytes_accessed=6 * 10**6, transcendentals=0),
        name="token_grads",
    )(in_hbm(dp), in_hbm(ab), at_start, pltpu.with_memory_space_constraint(near, pltpu.VMEM))


def sums_kernel(places, line_att, line_mix, *rest):
    planes = (len(rest) - 3) // 2
    early, late = rest[:planes], rest[planes : 2 * planes]
    mine, other, win = rest[2 * planes :]
    width = line_att.shape[1]
    wide = 2 * LANES
    seqs = line_att.shape[0] // planes
    heads_rows = HEADS * seqs

    def unfold(ref, base):
        return jnp.concatenate(
            [ref[base + j * seqs : base + (j + 1) * seqs, :] for j in range(width // wide)], 1
        )

    xs, px, starts, mixed, q0, dq, dm, da = ([] for _ in range(8))
    for k in range(planes):
        e, l = early[k], late[k]
        at = pl.ds(pl.multiple_of(places[planes + k], seqs), seqs)
        px.append(e[0:heads_rows, :])
        starts.append(e[heads_rows : heads_rows + seqs, :])
        mixed.append(e[heads_rows + seqs : heads_rows + 2 * seqs, :])
        q0.append(expand_heads(unfold(e, heads_rows + 2 * seqs)))
        xs.append(l[0:heads_rows, :])
        dq.append(unfold(l, heads_rows))
        dm.append(expand_heads(line_mix[at, :]))
        da.append(line_att[at, :])
    cat = functools.partial(jnp.concatenate, axis=0)
    dq = cat(dq)
    found = (
        dot_tn(cat(starts), dq),
        dot_tn(cat(xs), cat(q0)) * HEAD**-0.5,
        dot_tn(cat(px), cat(dm)),
        dot_tn(cat(mixed), cat(da)),
    )
    bias = jnp.broadcast_to(jnp.sum(dq.astype(F32), axis=0, keepdims=True), (16, width))
    slab = (mine.shape[0] - 16) // 4
    half = width // 2
    inside = pl.ds(pl.multiple_of(place_of(places, planes, "inside"), 8), slab)
    is_low = place_of(places, planes, "core") == 0
    for i in range(5):
        if i < 4:
            win[...] = found[i]
            v = win[inside, :]
        else:
            v = bias
        to = slice(i * slab, i * slab + v.shape[0])
        a, b = v[:, :half], v[:, half:]
        mine[to, :] = jnp.where(is_low, a, b)
        other[to, :] = jnp.where(is_low, b, a).astype(BF)


def partial_sums(places, line_att, line_mix, early, late, slab):
    width = line_att.shape[1]
    shape = (4 * slab + 16, width // 2)
    return pl.pallas_call(
        sums_kernel,
        in_specs=[smem()] + [vmem()] * (2 + 2 * len(early)),
        out_specs=[vmem()] * 2,
        out_shape=[jax.ShapeDtypeStruct(shape, F32), jax.ShapeDtypeStruct(shape, BF)],
        scratch_shapes=[pltpu.VMEM((2 * LANES, width), F32)],
        compiler_params=params(12),
        cost_estimate=pl.CostEstimate(flops=2 * 10**9, bytes_accessed=4 * 10**6, transcendentals=0),
        name="partial_sums",
    )(places, line_att, line_mix, *early, *late)


def fold_kernel(planes, places, mine, got, keep, send):
    total = mine[...] + got[...].astype(F32)
    slab = (mine.shape[0] - 16) // 4
    small = slab // 2
    is_low = place_of(places, planes, "y") == 0
    for i in range(5):
        base = i * slab
        if i < 4:
            a, b = total[base : base + small], total[base + small : base + slab]
            v, w = jnp.where(is_low, a, b), jnp.where(is_low, b, a)
        else:
            v = w = total[base : base + 16]
        to = slice(i * small, i * small + v.shape[0])
        keep[to, :] = v
        send[to, :] = w.astype(BF)


def fold(places, planes, mine, got):
    rows = (mine.shape[0] - 16) // 2 + 16
    shape = (rows, mine.shape[1])
    return pl.pallas_call(
        functools.partial(fold_kernel, planes),
        in_specs=[smem()] + [vmem()] * 2,
        out_specs=[vmem()] * 2,
        out_shape=[jax.ShapeDtypeStruct(shape, F32), jax.ShapeDtypeStruct(shape, BF)],
        compiler_params=params(8),
        name="fold",
    )(places, mine, got)


def add_kernel(a, b, out):
    out[...] = (a[...].astype(F32) + b[...].astype(F32)).astype(BF)


def add_low(a, b):
    return pl.pallas_call(
        add_kernel,
        in_specs=[vmem()] * 2,
        out_specs=vmem(),
        out_shape=jax.ShapeDtypeStruct(a.shape, BF),
        compiler_params=params(8),
        name="add_low",
    )(a, b)


def final_kernel(planes, places, mine, got, o0, o1, o2, o3, bias):
    is_low = place_of(places, planes, "core") == 0
    a, b = mine[...].astype(F32), got[...].astype(F32)
    both = jnp.concatenate([jnp.where(is_low, a, b), jnp.where(is_low, b, a)], 1)
    small = o0.shape[0]
    for i, out in enumerate((o0, o1, o2, o3)):
        out[...] = both[i * small : (i + 1) * small]
    bias[...] = both[4 * small : 4 * small + 8]


def finish(places, planes, mine, got):
    small = (mine.shape[0] - 16) // 4
    width = 2 * mine.shape[1]
    shapes = [jax.ShapeDtypeStruct((small, width), F32)] * 4 + [jax.ShapeDtypeStruct((8, width), F32)]
    return pl.pallas_call(
        functools.partial(final_kernel, planes),
        in_specs=[smem()] + [vmem()] * 2,
        out_specs=[vmem()] * 5,
        out_shape=shapes,
        compiler_params=params(8),
        name="finish",
    )(places, mine, got)


def permute(v, count, move):
    return lax.ppermute(v, AXES, [(i, move(i)) for i in range(count)])


def from_planes(parts, count):
    return [parts[0]] + [
        permute(parts[k], count, lambda i: (i + 8 * k) % count) for k in range(1, len(parts))
    ]


def gather_pair(v, count, bit, mine):
    got = permute(v, count, lambda i: i ^ bit)
    out = jnp.zeros((2,) + v.shape, v.dtype)
    out = lax.dynamic_update_slice_in_dim(out, v[None], mine, 0)
    return lax.dynamic_update_slice_in_dim(out, got[None], 1 - mine, 0)


def after(v, *others):
    return lax.optimization_barrier((v,) + others)[0]


def body(
    query_tokens, passage_tokens, query_length, passage_length, clusters, positives,
    w_query, b_query, w_key, w_value, b_value, w_mix, b_mix, gain_one, shift_one,
    w_inner, b_inner, w_outer, b_outer, gain_two, shift_two,
):
    pairs, query_rows, width = query_tokens.shape
    passage_rows = passage_tokens.shape[1]
    seqs = 2 * pairs
    batch_count = lax.axis_size("batch")
    count = batch_count * lax.axis_size("rep")
    planes = count // 8
    slab = width // planes
    me = lax.axis_index(AXES)
    z, y, x, core = me // 8, me // 4 % 2, me // 2 % 2, me % 2
    mats = whole_mats = (w_query, w_key, w_value, w_mix, w_inner, w_outer)
    vectors = (b_query, b_value, b_mix, gain_one, shift_one, b_outer, gain_two, shift_two, b_inner)
    batch_index = lax.axis_index("batch")
    first_rows, hidden_rows = width // batch_count, w_inner.shape[1] // batch_count

    def window(at, total, size):
        return jnp.minimum(at // LANES * LANES, total - size)

    slot = jnp.arange(2 * planes + len(PLACES), dtype=jnp.int32)
    places = jnp.where(
        slot < planes,
        window((z + slot) % planes * slab, width, 2 * LANES),
        (z - slot) % planes * seqs,
    )
    first_at, hidden_at = batch_index * first_rows, batch_index * hidden_rows
    first_off = window(first_at, width, 2 * LANES)
    hidden_off = window(hidden_at, w_inner.shape[1], window_size(hidden_rows))
    found = dict(
        own=me * seqs, line=me % 8, core=core, y=y, x=x,
        inside=z * slab - window(z * slab, width, 2 * LANES),
        first_off=first_off, first_inside=first_at - first_off,
        hidden_off=hidden_off, hidden_inside=hidden_at - hidden_off, pair=me * pairs,
    )
    for i, name in enumerate(PLACES):
        places = jnp.where(slot == 2 * planes + i, found[name], places)
    places = places.astype(jnp.int32)

    (packet, probs, a, pack, bi), mats, (near_query, near_passage), early = cls_forward(
        places, query_length, passage_length, positives, clusters,
        query_tokens, passage_tokens, mats, vectors, planes,
    )
    done = [None]

    def run(start, size, wait_for=None):
        lengths = passage_length
        if wait_for is not None:
            lengths, wait_for = lax.optimization_barrier((lengths, wait_for))
        done[0] = forward(near_passage, lengths, pack, bi, mats, False, start, size, done[0])
        return wait_for

    def hold(v):
        v, done[0] = lax.optimization_barrier((v, done[0]))
        return v

    def backward(packet_a, packet_b):
        if 2 * packet_a.shape[0] * seqs <= KERNEL_ROWS:
            return cls_backward(
                places, packet_a, packet_b, pack, bi, mats, near_query, near_passage, probs, a, planes, batch_count
            )
        return plain_backward(
            places, packet_a, packet_b, pack, bi, whole_mats, query_tokens, passage_tokens, probs, a, planes, batch_count
        )

    parts = from_planes([packet] * planes, count)
    cuts = [pairs * i // 8 for i in (2, 3, 4, 6)]
    run(0, cuts[0])
    parts[-1] = hold(parts[-1])
    packet = place_planes(places, parts)
    packet = run(cuts[0], cuts[1] - cuts[0], packet)
    early = list(early)
    early[0], packet = lax.optimization_barrier((early[0], packet))
    early = from_planes(early, count)
    got = hold(permute(packet, count, lambda i: i ^ 4))
    packet = place_pair(places, planes, "y", packet, got)
    packet = run(cuts[1], cuts[2] - cuts[1], packet)
    got = hold(permute(packet, count, lambda i: i ^ 2))
    got, early[-1] = lax.optimization_barrier((got, early[-1]))
    packet = place_pair(places, planes, "x", packet, got)
    got = permute(packet, count, lambda i: i ^ 1)
    (
        (grad_w_outer, grad_w_inner, sums, grad_b_inner, line_att, line_mix, dp_q, dp_p, ab, at_start),
        late,
    ) = backward(packet, got)
    if grad_w_inner.shape[0] != first_rows:
        grad_w_inner = lax.dynamic_slice_in_dim(
            grad_w_inner, first_at - first_off, first_rows, 0
        )

    late = list(late)
    late[0] = run(cuts[2], cuts[3] - cuts[2], late[0])
    late = from_planes(late, count)
    late[-1] = hold(late[-1])
    mine, other = partial_sums(places, line_att, line_mix, early, late, slab)
    got = permute(other, count, lambda i: i ^ 1)
    mine, other = fold(places, planes, mine, got)
    other = run(cuts[3], pairs - cuts[3], other)
    got = hold(permute(other, count, lambda i: i ^ 4))
    passage_out = done[0]
    mine = add_low(mine, got)
    lengths, mine = lax.optimization_barrier((query_length, mine))
    query_out = forward(near_query, lengths, pack, bi, mats, True, 0, pairs)
    got = permute(mine, count, lambda i: i ^ 2)
    got, query_out = lax.optimization_barrier((got, query_out))
    mine = add_low(mine, got)
    at_start, mine = lax.optimization_barrier((at_start, mine))
    query_grad, query_out = token_grads(dp_q, ab, at_start, query_out, 0, 1)
    passage_grad, passage_out = token_grads(dp_p, ab, at_start, passage_out, pairs, 2)
    got = permute(mine, count, lambda i: i ^ 1)
    grad_w_query, grad_w_key, grad_w_value, grad_w_mix, bias = finish(places, planes, mine, got)

    bias, sums, grad_b_inner, late_index = lax.optimization_barrier(
        (bias, sums, grad_b_inner, batch_index)
    )
    def piece(v, axis):
        size = v.shape[axis] // batch_count
        return lax.dynamic_slice_in_dim(v, late_index * size, size, axis)

    mean_loss = sums[7, 0] / (count * pairs)
    own = piece(jnp.concatenate([sums, bias[:1]]), 1)
    return (
        query_out, passage_out, mean_loss, query_grad, passage_grad,
        grad_w_query, own[8], grad_w_key, grad_w_value, own[6],
        grad_w_mix, own[5], own[3], own[4], grad_w_inner, piece(grad_b_inner[0], 0),
        grad_w_outer, own[0], own[1], own[2],
    )


def solution(mesh):
    rows = P(AXES, None, None)
    vector, matrix = P("batch"), P("batch", None)
    return jax.shard_map(
        body,
        mesh=mesh,
        in_specs=(rows, rows, P(AXES), P(AXES), P(), P(AXES)) + (P(),) * 15,
        out_specs=(
            rows, rows, P(), rows, rows,
            matrix, vector, matrix, matrix, vector,
            matrix, vector, vector, vector, matrix, vector,
            matrix, vector, vector, vector,
        ),
        check_vma=False,
    )
```

```python
import functools

import jax
import jax.numpy as jnp
from jax import lax
from jax.experimental import pallas as pl
from jax.experimental.pallas import tpu as pltpu
from jax.sharding import PartitionSpec as P

HEADS = 12
HEAD = 64
LANES = 128
AXES = ("batch", "rep")
BF = jnp.bfloat16
F32 = jnp.float32
MIB = 2**20
KERNEL_ROWS = 1024
B_QUERY, B_VALUE, B_MIX, GAIN_ONE, SHIFT_ONE, B_OUTER, GAIN_TWO, SHIFT_TWO = range(8)


def dot(a, b):
    return jnp.dot(a, b, preferred_element_type=F32)


def dot_nt(a, b):
    return lax.dot_general(a, b, (((1,), (1,)), ((), ())), preferred_element_type=F32)


def dot_tn(a, b):
    return lax.dot_general(a, b, (((0,), (0,)), ((), ())), preferred_element_type=F32)


def gelu(z):
    half = 0.5 * z
    return half + half * lax.erf(z * 0.5**0.5)


def gelu_slope(z):
    phi = jnp.exp(-0.5 * z * z) * 0.3989422804014327
    return 0.5 + 0.5 * lax.erf(z * 0.5**0.5) + z * phi


def center_scale(v):
    c = v - jnp.mean(v, axis=-1, keepdims=True)
    r = lax.rsqrt(jnp.mean(c * c, axis=-1, keepdims=True) + 1e-12)
    return c * r, r


def scores_of(qp, ka, own, sel):
    qa = jnp.concatenate([jnp.where(sel, qp, jnp.zeros_like(qp)), own], 1)
    return dot_nt(qa, ka)


def softened(scores):
    return jnp.exp(scores - jnp.max(scores, axis=-1, keepdims=True)).astype(BF)


def values_of(vp, key_low):
    zero, one = jnp.zeros_like(vp), jnp.ones_like(vp)
    top = jnp.concatenate([jnp.where(key_low, vp, zero), jnp.where(key_low, one, zero)], 1)
    low = jnp.concatenate([jnp.where(key_low, zero, vp), jnp.where(key_low, zero, one)], 1)
    return jnp.concatenate([top, low], 0)


def row(pack, index):
    return pack[index : index + 1, :]


def layer_rows(xs, own, biases, pack, bi, wq, wk, wv, wm, wi, wo, split):
    seqs = len(xs)
    rows, width = xs[0].shape
    x = jnp.concatenate(xs, 0)
    keys = biases[0].shape[0]
    wide = 2 * LANES
    groups = width // wide
    scale = HEAD**-0.5
    low = lax.broadcasted_iota(jnp.int32, (rows, LANES), 1) < HEAD
    key_low = lax.broadcasted_iota(jnp.int32, (keys, LANES), 1) < HEAD

    def projected(w, g, index=None, factor=None):
        cols = slice(g * wide, (g + 1) * wide)
        v = dot(x, w[:, cols])
        if index is not None:
            v = v + row(pack, index)[:, cols]
        if factor is not None:
            v = v * factor
        v = v.astype(BF)
        vs = [v[i * rows : (i + 1) * rows] for i in range(seqs)]
        if factor is not None or keys == rows:
            return vs
        return [jnp.concatenate([v, jnp.zeros((keys - rows, wide), BF)], 0) for v in vs]

    def pair_cols(p):
        return slice(p % 2 * LANES, (p % 2 + 1) * LANES)

    made = [(projected(wq, 0, B_QUERY, scale), projected(wk, 0), projected(wv, 0, B_VALUE))]

    def pair_scores(p):
        q, k, _ = made[p // 2]
        cols = pair_cols(p)
        out = []
        for i in range(seqs):
            ka = jnp.concatenate([k[i][:, cols], biases[i]], 1)
            out.append([scores_of(q[i][:, cols], ka, own, sel) for sel in (low, ~low)])
        return out

    ready = pair_scores(0)
    outs = [[] for _ in range(seqs)]
    for p in range(HEADS // 2):
        g = p // 2
        scores = ready
        if p % 2 == 0 and g + 1 < groups:
            part = projected(wq, g + 1, B_QUERY, scale), projected(wk, g + 1)
        if p % 2 == 1 and g + 1 < groups:
            made.append(part + (projected(wv, g + 1, B_VALUE),))
        if p + 1 < HEADS // 2:
            ready = pair_scores(p + 1)
        for i in range(seqs):
            e = jnp.concatenate([softened(v) for v in scores[i]], 1)
            o = dot(e, values_of(made[g][2][i][:, pair_cols(p)], key_low))
            outs[i].append((o[:, :LANES] / o[:, LANES:]).astype(BF))
    mixed = jnp.concatenate([jnp.concatenate(o, 1) for o in outs], 0)
    part = seqs * rows // split
    lows, accs = [], []
    for h in range(split):
        sl = slice(h * part, (h + 1) * part)
        nrm, _ = center_scale(x[sl].astype(F32) + dot(mixed[sl], wm[...]) + row(pack, B_MIX))
        first = nrm * row(pack, GAIN_ONE) + row(pack, SHIFT_ONE)
        lows.append(first.astype(BF))
        accs.append(first + row(pack, B_OUTER))
    for j in range(wi.shape[1] // width):
        cols = slice(j * width, (j + 1) * width)
        for h in range(split):
            z = dot(lows[h], wi[:, cols]) + bi[:, cols]
            accs[h] = accs[h] + dot(gelu(z).astype(BF), wo[cols, :])
    done = []
    for acc in accs:
        nrm, _ = center_scale(acc)
        done.append((nrm * row(pack, GAIN_TWO) + row(pack, SHIFT_TWO)).astype(BF))
    return jnp.concatenate(done, 0)


def forward_kernel(joint, group, start, len_ref, x_ref, pack, bi, wq, wk, wv, wm, wi, wo, *rest):
    out_ref = rest[-1]
    seqs, seq_rows, _ = x_ref.shape
    weights = (pack, bi, wq, wk, wv, wm, wi, wo)
    if joint:
        rows = seqs * seq_rows
        x = x_ref[...].reshape(rows, x_ref.shape[2])
        at = lax.broadcasted_iota(jnp.int32, (rows, LANES), 0)
        lane = lax.broadcasted_iota(jnp.int32, (rows, LANES), 1)
        length = jnp.zeros((rows, LANES), jnp.int32)
        for s in range(seqs):
            length = jnp.where(lane == s, len_ref[s], length)
        off = at - lane * seq_rows
        bias = jnp.where((off >= 0) & (off < length), 0.0, -1e30).astype(BF)
        own = jnp.where((off >= 0) & (off < seq_rows), 1.0, 0.0).astype(BF)

        out_ref[...] = layer_rows([x], own, [bias], *weights, 1).reshape(out_ref.shape)
        return
    biases = []
    for b in range(group):
        at_seq = start + pl.program_id(0) * group + b
        keys = -(-seq_rows // LANES) * LANES
        at = lax.broadcasted_iota(jnp.int32, (keys, LANES), 0)
        lane = lax.broadcasted_iota(jnp.int32, (keys, LANES), 1)
        biases.append(jnp.where((lane == 0) & (at >= len_ref[at_seq]), -1e30, 0.0).astype(BF))
    own = jnp.where(
        lax.broadcasted_iota(jnp.int32, (seq_rows, LANES), 1) == 0, 1.0, 0.0
    ).astype(BF)
    base = start + pl.program_id(0) * group

    v = layer_rows([x_ref[base + b] for b in range(group)], own, biases, *weights, group)
    for b in range(group):
        out_ref[base + b] = v[b * seq_rows : (b + 1) * seq_rows]


def forward(tokens, lengths, pack, bi, mats, joint, start, count, into=None):
    _, rows, width = tokens.shape
    total = count * rows
    weight_bytes = sum(m.size * 2 for m in mats)
    group = 2 if count % 2 == 0 else 1
    extra = [] if into is None else [in_vmem(into)]
    operands = [in_hbm(lengths), tokens, pack, bi, *mats] + extra
    return pl.pallas_call(
        functools.partial(forward_kernel, joint, group, start),
        grid=(1 if joint else count // group,),
        in_specs=[smem()] + [vmem()] * 9 + [anywhere()] * len(extra),
        out_specs=vmem(),
        out_shape=pltpu.VMEM(tokens.shape, BF),
        input_output_aliases={} if into is None else {len(operands) - 1: 0},
        compiler_params=params(16),
        cost_estimate=pl.CostEstimate(
            flops=int(total * weight_bytes * 1.9),
            bytes_accessed=weight_bytes + total * width * 4,
            transcendentals=total * 4096,
        ),
        name="forward_rows",
    )(*operands)


def head_of_lane(shape):
    return lax.broadcasted_iota(jnp.int32, shape, 1) // HEAD


def expand_heads(v):
    head = head_of_lane(v.shape)
    zero = jnp.zeros_like(v)
    return jnp.concatenate([jnp.where(head == h, v, zero) for h in range(HEADS)], 0)


def collapse_heads(v):
    seqs = v.shape[0] // HEADS
    out = jnp.zeros((seqs, v.shape[1]), v.dtype)
    head = head_of_lane(out.shape)
    for h in range(HEADS):
        out = jnp.where(head == h, v[h * seqs : (h + 1) * seqs], out)
    return out


SQUARE = ((0, 0), (0, 1), (1, 0), (1, 1))
PLACES = ("own", "line", "core", "y", "x", "inside", "first_off", "first_inside", "hidden_off", "hidden_inside", "pair")


def place_of(places, planes, name):
    return places[2 * planes + PLACES.index(name)]


def window_size(size):
    return size if size % LANES == 0 else 2 * LANES


def split3(v):
    hi = v.astype(BF)
    mid = (v - hi.astype(F32)).astype(BF)
    lo = (v - hi.astype(F32) - mid.astype(F32)).astype(BF)
    return hi, mid, lo


def load(pairs, sems):
    copies = [pltpu.make_async_copy(a, b, sems.at[i]) for i, (a, b) in enumerate(pairs)]
    for c in copies:
        c.start()
    return copies


def cls_kernel(places, query_len, passage_len, target, clusters, qt_h, pt_h, wq_h, wk_h, wv_h, wm_h, wi_h, wo_h, *rest):
    planes = len(rest) - 34
    vectors_h, (packet, probs_out, a_out, pack, bi), rest = rest[:9], rest[9:14], rest[14:]
    wq, wk, wv, wm, wi, wo, qt, pt = rest[:8]
    early = rest[8 : 8 + planes]
    px_s, pair_s, *vectors, sems = rest[8 + planes :]
    copies = load(
        (*zip(vectors_h, vectors), (qt_h, qt), (pt_h, pt), (wq_h, wq), (wk_h, wk), (wv_h, wv), (wm_h, wm), (wi_h, wi), (wo_h, wo)),
        sems,
    )
    small, (q_copy, p_copy), copies = copies[:9], copies[9:11], copies[11:]
    for c in small:
        c.wait()
    for i, v in enumerate(vectors[:8]):
        pack[i : i + 1, :] = v[...].astype(F32).reshape(1, -1)
    bi[...] = vectors[8][...].astype(F32).reshape(1, -1)
    pairs, query_rows, width = qt.shape
    passage_rows = pt.shape[1]
    seqs = 2 * pairs
    at = lax.broadcasted_iota(jnp.int32, (seqs, width), 0)
    start = jnp.zeros((seqs, width), F32)
    q_copy.wait()
    p_copy.wait()
    for s in range(seqs):
        src = qt[s, 0:16, :] if s < pairs else pt[s - pairs, 0:16, :]
        start = jnp.where(at == s, src.astype(F32)[0:1, :], start)
    low_start = start.astype(BF)
    copies[0].wait()
    q0 = (dot(low_start, wq[...]) + row(pack, B_QUERY)).astype(BF)
    copies[1].wait()
    a = (dot_nt(expand_heads(q0), wk[...]) * HEAD**-0.5).astype(BF)
    a_out[...] = a
    xq = qt[...].reshape(pairs * query_rows, width)
    xp = pt[...].reshape(pairs * passage_rows, width)
    scores = jnp.concatenate([dot_nt(a, xq), dot_nt(a, xp)], 1)
    s_row = lax.broadcasted_iota(jnp.int32, (HEADS * seqs, 1), 0) % seqs
    lo = jnp.zeros((HEADS * seqs, 1), jnp.int32)
    hi = jnp.zeros((HEADS * seqs, 1), jnp.int32)
    for s in range(seqs):
        if s < pairs:
            first_at, length = s * query_rows, query_len[s]
        else:
            first_at = pairs * query_rows + (s - pairs) * passage_rows
            length = passage_len[s - pairs]
        lo = jnp.where(s_row == s, first_at, lo)
        hi = jnp.where(s_row == s, first_at + length, hi)
    column = lax.broadcasted_iota(jnp.int32, scores.shape, 1)
    scores = jnp.where((column >= lo) & (column < hi), scores, -1e30)
    e = jnp.exp(scores - jnp.max(scores, axis=-1, keepdims=True))
    probs = e / jnp.sum(e, axis=-1, keepdims=True)
    probs_out[...] = probs
    probs = probs.astype(BF)
    cut = pairs * query_rows
    px = (dot(probs[:, :cut], xq) + dot(probs[:, cut:], xp)).astype(BF)
    px_s[...] = px
    copies[2].wait()
    mixed = (collapse_heads(dot(px, wv[...])) + row(pack, B_VALUE)).astype(BF)
    pair_s[0:seqs, :] = low_start
    pair_s[seqs : 2 * seqs, :] = mixed
    heads_rows = HEADS * seqs
    for k, out in enumerate(early):
        window = pl.ds(pl.multiple_of(places[k], LANES), 2 * LANES)
        out[0:heads_rows, :] = px_s[:, window]
        out[heads_rows : heads_rows + 2 * seqs, :] = pair_s[:, window]
        for j in range(width // (2 * LANES)):
            base = heads_rows + (2 + j) * seqs
            out[base : base + seqs, :] = q0[:, j * 2 * LANES : (j + 1) * 2 * LANES]
    copies[3].wait()
    nrm, r_one = center_scale(start + dot(mixed, wm[...]) + row(pack, B_MIX))
    first = nrm * row(pack, GAIN_ONE) + row(pack, SHIFT_ONE)
    low = first.astype(BF)
    acc = first + row(pack, B_OUTER)
    copies[4].wait()
    hidden = gelu(dot(low, wi[...]) + bi[...]).astype(BF)
    copies[5].wait()
    acc = acc + dot(hidden, wo[...])
    nrm, r_two = center_scale(acc)
    packet[:, :width] = (nrm * row(pack, GAIN_TWO) + row(pack, SHIFT_TWO)).astype(BF)
    packet[:, width : 2 * width] = low
    lane = lax.broadcasted_iota(jnp.int32, (seqs, LANES), 1)
    at = lax.broadcasted_iota(jnp.int32, (seqs, LANES), 0)
    wanted = jnp.zeros((seqs, LANES), jnp.int32)
    cluster = jnp.zeros((seqs, LANES), jnp.int32)
    base = place_of(places, planes, "pair")
    for s in range(seqs):
        cluster = jnp.where(at == s, clusters[base + s % pairs], cluster)
        if s < pairs:
            wanted = jnp.where(at == s, target[s], wanted)
    extra = jnp.zeros((seqs, LANES), jnp.int32)
    for j, v in enumerate((wanted // LANES, wanted % LANES, cluster // LANES, cluster % LANES)):
        extra = jnp.where(lane == 6 + j, v, extra)
    extra = extra.astype(F32)
    for j, part in enumerate(split3(r_one) + split3(r_two)):
        extra = jnp.where(lane == j, part.astype(F32), extra)
    packet[:, 2 * width :] = extra.astype(BF)


def vmem():
    return pl.BlockSpec(memory_space=pltpu.VMEM)


def smem():
    return pl.BlockSpec(memory_space=pltpu.SMEM)


def anywhere():
    return pl.BlockSpec(memory_space=pl.ANY)


def params(mib):
    return pltpu.CompilerParams(vmem_limit_bytes=mib * MIB)


def in_hbm(v):
    return pltpu.with_memory_space_constraint(v, pltpu.HBM)


def in_vmem(v):
    return pltpu.with_memory_space_constraint(v, pltpu.VMEM)


def cls_forward(places, query_length, passage_length, positives, clusters, query_tokens, passage_tokens, mats, vectors, planes):
    pairs, query_rows, width = query_tokens.shape
    seqs = 2 * pairs
    tokens = pairs * (query_rows + passage_tokens.shape[1])
    early_rows = seqs * (HEADS + 2 + width // (2 * LANES))
    outs = [
        jax.ShapeDtypeStruct((seqs, 2 * width + LANES), BF),
        pltpu.VMEM((HEADS * seqs, tokens), F32),
        pltpu.VMEM((HEADS * seqs, width), BF),
        jax.ShapeDtypeStruct((8, width), F32),
        jax.ShapeDtypeStruct((1, mats[4].shape[1]), F32),
    ]
    outs += [pltpu.VMEM(v.shape, v.dtype) for v in (*mats, query_tokens, passage_tokens)]
    outs += [jax.ShapeDtypeStruct((early_rows, 2 * LANES), BF)] * planes
    got = pl.pallas_call(
        cls_kernel,
        in_specs=[smem()] * 5 + [anywhere()] * 17,
        out_specs=[vmem()] * len(outs),
        out_shape=outs,
        scratch_shapes=[
            pltpu.VMEM((HEADS * seqs, width), BF),
            pltpu.VMEM((2 * seqs, width), BF),
            *[pltpu.VMEM(v.shape, v.dtype) for v in vectors],
            pltpu.SemaphoreType.DMA((17,)),
        ],
        compiler_params=params(16),
        cost_estimate=pl.CostEstimate(flops=8 * 10**9, bytes_accessed=20 * 10**6, transcendentals=0),
        name="cls_forward",
    )(
        places, *[in_hbm(v) for v in (query_length, passage_length, positives, clusters)],
        in_hbm(query_tokens), in_hbm(passage_tokens), *[in_hbm(m) for m in mats], *[in_hbm(v) for v in vectors],
    )
    kept = [in_vmem(v) for v in got[5:13]]
    return got[:5], kept[:6], kept[6:], got[13:]


def place_planes_kernel(places, *refs):
    *parts, out = refs
    for k, part in enumerate(parts):
        at = places[len(parts) + k]
        out[pl.ds(at // part.shape[0], 1)] = part[...][None]


def place_planes(places, parts):
    shape = (len(parts),) + parts[0].shape
    return pl.pallas_call(
        place_planes_kernel,
        in_specs=[smem()] + [vmem()] * len(parts),
        out_specs=vmem(),
        out_shape=jax.ShapeDtypeStruct(shape, BF),
        compiler_params=params(8),
        name="place_planes",
    )(places, *parts)


def place_square_kernel(planes, places, *refs):
    *parts, out = refs
    y, x = place_of(places, planes, "y"), place_of(places, planes, "x")
    for (dy, dx), part in zip(SQUARE, parts):
        at_y, at_x = (1 - y if dy else y), (1 - x if dx else x)
        out[:, pl.ds(at_y * 2 + at_x, 1)] = part[...][:, None]


def place_square(places, planes, parts):
    v = parts[0]
    out = pl.pallas_call(
        functools.partial(place_square_kernel, planes),
        in_specs=[smem()] + [vmem()] * 4,
        out_specs=vmem(),
        out_shape=jax.ShapeDtypeStruct((planes, 4) + v.shape[1:], BF),
        compiler_params=params(8),
        name="place_square",
    )(places, *parts)
    return out.reshape((-1,) + v.shape[1:])


def norm_back(grad, nrm, r, gain):
    g = grad * gain
    return r * (
        g - jnp.mean(g, axis=-1, keepdims=True) - nrm * jnp.mean(g * nrm, axis=-1, keepdims=True)
    )


def back_kernel(
    planes, slice_first, places, packet_a, packet_b, pack, bi, wq, wk, wv, wm, wi, wo,
    qt, pt, probs_ref, a_ref, *rest,
):
    grad_wo_h, grad_wi_h, vectors, grad_bi, line_att, line_mix, dp_out, ab_out = rest[:8]
    late = rest[8 : 8 + planes]
    grad_wo, grad_wi, packet_s, mix_s, line_s, start_s, xs_s, win_s, sems = rest[8 + planes :]
    sent = []

    def send(a, b):
        copy = pltpu.make_async_copy(a, b, sems.at[len(sent)])
        copy.start()
        sent.append(copy)

    core = place_of(places, planes, "core")
    packet_s[:, pl.ds(core, 1)] = packet_a[...][:, None]
    packet_s[:, pl.ds(1 - core, 1)] = packet_b[...][:, None]
    pairs, query_rows, width = qt.shape
    passage_rows = pt.shape[1]
    seqs = 2 * pairs
    packet = packet_s[...].reshape(-1, packet_s.shape[-1])
    rows = packet.shape[0]
    scale = 2.0 * width**-0.5

    cls = packet[:, :width]
    tail = packet[:, 2 * width :].astype(F32)
    scores = dot_nt(cls, cls) * scale
    is_query = lax.broadcasted_iota(jnp.int32, (rows, 1), 0) % seqs < pairs
    is_passage = lax.broadcasted_iota(jnp.int32, (1, rows), 1) % seqs >= pairs
    wanted = (tail[:, 6:7] * LANES + tail[:, 7:8]).astype(jnp.int32)
    column = lax.broadcasted_iota(jnp.int32, (1, rows), 1)
    chosen = (column // seqs * pairs + column % pairs == wanted) & is_passage
    across = tail.T
    cluster_row = across[8:9, :] * LANES + across[9:10, :]
    cluster_col = tail[:, 8:9] * LANES + tail[:, 9:10]
    counted = ((cluster_row != cluster_col) | chosen) & is_passage
    masked = jnp.where(counted, scores, -1e30)
    peak = jnp.max(masked, axis=1, keepdims=True)
    log_total = peak + jnp.log(jnp.sum(jnp.exp(masked - peak), axis=1, keepdims=True))
    one = jnp.where(chosen, 1.0, 0.0)
    picked = jnp.sum(one * scores, axis=1, keepdims=True)
    loss = jnp.sum(jnp.where(is_query, log_total - picked, 0.0), axis=0, keepdims=True)
    d_pair = jnp.where(is_query, jnp.exp(masked - log_total) - one, 0.0).astype(BF)
    d_cls = (dot(d_pair, cls) + dot_tn(d_pair, cls)) * scale

    first = packet[:, width : 2 * width]
    nrm_two = (cls.astype(F32) - row(pack, SHIFT_TWO)) / row(pack, GAIN_TWO)
    r_two = tail[:, 3:4] + tail[:, 4:5] + tail[:, 5:6]
    d_second = norm_back(d_cls, nrm_two, r_two, row(pack, GAIN_TWO))
    d_outer = d_second.astype(BF)
    vectors[0:1, :] = jnp.sum(d_outer.astype(F32), axis=0, keepdims=True)
    vectors[1:2, :] = jnp.sum(d_cls * nrm_two, axis=0, keepdims=True)
    vectors[2:3, :] = jnp.sum(d_cls, axis=0, keepdims=True)
    piece = grad_wi.shape[0]
    first_window = pl.ds(
        pl.multiple_of(place_of(places, planes, "first_off"), LANES), 2 * LANES
    )
    mix_s[...] = first
    first_piece = mix_s[:, first_window]
    inside = pl.ds(pl.multiple_of(place_of(places, planes, "first_inside"), 8), piece)
    d_first = d_second
    for j in range(wi.shape[1] // width):
        cols = slice(j * width, (j + 1) * width)
        inner = dot(first, wi[:, cols]) + bi[:, cols]
        d_inner = (dot_nt(d_outer, wo[cols, :]) * gelu_slope(inner)).astype(BF)
        d_first = d_first + dot_nt(d_inner, wi[:, cols])
        found = dot_tn(first_piece, d_inner)
        if slice_first:
            win_s[: 2 * LANES, :] = found
            found = win_s[inside, :]
        grad_wi[:, cols] = found
        send(grad_wi.at[:, cols], grad_wi_h.at[:, cols])
        grad_bi[:, cols] = jnp.sum(d_inner.astype(F32), axis=0, keepdims=True)
    size = grad_wo.shape[0]
    off = pl.multiple_of(place_of(places, planes, "hidden_off"), LANES)
    window = pl.ds(off, window_size(size))
    hidden = gelu(dot(first, wi[:, window]) + bi[:, window]).astype(BF)
    found = dot_tn(hidden, d_outer)
    if size != window_size(size):
        win_s[: window_size(size), :] = found
        found = win_s[pl.ds(pl.multiple_of(place_of(places, planes, "hidden_inside"), 8), size), :]
    grad_wo[...] = found
    send(grad_wo, grad_wo_h)
    nrm_one = (first.astype(F32) - row(pack, SHIFT_ONE)) / row(pack, GAIN_ONE)
    r_one = tail[:, 0:1] + tail[:, 1:2] + tail[:, 2:3]
    d_start = norm_back(d_first, nrm_one, r_one, row(pack, GAIN_ONE))
    vectors[3:4, :] = jnp.sum(d_first * nrm_one, axis=0, keepdims=True)
    vectors[4:5, :] = jnp.sum(d_first, axis=0, keepdims=True)
    start_s[...] = d_start
    d_attended = d_start.astype(BF)
    vectors[5:6, :] = jnp.sum(d_attended.astype(F32), axis=0, keepdims=True)
    d_mixed = dot_nt(d_attended, wm[...]).astype(BF)
    vectors[6:7, :] = jnp.sum(d_mixed.astype(F32), axis=0, keepdims=True)
    vectors[7:8, :] = jnp.broadcast_to(loss * (2.0 / rows), (1, width))
    line_rows = line_att.shape[0]
    by_line = (planes, rows // line_rows, seqs, width)
    line = pl.ds(place_of(places, planes, "line"), 1)
    line_s[...] = d_attended.reshape(by_line)
    line_att[...] = line_s[:, line].reshape(line_rows, width)
    line_s[...] = d_mixed.reshape(by_line)
    line_mix[...] = line_s[:, line].reshape(line_rows, width)
    mix_s[...] = d_mixed

    own = pl.ds(pl.multiple_of(place_of(places, planes, "own"), seqs), seqs)
    own_mixed = mix_s[own, :]
    bm = dot_nt(expand_heads(own_mixed), wv[...]).astype(BF)
    xq = qt[...].reshape(pairs * query_rows, width)
    xp = pt[...].reshape(pairs * passage_rows, width)
    d_probs = jnp.concatenate([dot_nt(bm, xq), dot_nt(bm, xp)], 1)
    probs = probs_ref[...]
    d_scores = (probs * (d_probs - jnp.sum(probs * d_probs, axis=-1, keepdims=True))).astype(BF)
    cut = pairs * query_rows
    xs = (dot(d_scores[:, :cut], xq) + dot(d_scores[:, cut:], xp)).astype(BF)
    xs_s[...] = xs
    d_query = (collapse_heads(dot(xs, wk[...])) * HEAD**-0.5).astype(BF)
    heads_rows = HEADS * seqs
    for k, out in enumerate(late):
        window = pl.ds(pl.multiple_of(places[k], LANES), 2 * LANES)
        out[0:heads_rows, :] = xs_s[:, window]
        for j in range(width // (2 * LANES)):
            base = heads_rows + j * seqs
            out[base : base + seqs, :] = d_query[:, j * 2 * LANES : (j + 1) * 2 * LANES]
    dp_out[0:heads_rows, :] = d_scores
    dp_out[heads_rows : 2 * heads_rows, :] = probs.astype(BF)
    shape = (seqs, dp_out.shape[1])
    seq = lax.broadcasted_iota(jnp.int32, shape, 0)
    first_row = jnp.where(seq < pairs, seq * query_rows, cut + (seq - pairs) * passage_rows)
    first_row = jnp.where(lax.broadcasted_iota(jnp.int32, shape, 1) == first_row, 1.0, 0.0).astype(BF)
    ab_out[0:heads_rows, :] = a_ref[...]
    ab_out[heads_rows : 2 * heads_rows, :] = bm
    at_start = dot_nt(d_query, wq[...]) + start_s[own, :]
    for j, part in enumerate(split3(at_start)):
        rows_of = slice(2 * heads_rows + j * seqs, 2 * heads_rows + (j + 1) * seqs)
        ab_out[rows_of, :] = part
        dp_out[rows_of, :] = first_row
    for copy in sent:
        copy.wait()


def cls_backward(places, packet_a, packet_b, pack, bi, mats, query_tokens, passage_tokens, probs, a, planes, batch_count):
    pairs, _, width = query_tokens.shape
    seqs = 2 * pairs
    blocks = packet_a.shape[0]
    rows = 2 * blocks * seqs
    late_rows = seqs * (HEADS + width // (2 * LANES))
    factors = (2 * HEADS + 3) * seqs
    hidden = mats[4].shape[1]
    first_rows, hidden_rows = width // batch_count, hidden // batch_count
    slice_first = first_rows % 8 == 0

    def out(shape, kind):
        return jax.ShapeDtypeStruct(shape, kind)

    outs = [
        pltpu.HBM((hidden_rows, width), F32),
        pltpu.HBM((first_rows if slice_first else 2 * LANES, hidden), F32),
        out((8, width), F32),
        out((1, hidden), F32),
        out((planes * seqs, width), BF),
        out((planes * seqs, width), BF),
        pltpu.VMEM((factors, probs.shape[1]), BF),
        pltpu.VMEM((factors, width), BF),
    ] + [out((late_rows, 2 * LANES), BF)] * planes
    got = pl.pallas_call(
        functools.partial(back_kernel, planes, slice_first),
        in_specs=[smem()] + [vmem()] * 14,
        out_specs=[anywhere()] * 2 + [vmem()] * (len(outs) - 2),
        out_shape=outs,
        scratch_shapes=[
            pltpu.VMEM(outs[0].shape, F32),
            pltpu.VMEM(outs[1].shape, F32),
            pltpu.VMEM((blocks, 2) + packet_a.shape[1:], BF),
            pltpu.VMEM((rows, width), BF),
            pltpu.VMEM((planes, rows // (planes * seqs), seqs, width), BF),
            pltpu.VMEM((rows, width), F32),
            pltpu.VMEM((HEADS * seqs, width), BF),
            pltpu.VMEM((2 * LANES, width), F32),
            pltpu.SemaphoreType.DMA((hidden // width + 1,)),
        ],
        compiler_params=params(22),
        cost_estimate=pl.CostEstimate(flops=16 * 10**9, bytes_accessed=25 * 10**6, transcendentals=0),
        name="cls_backward",
    )(
        places, packet_a, packet_b, pack, bi, *mats,
        query_tokens, passage_tokens, in_vmem(probs), in_vmem(a),
    )
    return got[:8], got[8:]


def plain_backward(places, packet_a, packet_b, pack, bi, mats, query_tokens, passage_tokens, probs, a, planes, batch_count):
    wq, wk, wv, wm, wi, wo = mats
    pairs, query_rows, width = query_tokens.shape
    seqs = 2 * pairs
    blocks = packet_a.shape[0]
    rows = 2 * blocks * seqs
    cut = pairs * query_rows
    hidden = wi.shape[1]

    def at(name):
        return places[2 * planes + PLACES.index(name)]

    core = at("core")
    packet = jnp.stack(
        [jnp.where(core == 0, packet_a, packet_b), jnp.where(core == 0, packet_b, packet_a)], 1
    )
    packet = packet.reshape(2 * blocks, seqs, -1)
    cls_query = packet[:, :pairs, :width].reshape(-1, width)
    cls_passage = packet[:, pairs:, :width].reshape(-1, width)
    packet = packet.reshape(rows, -1)
    tail = packet[:, 2 * width :].astype(F32)

    def sides(v):
        v = v.reshape(2 * blocks, seqs)
        return v[:, :pairs].reshape(-1), v[:, pairs:].reshape(-1)

    scale = 2.0 * width**-0.5
    scores = dot_nt(cls_query, cls_passage) * scale
    wanted = sides(tail[:, 6] * LANES + tail[:, 7])[0]
    query_cluster, passage_cluster = sides(tail[:, 8] * LANES + tail[:, 9])
    chosen = jnp.arange(scores.shape[1], dtype=F32)[None] == wanted[:, None]
    counted = (query_cluster[:, None] != passage_cluster[None]) | chosen
    masked = jnp.where(counted, scores, -1e30)
    log_total = jax.nn.logsumexp(masked, axis=1, keepdims=True)
    one = chosen.astype(F32)
    loss = jnp.sum(log_total - jnp.sum(one * scores, axis=1, keepdims=True))
    d_pair = (jnp.exp(masked - log_total) - one).astype(BF)
    d_cls = jnp.concatenate(
        [
            dot(d_pair, cls_passage).reshape(2 * blocks, pairs, width),
            dot_tn(d_pair, cls_query).reshape(2 * blocks, pairs, width),
        ],
        1,
    ).reshape(rows, width) * scale
    first = packet[:, width : 2 * width]
    nrm_two = (packet[:, :width].astype(F32) - row(pack, SHIFT_TWO)) / row(pack, GAIN_TWO)
    nrm_one = (first.astype(F32) - row(pack, SHIFT_ONE)) / row(pack, GAIN_ONE)
    d_second = norm_back(
        d_cls, nrm_two, jnp.sum(tail[:, 3:6], 1, keepdims=True), row(pack, GAIN_TWO)
    )
    d_outer = d_second.astype(BF)
    hidden_rows, first_rows = hidden // batch_count, width // batch_count
    hidden_at = at("hidden_off") + at("hidden_inside")
    first_at = at("first_off") + at("first_inside")
    wi_piece = lax.dynamic_slice_in_dim(wi, hidden_at, hidden_rows, 1)
    bi_piece = lax.dynamic_slice_in_dim(bi, hidden_at, hidden_rows, 1)

    def block(parts):
        first, d_outer = parts
        d_inner = (dot_nt(d_outer, wo) * gelu_slope(dot(first, wi) + bi)).astype(BF)
        return d_inner, dot_nt(d_inner, wi), gelu(dot(first, wi_piece) + bi_piece).astype(BF)

    size = rows // 8
    parts = first.reshape(-1, size, width), d_outer.reshape(-1, size, width)
    d_inner, more, hidden_piece = (v.reshape(rows, -1) for v in lax.map(block, parts))
    d_first = d_second + more
    first_piece = lax.dynamic_slice_in_dim(first, first_at, first_rows, 1)
    grad_wo, grad_wi = dot_tn(hidden_piece, d_outer), dot_tn(first_piece, d_inner)
    if first_rows % 8:
        grad_wi = lax.dynamic_update_slice_in_dim(
            jnp.zeros((2 * LANES, hidden), F32), grad_wi, at("first_inside"), 0
        )
    d_start = norm_back(
        d_first, nrm_one, jnp.sum(tail[:, 0:3], 1, keepdims=True), row(pack, GAIN_ONE)
    )
    d_attended = d_start.astype(BF)
    d_mixed = dot_nt(d_attended, wm).astype(BF)
    sums = (d_outer, d_cls * nrm_two, d_cls, d_first * nrm_one, d_first, d_attended, d_mixed)
    vectors = [jnp.sum(v.astype(F32), 0) for v in sums] + [jnp.full((width,), loss * (2.0 / rows))]

    def line(v):
        v = v.reshape(planes, -1, seqs, width)
        return lax.dynamic_slice_in_dim(v, at("line"), 1, 1).reshape(planes * seqs, width)

    def own(v):
        return lax.dynamic_slice_in_dim(v, at("own"), seqs, 0)

    bm = dot_nt(expand_heads(own(d_mixed)), wv).astype(BF)
    xq = query_tokens.reshape(-1, width)
    xp = passage_tokens.reshape(-1, width)
    d_probs = jnp.concatenate([dot_nt(bm, xq), dot_nt(bm, xp)], 1)
    d_scores = (probs * (d_probs - jnp.sum(probs * d_probs, axis=-1, keepdims=True))).astype(BF)
    xs = (dot(d_scores[:, :cut], xq) + dot(d_scores[:, cut:], xp)).astype(BF)
    d_query = (collapse_heads(dot(xs, wk)) * HEAD**-0.5).astype(BF)
    blocks_of_query = [
        d_query[:, j : j + 2 * LANES] for j in range(0, width, 2 * LANES)
    ]
    late = [
        jnp.concatenate(
            [lax.dynamic_slice_in_dim(xs, places[k], 2 * LANES, 1)] + blocks_of_query
        )
        for k in range(planes)
    ]
    at_start = [lax.reduce_precision(dot_nt(d_query, wq) + own(d_start), 8, 23)]
    for _ in range(2):
        high = lax.reduce_precision(at_start[-1], 8, 7)
        at_start[-1:] = [high, at_start[-1] - high]
    seq = jnp.arange(seqs)
    first_row = jnp.where(seq < pairs, seq * query_rows, cut + (seq - pairs) * passage_tokens.shape[1])
    first_row = (jnp.arange(probs.shape[1])[None] == first_row[:, None]).astype(BF)
    dp = jnp.concatenate([d_scores, probs.astype(BF)] + [first_row] * 3)
    ab = jnp.concatenate([a, bm] + [v.astype(BF) for v in at_start])
    return (
        grad_wo, grad_wi, jnp.stack(vectors), jnp.sum(d_inner.astype(F32), 0, keepdims=True),
        line(d_attended), line(d_mixed), dp, ab,
    ), late


def tokens_kernel(dp, ab, near_q, near_p, out_q, out_p, far_q, far_p, stage, sems):
    copies = [
        pltpu.make_async_copy(near_q, far_q, sems.at[0]),
        pltpu.make_async_copy(near_p, far_p, sems.at[1]),
    ]
    for c in copies:
        c.start()
    size = stage.shape[1]
    chunks = [(out_q, i) for i in range(0, out_q.shape[0], size)]
    chunks += [(out_p, i) for i in range(0, out_p.shape[0], size)]
    for n, (out, at) in enumerate(chunks):
        stage[n] = dot_tn(dp[:, n * size : (n + 1) * size], ab[...])
        copy = pltpu.make_async_copy(stage.at[n], out.at[pl.ds(at, size)], sems.at[2 + n])
        copy.start()
        copies.append(copy)
    for c in copies:
        c.wait()


def token_grads(dp, ab, near_q, near_p):
    width = ab.shape[1]
    sides = (near_q, near_p)
    chunks = dp.shape[1] // (2 * LANES)
    got = pl.pallas_call(
        tokens_kernel,
        in_specs=[vmem()] * 2 + [anywhere()] * 2,
        out_specs=[anywhere()] * 4,
        out_shape=[pltpu.HBM((v.shape[0] * v.shape[1], width), F32) for v in sides]
        + [pltpu.HBM(v.shape, BF) for v in sides],
        scratch_shapes=[
            pltpu.VMEM((chunks, 2 * LANES, width), F32),
            pltpu.SemaphoreType.DMA((2 + chunks,)),
        ],
        compiler_params=params(16),
        cost_estimate=pl.CostEstimate(flops=3 * 10**9, bytes_accessed=12 * 10**6, transcendentals=0),
        name="token_grads",
    )(in_vmem(dp), in_vmem(ab), in_vmem(near_q), in_vmem(near_p))
    return got[0].reshape(near_q.shape), got[1].reshape(near_p.shape), got[2], got[3]


def sums_kernel(places, line_att, line_mix, *rest):
    planes = (len(rest) - 3) // 2
    early, late = rest[:planes], rest[planes : 2 * planes]
    mine, other, win = rest[2 * planes :]
    width = line_att.shape[1]
    wide = 2 * LANES
    seqs = line_att.shape[0] // planes
    heads_rows = HEADS * seqs

    def unfold(ref, base):
        return jnp.concatenate(
            [ref[base + j * seqs : base + (j + 1) * seqs, :] for j in range(width // wide)], 1
        )

    xs, px, starts, mixed, q0, dq, dm, da = ([] for _ in range(8))
    for k in range(planes):
        e, l = early[k], late[k]
        at = pl.ds(pl.multiple_of(places[planes + k], seqs), seqs)
        px.append(e[0:heads_rows, :])
        starts.append(e[heads_rows : heads_rows + seqs, :])
        mixed.append(e[heads_rows + seqs : heads_rows + 2 * seqs, :])
        q0.append(expand_heads(unfold(e, heads_rows + 2 * seqs)))
        xs.append(l[0:heads_rows, :])
        dq.append(unfold(l, heads_rows))
        dm.append(expand_heads(line_mix[at, :]))
        da.append(line_att[at, :])
    cat = functools.partial(jnp.concatenate, axis=0)
    dq = cat(dq)
    found = (
        dot_tn(cat(starts), dq),
        dot_tn(cat(xs), cat(q0)) * HEAD**-0.5,
        dot_tn(cat(px), cat(dm)),
        dot_tn(cat(mixed), cat(da)),
    )
    bias = jnp.broadcast_to(jnp.sum(dq.astype(F32), axis=0, keepdims=True), (16, width))
    slab = (mine.shape[0] - 16) // 4
    half = width // 2
    inside = pl.ds(pl.multiple_of(place_of(places, planes, "inside"), 8), slab)
    is_low = place_of(places, planes, "core") == 0
    for i in range(5):
        if i < 4:
            win[...] = found[i]
            v = win[inside, :]
        else:
            v = bias
        to = slice(i * slab, i * slab + v.shape[0])
        a, b = v[:, :half], v[:, half:]
        mine[to, :] = jnp.where(is_low, a, b)
        other[to, :] = jnp.where(is_low, b, a).astype(BF)


def partial_sums(places, line_att, line_mix, early, late, slab):
    width = line_att.shape[1]
    shape = (4 * slab + 16, width // 2)
    return pl.pallas_call(
        sums_kernel,
        in_specs=[smem()] + [vmem()] * (2 + 2 * len(early)),
        out_specs=[vmem()] * 2,
        out_shape=[jax.ShapeDtypeStruct(shape, F32), jax.ShapeDtypeStruct(shape, BF)],
        scratch_shapes=[pltpu.VMEM((2 * LANES, width), F32)],
        compiler_params=params(12),
        cost_estimate=pl.CostEstimate(flops=2 * 10**9, bytes_accessed=4 * 10**6, transcendentals=0),
        name="partial_sums",
    )(places, line_att, line_mix, *early, *late)


def fold_kernel(planes, places, mine, got, keep, send):
    total = mine[...] + got[...].astype(F32)
    slab = (mine.shape[0] - 16) // 4
    small = slab // 2
    is_low = place_of(places, planes, "y") == 0
    for i in range(5):
        base = i * slab
        if i < 4:
            a, b = total[base : base + small], total[base + small : base + slab]
            v, w = jnp.where(is_low, a, b), jnp.where(is_low, b, a)
        else:
            v = w = total[base : base + 16]
        to = slice(i * small, i * small + v.shape[0])
        keep[to, :] = v
        send[to, :] = w.astype(BF)


def fold(places, planes, mine, got):
    rows = (mine.shape[0] - 16) // 2 + 16
    shape = (rows, mine.shape[1])
    return pl.pallas_call(
        functools.partial(fold_kernel, planes),
        in_specs=[smem()] + [vmem()] * 2,
        out_specs=[vmem()] * 2,
        out_shape=[jax.ShapeDtypeStruct(shape, F32), jax.ShapeDtypeStruct(shape, BF)],
        compiler_params=params(8),
        name="fold",
    )(places, mine, got)


def add_kernel(a, b, out):
    out[...] = (a[...].astype(F32) + b[...].astype(F32)).astype(BF)


def add_low(a, b):
    return pl.pallas_call(
        add_kernel,
        in_specs=[vmem()] * 2,
        out_specs=vmem(),
        out_shape=jax.ShapeDtypeStruct(a.shape, BF),
        compiler_params=params(8),
        name="add_low",
    )(a, b)


def take_lanes(v, off, inside, size):
    wide = min(v.shape[1], window_size(size) if size % LANES == 0 else 2 * LANES)
    v = v[:, pl.ds(pl.multiple_of(off, LANES), wide)]
    if wide != size:
        v = pltpu.roll(v, jnp.where(inside == 0, 0, wide - inside), 1)
    return v[:, :size]


def final_kernel(planes, places, mine, got, sums, grad_bi, *rest):
    matrices, small_outs, (bi_out, loss, both) = rest[:4], rest[4:12], rest[12:]
    is_low = place_of(places, planes, "core") == 0
    a, b = mine[...].astype(F32), got[...].astype(F32)
    half = a.shape[1]
    both[:, :half] = jnp.where(is_low, a, b)
    both[:, half:] = jnp.where(is_low, b, a)
    small = matrices[0].shape[0]
    for i, out in enumerate(matrices):
        out[...] = both[i * small : (i + 1) * small]
    first = place_of(places, planes, "first_off"), place_of(places, planes, "first_inside")
    hidden = place_of(places, planes, "hidden_off"), place_of(places, planes, "hidden_inside")
    found = take_lanes(sums, *first, small)
    bias = take_lanes(both.at[4 * small : 4 * small + 8], *first, small)
    for i, out in enumerate(small_outs):
        v = found[i : i + 1] if i < 7 else bias[:1]
        out[...] = v.reshape(small)
    size = bi_out.shape[0]
    bi_out[...] = take_lanes(grad_bi, *hidden, size)[:1].reshape(size)
    loss[...] = sums[7:8, :LANES].reshape(LANES)


def finish(places, planes, mine, got, sums, grad_bi, hidden_rows):
    small = (mine.shape[0] - 16) // 4
    width = 2 * mine.shape[1]
    shapes = [jax.ShapeDtypeStruct((small, width), F32)] * 4
    shapes += [jax.ShapeDtypeStruct((small,), F32)] * 8
    shapes += [jax.ShapeDtypeStruct((hidden_rows,), F32), jax.ShapeDtypeStruct((LANES,), F32)]
    got = pl.pallas_call(
        functools.partial(final_kernel, planes),
        in_specs=[smem()] + [vmem()] * 4,
        out_specs=[vmem()] * len(shapes),
        out_shape=shapes,
        scratch_shapes=[pltpu.VMEM((mine.shape[0], width), F32)],
        compiler_params=params(8),
        name="finish",
    )(places, mine, got, sums, grad_bi)
    return got[:4], got[4:12], got[12], got[13][0]


def permute(v, count, move):
    return lax.ppermute(v, AXES, [(i, move(i)) for i in range(count)])


def from_planes(parts, count):
    return [parts[0]] + [
        permute(parts[k], count, lambda i: (i + 8 * k) % count) for k in range(1, len(parts))
    ]


def gather_pair(v, count, bit, mine):
    got = permute(v, count, lambda i: i ^ bit)
    out = jnp.zeros((2,) + v.shape, v.dtype)
    out = lax.dynamic_update_slice_in_dim(out, v[None], mine, 0)
    return lax.dynamic_update_slice_in_dim(out, got[None], 1 - mine, 0)


def after(v, *others):
    return lax.optimization_barrier((v,) + others)[0]


def body(
    query_tokens, passage_tokens, query_length, passage_length, clusters, positives,
    w_query, b_query, w_key, w_value, b_value, w_mix, b_mix, gain_one, shift_one,
    w_inner, b_inner, w_outer, b_outer, gain_two, shift_two,
):
    pairs, query_rows, width = query_tokens.shape
    passage_rows = passage_tokens.shape[1]
    seqs = 2 * pairs
    batch_count = lax.axis_size("batch")
    count = batch_count * lax.axis_size("rep")
    planes = count // 8
    slab = width // planes
    me = lax.axis_index(AXES)
    z, y, x, core = me // 8, me // 4 % 2, me // 2 % 2, me % 2
    mats = whole_mats = (w_query, w_key, w_value, w_mix, w_inner, w_outer)
    vectors = (b_query, b_value, b_mix, gain_one, shift_one, b_outer, gain_two, shift_two, b_inner)
    batch_index = lax.axis_index("batch")
    first_rows, hidden_rows = width // batch_count, w_inner.shape[1] // batch_count

    def window(at, total, size):
        return jnp.minimum(at // LANES * LANES, total - size)

    slot = jnp.arange(2 * planes + len(PLACES), dtype=jnp.int32)
    places = jnp.where(
        slot < planes,
        window((z + slot) % planes * slab, width, 2 * LANES),
        (z - slot) % planes * seqs,
    )
    first_at, hidden_at = batch_index * first_rows, batch_index * hidden_rows
    first_off = window(first_at, width, 2 * LANES)
    hidden_off = window(hidden_at, w_inner.shape[1], window_size(hidden_rows))
    found = dict(
        own=me * seqs, line=me % 8, core=core, y=y, x=x,
        inside=z * slab - window(z * slab, width, 2 * LANES),
        first_off=first_off, first_inside=first_at - first_off,
        hidden_off=hidden_off, hidden_inside=hidden_at - hidden_off, pair=me * pairs,
    )
    for i, name in enumerate(PLACES):
        places = jnp.where(slot == 2 * planes + i, found[name], places)
    places = places.astype(jnp.int32)

    (packet, probs, a, pack, bi), mats, (near_query, near_passage), early = cls_forward(
        places, query_length, passage_length, positives, clusters,
        query_tokens, passage_tokens, mats, vectors, planes,
    )
    done = [None]

    def run(start, size, wait_for=None):
        lengths = passage_length
        if wait_for is not None:
            lengths, wait_for = lax.optimization_barrier((lengths, wait_for))
        done[0] = forward(near_passage, lengths, pack, bi, mats, False, start, size, done[0])
        return wait_for

    def hold(v):
        v, done[0] = lax.optimization_barrier((v, done[0]))
        return v

    def backward(packet_a, packet_b):
        if 2 * packet_a.shape[0] * seqs <= KERNEL_ROWS:
            return cls_backward(
                places, packet_a, packet_b, pack, bi, mats, near_query, near_passage, probs, a, planes, batch_count
            )
        return plain_backward(
            places, packet_a, packet_b, pack, bi, whole_mats, query_tokens, passage_tokens, probs, a, planes, batch_count
        )

    parts = from_planes([packet] * planes, count)
    cuts = [pairs * i // 4 for i in (1, 2, 3)]
    run(0, cuts[0])
    parts[-1] = hold(parts[-1])
    packet = place_planes(places, parts)
    packet = run(cuts[0], cuts[1] - cuts[0], packet)
    early = list(early)
    early[0], packet = lax.optimization_barrier((early[0], packet))
    parts = [packet] + [
        permute(packet, count, lambda i: i ^ (4 * dy + 2 * dx)) for dy, dx in SQUARE[1:]
    ]
    early = from_planes(early, count)
    parts[-1] = hold(parts[-1])
    parts[-1], early[-1] = lax.optimization_barrier((parts[-1], early[-1]))
    packet = place_square(places, planes, parts)
    got = permute(packet, count, lambda i: i ^ 1)
    (
        (grad_w_outer, grad_w_inner, sums, grad_b_inner, line_att, line_mix, dp, ab),
        late,
    ) = backward(packet, got)
    if grad_w_inner.shape[0] != first_rows:
        grad_w_inner = lax.dynamic_slice_in_dim(
            grad_w_inner, first_at - first_off, first_rows, 0
        )

    late = list(late)
    late[0] = run(cuts[1], cuts[2] - cuts[1], late[0])
    late = from_planes(late, count)
    late[-1] = hold(late[-1])
    mine, other = partial_sums(places, line_att, line_mix, early, late, slab)
    got = permute(other, count, lambda i: i ^ 1)
    mine, other = fold(places, planes, mine, got)
    other = run(cuts[2], pairs - cuts[2], other)
    got = hold(permute(other, count, lambda i: i ^ 4))
    passage_out = done[0]
    mine = add_low(mine, got)
    lengths, mine = lax.optimization_barrier((query_length, mine))
    query_out = forward(near_query, lengths, pack, bi, mats, True, 0, pairs)
    got = permute(mine, count, lambda i: i ^ 2)
    got, query_out = lax.optimization_barrier((got, query_out))
    mine = add_low(mine, got)
    ab, mine = lax.optimization_barrier((ab, mine))
    query_grad, passage_grad, query_out, passage_out = token_grads(dp, ab, query_out, passage_out)
    got = permute(mine, count, lambda i: i ^ 1)
    matrices, small, grad_b_inner, loss = finish(
        places, planes, mine, got, sums, grad_b_inner, hidden_rows
    )
    grad_w_query, grad_w_key, grad_w_value, grad_w_mix = matrices
    b_outer, gain_two, shift_two, gain_one, shift_one, b_mix, b_value, b_query = small
    return (
        query_out, passage_out, loss, query_grad, passage_grad,
        grad_w_query, b_query, grad_w_key, grad_w_value, b_value,
        grad_w_mix, b_mix, gain_one, shift_one, grad_w_inner, grad_b_inner,
        grad_w_outer, b_outer, gain_two, shift_two,
    )


def solution(mesh):
    rows = P(AXES, None, None)
    vector, matrix = P("batch"), P("batch", None)
    return jax.shard_map(
        body,
        mesh=mesh,
        in_specs=(rows, rows, P(AXES), P(AXES), P(), P(AXES)) + (P(),) * 15,
        out_specs=(
            rows, rows, P(), rows, rows,
            matrix, vector, matrix, matrix, vector,
            matrix, vector, vector, vector, matrix, vector,
            matrix, vector, vector, vector,
        ),
        check_vma=False,
    )
```

```python
import functools

import jax
import jax.numpy as jnp
from jax import lax
from jax.experimental import pallas as pl
from jax.experimental.pallas import tpu as pltpu
from jax.sharding import PartitionSpec as P

HEADS = 12
HEAD = 64
LANES = 128
AXES = ("batch", "rep")
BF = jnp.bfloat16
F32 = jnp.float32
MIB = 2**20
KERNEL_ROWS = 1024
B_QUERY, B_VALUE, B_MIX, GAIN_ONE, SHIFT_ONE, B_OUTER, GAIN_TWO, SHIFT_TWO = range(8)


def dot(a, b):
    return jnp.dot(a, b, preferred_element_type=F32)


def dot_nt(a, b):
    return lax.dot_general(a, b, (((1,), (1,)), ((), ())), preferred_element_type=F32)


def dot_tn(a, b):
    return lax.dot_general(a, b, (((0,), (0,)), ((), ())), preferred_element_type=F32)


def gelu(z):
    half = 0.5 * z
    return half + half * lax.erf(z * 0.5**0.5)


def gelu_slope(z):
    phi = jnp.exp(-0.5 * z * z) * 0.3989422804014327
    return 0.5 + 0.5 * lax.erf(z * 0.5**0.5) + z * phi


def center_scale(v):
    c = v - jnp.mean(v, axis=-1, keepdims=True)
    r = lax.rsqrt(jnp.mean(c * c, axis=-1, keepdims=True) + 1e-12)
    return c * r, r


def scores_of(qp, ka, own, sel):
    qa = jnp.concatenate([jnp.where(sel, qp, jnp.zeros_like(qp)), own], 1)
    return dot_nt(qa, ka)


def softened(scores):
    return jnp.exp(scores - jnp.max(scores, axis=-1, keepdims=True)).astype(BF)


def values_of(vp, key_low):
    zero, one = jnp.zeros_like(vp), jnp.ones_like(vp)
    top = jnp.concatenate([jnp.where(key_low, vp, zero), jnp.where(key_low, one, zero)], 1)
    low = jnp.concatenate([jnp.where(key_low, zero, vp), jnp.where(key_low, zero, one)], 1)
    return jnp.concatenate([top, low], 0)


def row(pack, index):
    return pack[index : index + 1, :]


def layer_rows(xs, own, biases, pack, bi, wq, wk, wv, wm, wi, wo, split):
    seqs = len(xs)
    rows, width = xs[0].shape
    x = jnp.concatenate(xs, 0)
    keys = biases[0].shape[0]
    wide = 2 * LANES
    groups = width // wide
    scale = HEAD**-0.5
    low = lax.broadcasted_iota(jnp.int32, (rows, LANES), 1) < HEAD
    key_low = lax.broadcasted_iota(jnp.int32, (keys, LANES), 1) < HEAD

    def projected(w, g, index=None, factor=None):
        cols = slice(g * wide, (g + 1) * wide)
        v = dot(x, w[:, cols])
        if index is not None:
            v = v + row(pack, index)[:, cols]
        if factor is not None:
            v = v * factor
        v = v.astype(BF)
        vs = [v[i * rows : (i + 1) * rows] for i in range(seqs)]
        if factor is not None or keys == rows:
            return vs
        return [jnp.concatenate([v, jnp.zeros((keys - rows, wide), BF)], 0) for v in vs]

    def pair_cols(p):
        return slice(p % 2 * LANES, (p % 2 + 1) * LANES)

    made = [(projected(wq, 0, B_QUERY, scale), projected(wk, 0), projected(wv, 0, B_VALUE))]

    def pair_scores(p):
        q, k, _ = made[p // 2]
        cols = pair_cols(p)
        out = []
        for i in range(seqs):
            ka = jnp.concatenate([k[i][:, cols], biases[i]], 1)
            out.append([scores_of(q[i][:, cols], ka, own, sel) for sel in (low, ~low)])
        return out

    ready = pair_scores(0)
    outs = [[] for _ in range(seqs)]
    for p in range(HEADS // 2):
        g = p // 2
        scores = ready
        if p % 2 == 0 and g + 1 < groups:
            part = projected(wq, g + 1, B_QUERY, scale), projected(wk, g + 1)
        if p % 2 == 1 and g + 1 < groups:
            made.append(part + (projected(wv, g + 1, B_VALUE),))
        if p + 1 < HEADS // 2:
            ready = pair_scores(p + 1)
        for i in range(seqs):
            e = jnp.concatenate([softened(v) for v in scores[i]], 1)
            o = dot(e, values_of(made[g][2][i][:, pair_cols(p)], key_low))
            outs[i].append((o[:, :LANES] / o[:, LANES:]).astype(BF))
    mixed = jnp.concatenate([jnp.concatenate(o, 1) for o in outs], 0)
    part = seqs * rows // split
    lows, accs = [], []
    for h in range(split):
        sl = slice(h * part, (h + 1) * part)
        nrm, _ = center_scale(x[sl].astype(F32) + dot(mixed[sl], wm[...]) + row(pack, B_MIX))
        first = nrm * row(pack, GAIN_ONE) + row(pack, SHIFT_ONE)
        lows.append(first.astype(BF))
        accs.append(first + row(pack, B_OUTER))
    hidden = [[] for _ in range(split)]
    for j in range(wi.shape[1] // width):
        cols = slice(j * width, (j + 1) * width)
        for h in range(split):
            v = gelu(dot(lows[h], wi[:, cols]) + bi[:, cols]).astype(BF)
            if split == 1:
                accs[h] = accs[h] + dot(v, wo[cols, :])
            hidden[h].append(v)
    if split > 1:
        accs = [acc + dot(jnp.concatenate(v, 1), wo[...]) for acc, v in zip(accs, hidden)]
    done = []
    for acc in accs:
        nrm, _ = center_scale(acc)
        done.append((nrm * row(pack, GAIN_TWO) + row(pack, SHIFT_TWO)).astype(BF))
    return jnp.concatenate(done, 0)


def forward_kernel(joint, group, start, len_ref, x_ref, pack, bi, wq, wk, wv, wm, wi, wo, *rest):
    out_ref = rest[1]
    seqs, seq_rows, _ = x_ref.shape
    weights = (pack, bi, wq, wk, wv, wm, wi, wo)
    if joint:
        rows = seqs * seq_rows
        x = x_ref[...].reshape(rows, x_ref.shape[2])
        at = lax.broadcasted_iota(jnp.int32, (rows, LANES), 0)
        lane = lax.broadcasted_iota(jnp.int32, (rows, LANES), 1)
        length = jnp.zeros((rows, LANES), jnp.int32)
        for s in range(seqs):
            length = jnp.where(lane == s, len_ref[s], length)
        off = at - lane * seq_rows
        bias = jnp.where((off >= 0) & (off < length), 0.0, -1e30).astype(BF)
        own = jnp.where((off >= 0) & (off < seq_rows), 1.0, 0.0).astype(BF)

        near, _, far, sem = rest
        copy = pltpu.make_async_copy(near, far, sem.at[0])
        copy.start()
        out_ref[...] = layer_rows([x], own, [bias], *weights, 1).reshape(out_ref.shape)
        copy.wait()
        return
    biases = []
    for b in range(group):
        at_seq = start + pl.program_id(0) * group + b
        keys = -(-seq_rows // LANES) * LANES
        at = lax.broadcasted_iota(jnp.int32, (keys, LANES), 0)
        lane = lax.broadcasted_iota(jnp.int32, (keys, LANES), 1)
        biases.append(jnp.where((lane == 0) & (at >= len_ref[at_seq]), -1e30, 0.0).astype(BF))
    own = jnp.where(
        lax.broadcasted_iota(jnp.int32, (seq_rows, LANES), 1) == 0, 1.0, 0.0
    ).astype(BF)
    base = start + pl.program_id(0) * group

    v = layer_rows([x_ref[base + b] for b in range(group)], own, biases, *weights, group)
    for b in range(group):
        out_ref[base + b] = v[b * seq_rows : (b + 1) * seq_rows]


def forward(tokens, lengths, pack, bi, mats, joint, start, count, other):
    _, rows, width = tokens.shape
    total = count * rows
    weight_bytes = sum(m.size * 2 for m in mats)
    group = 2 if count % 2 == 0 else 1
    if other is None:
        other = tokens
    operands = [in_hbm(lengths), tokens, pack, bi, *mats, in_vmem(other)]
    fresh = not joint and other is tokens
    outs = [pltpu.VMEM(tokens.shape, BF)]
    if joint:
        outs.append(pltpu.HBM(other.shape, BF))
    got = pl.pallas_call(
        functools.partial(forward_kernel, joint, group, start),
        grid=(1 if joint else count // group,),
        in_specs=[smem()] + [vmem()] * 9 + [anywhere()],
        out_specs=[vmem()] + [anywhere()] * (len(outs) - 1),
        out_shape=outs,
        scratch_shapes=[pltpu.SemaphoreType.DMA((1,))] if joint else [],
        input_output_aliases={} if joint or fresh else {len(operands) - 1: 0},
        compiler_params=params(16),
        cost_estimate=pl.CostEstimate(
            flops=int(total * weight_bytes * 1.9),
            bytes_accessed=weight_bytes + total * width * 4,
            transcendentals=total * 4096,
        ),
        name="forward_rows",
    )(*operands)
    return got if joint else got[0]


def head_of_lane(shape):
    return lax.broadcasted_iota(jnp.int32, shape, 1) // HEAD


def expand_heads(v):
    head = head_of_lane(v.shape)
    zero = jnp.zeros_like(v)
    return jnp.concatenate([jnp.where(head == h, v, zero) for h in range(HEADS)], 0)


def collapse_heads(v):
    seqs = v.shape[0] // HEADS
    out = jnp.zeros((seqs, v.shape[1]), v.dtype)
    head = head_of_lane(out.shape)
    for h in range(HEADS):
        out = jnp.where(head == h, v[h * seqs : (h + 1) * seqs], out)
    return out


SQUARE = ((0, 0), (0, 1), (1, 0), (1, 1))
PLACES = ("own", "line", "core", "y", "x", "inside", "first_off", "first_inside", "hidden_off", "hidden_inside", "pair")


def place_of(places, planes, name):
    return places[2 * planes + PLACES.index(name)]


def window_size(size):
    return size if size % LANES == 0 else 2 * LANES


def split3(v):
    hi = v.astype(BF)
    mid = (v - hi.astype(F32)).astype(BF)
    lo = (v - hi.astype(F32) - mid.astype(F32)).astype(BF)
    return hi, mid, lo


def load(pairs, sems):
    copies = [pltpu.make_async_copy(a, b, sems.at[i]) for i, (a, b) in enumerate(pairs)]
    for c in copies:
        c.start()
    return copies


def cls_kernel(places, query_len, passage_len, target, clusters, qt_h, pt_h, wq_h, wk_h, wv_h, wm_h, wi_h, wo_h, *rest):
    planes = len(rest) - 34
    vectors_h, (packet, probs_out, a_out, pack, bi), rest = rest[:9], rest[9:14], rest[14:]
    wq, wk, wv, wm, wi, wo, qt, pt = rest[:8]
    early = rest[8 : 8 + planes]
    px_s, pair_s, *vectors, sems = rest[8 + planes :]
    copies = load(
        (*zip(vectors_h, vectors), (qt_h, qt), (pt_h, pt), (wq_h, wq), (wk_h, wk), (wv_h, wv), (wm_h, wm), (wi_h, wi), (wo_h, wo)),
        sems,
    )
    small, (q_copy, p_copy), copies = copies[:9], copies[9:11], copies[11:]
    for c in small:
        c.wait()
    for i, v in enumerate(vectors[:8]):
        pack[i : i + 1, :] = v[...].astype(F32).reshape(1, -1)
    bi[...] = vectors[8][...].astype(F32).reshape(1, -1)
    pairs, query_rows, width = qt.shape
    passage_rows = pt.shape[1]
    seqs = 2 * pairs
    at = lax.broadcasted_iota(jnp.int32, (seqs, width), 0)
    start = jnp.zeros((seqs, width), F32)
    q_copy.wait()
    p_copy.wait()
    for s in range(seqs):
        src = qt[s, 0:16, :] if s < pairs else pt[s - pairs, 0:16, :]
        start = jnp.where(at == s, src.astype(F32)[0:1, :], start)
    low_start = start.astype(BF)
    copies[0].wait()
    q0 = (dot(low_start, wq[...]) + row(pack, B_QUERY)).astype(BF)
    copies[1].wait()
    a = (dot_nt(expand_heads(q0), wk[...]) * HEAD**-0.5).astype(BF)
    a_out[...] = a
    xq = qt[...].reshape(pairs * query_rows, width)
    xp = pt[...].reshape(pairs * passage_rows, width)
    scores = jnp.concatenate([dot_nt(a, xq), dot_nt(a, xp)], 1)
    s_row = lax.broadcasted_iota(jnp.int32, (HEADS * seqs, 1), 0) % seqs
    lo = jnp.zeros((HEADS * seqs, 1), jnp.int32)
    hi = jnp.zeros((HEADS * seqs, 1), jnp.int32)
    for s in range(seqs):
        if s < pairs:
            first_at, length = s * query_rows, query_len[s]
        else:
            first_at = pairs * query_rows + (s - pairs) * passage_rows
            length = passage_len[s - pairs]
        lo = jnp.where(s_row == s, first_at, lo)
        hi = jnp.where(s_row == s, first_at + length, hi)
    column = lax.broadcasted_iota(jnp.int32, scores.shape, 1)
    scores = jnp.where((column >= lo) & (column < hi), scores, -1e30)
    e = jnp.exp(scores - jnp.max(scores, axis=-1, keepdims=True))
    probs = e / jnp.sum(e, axis=-1, keepdims=True)
    probs_out[...] = probs
    probs = probs.astype(BF)
    cut = pairs * query_rows
    px = (dot(probs[:, :cut], xq) + dot(probs[:, cut:], xp)).astype(BF)
    px_s[...] = px
    copies[2].wait()
    mixed = (collapse_heads(dot(px, wv[...])) + row(pack, B_VALUE)).astype(BF)
    pair_s[0:seqs, :] = low_start
    pair_s[seqs : 2 * seqs, :] = mixed
    heads_rows = HEADS * seqs
    for k, out in enumerate(early):
        window = pl.ds(pl.multiple_of(places[k], LANES), 2 * LANES)
        out[0:heads_rows, :] = px_s[:, window]
        out[heads_rows : heads_rows + 2 * seqs, :] = pair_s[:, window]
        for j in range(width // (2 * LANES)):
            base = heads_rows + (2 + j) * seqs
            out[base : base + seqs, :] = q0[:, j * 2 * LANES : (j + 1) * 2 * LANES]
    copies[3].wait()
    nrm, r_one = center_scale(start + dot(mixed, wm[...]) + row(pack, B_MIX))
    first = nrm * row(pack, GAIN_ONE) + row(pack, SHIFT_ONE)
    low = first.astype(BF)
    acc = first + row(pack, B_OUTER)
    copies[4].wait()
    hidden = gelu(dot(low, wi[...]) + bi[...]).astype(BF)
    copies[5].wait()
    acc = acc + dot(hidden, wo[...])
    nrm, r_two = center_scale(acc)
    packet[:, :width] = (nrm * row(pack, GAIN_TWO) + row(pack, SHIFT_TWO)).astype(BF)
    packet[:, width : 2 * width] = low
    lane = lax.broadcasted_iota(jnp.int32, (seqs, LANES), 1)
    at = lax.broadcasted_iota(jnp.int32, (seqs, LANES), 0)
    wanted = jnp.zeros((seqs, LANES), jnp.int32)
    cluster = jnp.zeros((seqs, LANES), jnp.int32)
    base = place_of(places, planes, "pair")
    for s in range(seqs):
        cluster = jnp.where(at == s, clusters[base + s % pairs], cluster)
        if s < pairs:
            wanted = jnp.where(at == s, target[s], wanted)
    extra = jnp.zeros((seqs, LANES), jnp.int32)
    for j, v in enumerate((wanted // LANES, wanted % LANES, cluster // LANES, cluster % LANES)):
        extra = jnp.where(lane == 6 + j, v, extra)
    extra = extra.astype(F32)
    for j, part in enumerate(split3(r_one) + split3(r_two)):
        extra = jnp.where(lane == j, part.astype(F32), extra)
    packet[:, 2 * width :] = extra.astype(BF)


def vmem():
    return pl.BlockSpec(memory_space=pltpu.VMEM)


def smem():
    return pl.BlockSpec(memory_space=pltpu.SMEM)


def anywhere():
    return pl.BlockSpec(memory_space=pl.ANY)


def params(mib):
    return pltpu.CompilerParams(vmem_limit_bytes=mib * MIB)


def in_hbm(v):
    return pltpu.with_memory_space_constraint(v, pltpu.HBM)


def in_vmem(v):
    return pltpu.with_memory_space_constraint(v, pltpu.VMEM)


def cls_forward(places, query_length, passage_length, positives, clusters, query_tokens, passage_tokens, mats, vectors, planes):
    pairs, query_rows, width = query_tokens.shape
    seqs = 2 * pairs
    tokens = pairs * (query_rows + passage_tokens.shape[1])
    early_rows = seqs * (HEADS + 2 + width // (2 * LANES))
    outs = [
        jax.ShapeDtypeStruct((seqs, 2 * width + LANES), BF),
        pltpu.VMEM((HEADS * seqs, tokens), F32),
        pltpu.VMEM((HEADS * seqs, width), BF),
        jax.ShapeDtypeStruct((8, width), F32),
        jax.ShapeDtypeStruct((1, mats[4].shape[1]), F32),
    ]
    outs += [pltpu.VMEM(v.shape, v.dtype) for v in (*mats, query_tokens, passage_tokens)]
    outs += [jax.ShapeDtypeStruct((early_rows, 2 * LANES), BF)] * planes
    got = pl.pallas_call(
        cls_kernel,
        in_specs=[smem()] * 5 + [anywhere()] * 17,
        out_specs=[vmem()] * len(outs),
        out_shape=outs,
        scratch_shapes=[
            pltpu.VMEM((HEADS * seqs, width), BF),
            pltpu.VMEM((2 * seqs, width), BF),
            *[pltpu.VMEM(v.shape, v.dtype) for v in vectors],
            pltpu.SemaphoreType.DMA((17,)),
        ],
        compiler_params=params(16),
        cost_estimate=pl.CostEstimate(flops=8 * 10**9, bytes_accessed=20 * 10**6, transcendentals=0),
        name="cls_forward",
    )(
        places, *[in_hbm(v) for v in (query_length, passage_length, positives, clusters)],
        in_hbm(query_tokens), in_hbm(passage_tokens), *[in_hbm(m) for m in mats], *[in_hbm(v) for v in vectors],
    )
    kept = [in_vmem(v) for v in got[5:13]]
    return got[:5], kept[:6], kept[6:], got[13:]


def place_planes_kernel(places, *refs):
    *parts, out = refs
    for k, part in enumerate(parts):
        at = places[len(parts) + k]
        out[pl.ds(at // part.shape[0], 1)] = part[...][None]


def place_planes(places, parts):
    shape = (len(parts),) + parts[0].shape
    return pl.pallas_call(
        place_planes_kernel,
        in_specs=[smem()] + [vmem()] * len(parts),
        out_specs=vmem(),
        out_shape=jax.ShapeDtypeStruct(shape, BF),
        compiler_params=params(8),
        name="place_planes",
    )(places, *parts)


def place_square_kernel(planes, places, *refs):
    *parts, out = refs
    y, x = place_of(places, planes, "y"), place_of(places, planes, "x")
    for (dy, dx), part in zip(SQUARE, parts):
        at_y, at_x = (1 - y if dy else y), (1 - x if dx else x)
        out[:, pl.ds(at_y * 2 + at_x, 1)] = part[...][:, None]


def place_square(places, planes, parts):
    v = parts[0]
    out = pl.pallas_call(
        functools.partial(place_square_kernel, planes),
        in_specs=[smem()] + [vmem()] * 4,
        out_specs=vmem(),
        out_shape=jax.ShapeDtypeStruct((planes, 4) + v.shape[1:], BF),
        compiler_params=params(8),
        name="place_square",
    )(places, *parts)
    return out.reshape((-1,) + v.shape[1:])


def norm_back(grad, nrm, r, gain):
    g = grad * gain
    return r * (
        g - jnp.mean(g, axis=-1, keepdims=True) - nrm * jnp.mean(g * nrm, axis=-1, keepdims=True)
    )


def back_kernel(
    planes, slice_first, places, packet_a, packet_b, pack, bi, wq, wk, wv, wm, wi, wo,
    qt, pt, probs_ref, a_ref, *rest,
):
    grad_wo_h, grad_wi_h, vectors, grad_bi, line_att, line_mix, dp_out, ab_out = rest[:8]
    late = rest[8 : 8 + planes]
    grad_wo, grad_wi, packet_s, mix_s, line_s, start_s, own_s, xs_s, win_s, sems = rest[8 + planes :]
    sent = []

    def send(a, b):
        copy = pltpu.make_async_copy(a, b, sems.at[len(sent)])
        copy.start()
        sent.append(copy)

    core = place_of(places, planes, "core")
    packet_s[:, pl.ds(core, 1)] = packet_a[...][:, None]
    packet_s[:, pl.ds(1 - core, 1)] = packet_b[...][:, None]
    pairs, query_rows, width = qt.shape
    passage_rows = pt.shape[1]
    seqs = 2 * pairs
    packet = packet_s[...].reshape(-1, packet_s.shape[-1])
    rows = packet.shape[0]
    scale = 2.0 * width**-0.5

    cls = packet[:, :width]
    tail = packet[:, 2 * width :].astype(F32)
    scores = dot_nt(cls, cls) * scale
    is_query = lax.broadcasted_iota(jnp.int32, (rows, 1), 0) % seqs < pairs
    is_passage = lax.broadcasted_iota(jnp.int32, (1, rows), 1) % seqs >= pairs
    wanted = (tail[:, 6:7] * LANES + tail[:, 7:8]).astype(jnp.int32)
    column = lax.broadcasted_iota(jnp.int32, (1, rows), 1)
    chosen = (column // seqs * pairs + column % pairs == wanted) & is_passage
    across = tail.T
    cluster_row = across[8:9, :] * LANES + across[9:10, :]
    cluster_col = tail[:, 8:9] * LANES + tail[:, 9:10]
    counted = ((cluster_row != cluster_col) | chosen) & is_passage
    masked = jnp.where(counted, scores, -1e30)
    peak = jnp.max(masked, axis=1, keepdims=True)
    log_total = peak + jnp.log(jnp.sum(jnp.exp(masked - peak), axis=1, keepdims=True))
    one = jnp.where(chosen, 1.0, 0.0)
    picked = jnp.sum(one * scores, axis=1, keepdims=True)
    loss = jnp.sum(jnp.where(is_query, log_total - picked, 0.0), axis=0, keepdims=True)
    d_pair = jnp.where(is_query, jnp.exp(masked - log_total) - one, 0.0).astype(BF)
    d_cls = (dot(d_pair, cls) + dot_tn(d_pair, cls)) * scale

    first = packet[:, width : 2 * width]
    nrm_two = (cls.astype(F32) - row(pack, SHIFT_TWO)) / row(pack, GAIN_TWO)
    r_two = tail[:, 3:4] + tail[:, 4:5] + tail[:, 5:6]
    d_second = norm_back(d_cls, nrm_two, r_two, row(pack, GAIN_TWO))
    d_outer = d_second.astype(BF)
    vectors[0:1, :] = jnp.sum(d_outer.astype(F32), axis=0, keepdims=True)
    vectors[1:2, :] = jnp.sum(d_cls * nrm_two, axis=0, keepdims=True)
    vectors[2:3, :] = jnp.sum(d_cls, axis=0, keepdims=True)
    piece = grad_wi.shape[0]
    first_window = pl.ds(
        pl.multiple_of(place_of(places, planes, "first_off"), LANES), 2 * LANES
    )
    mix_s[...] = first
    first_piece = mix_s[:, first_window]
    inside = pl.ds(pl.multiple_of(place_of(places, planes, "first_inside"), 8), piece)
    line = pl.ds(place_of(places, planes, "line"), 1)
    line_rows = planes * seqs
    by_line = (planes, rows // line_rows, seqs, width)
    start_s[...] = d_second.reshape(by_line)
    d_first = start_s[:, line].reshape(line_rows, width)
    for j in range(wi.shape[1] // width):
        cols = slice(j * width, (j + 1) * width)
        inner = dot(first, wi[:, cols]) + bi[:, cols]
        d_inner = (dot_nt(d_outer, wo[cols, :]) * gelu_slope(inner)).astype(BF)
        line_s[...] = d_inner.reshape(by_line)
        d_first = d_first + dot_nt(line_s[:, line].reshape(line_rows, width), wi[:, cols])
        found = dot_tn(first_piece, d_inner)
        if slice_first:
            win_s[: 2 * LANES, :] = found
            found = win_s[inside, :]
        grad_wi[:, cols] = found
        send(grad_wi.at[:, cols], grad_wi_h.at[:, cols])
        grad_bi[:, cols] = jnp.sum(d_inner.astype(F32), axis=0, keepdims=True)
    size = grad_wo.shape[0]
    off = pl.multiple_of(place_of(places, planes, "hidden_off"), LANES)
    window = pl.ds(off, window_size(size))
    hidden = gelu(dot(first, wi[:, window]) + bi[:, window]).astype(BF)
    found = dot_tn(hidden, d_outer)
    if size != window_size(size):
        win_s[: window_size(size), :] = found
        found = win_s[pl.ds(pl.multiple_of(place_of(places, planes, "hidden_inside"), 8), size), :]
    grad_wo[...] = found
    send(grad_wo, grad_wo_h)
    at_line = place_of(places, planes, "line")
    lined = jnp.concatenate(
        [
            packet_s[pl.ds(p * 4 + at_line // 2, 1), pl.ds(at_line % 2, 1)].reshape(seqs, -1)
            for p in range(planes)
        ],
        0,
    )
    nrm_one = (lined[:, width : 2 * width].astype(F32) - row(pack, SHIFT_ONE)) / row(pack, GAIN_ONE)
    tail = lined[:, 2 * width :].astype(F32)
    r_one = tail[:, 0:1] + tail[:, 1:2] + tail[:, 2:3]
    d_start = norm_back(d_first, nrm_one, r_one, row(pack, GAIN_ONE))
    vectors[3:4, :] = jnp.sum(d_first * nrm_one, axis=0, keepdims=True)
    vectors[4:5, :] = jnp.sum(d_first, axis=0, keepdims=True)
    d_attended = d_start.astype(BF)
    vectors[5:6, :] = jnp.sum(d_attended.astype(F32), axis=0, keepdims=True)
    d_mixed = dot_nt(d_attended, wm[...]).astype(BF)
    vectors[6:7, :] = jnp.sum(d_mixed.astype(F32), axis=0, keepdims=True)
    vectors[7:8, :] = jnp.broadcast_to(loss * (2.0 / rows), (1, width))
    line_att[...] = d_attended
    line_mix[...] = d_mixed

    own = pl.ds(pl.multiple_of(places[planes], seqs), seqs)
    own_s[...] = d_start
    own_start = own_s[own, :]
    own_mixed = line_mix[own, :]
    bm = dot_nt(expand_heads(own_mixed), wv[...]).astype(BF)
    xq = qt[...].reshape(pairs * query_rows, width)
    xp = pt[...].reshape(pairs * passage_rows, width)
    d_probs = jnp.concatenate([dot_nt(bm, xq), dot_nt(bm, xp)], 1)
    probs = probs_ref[...]
    d_scores = (probs * (d_probs - jnp.sum(probs * d_probs, axis=-1, keepdims=True))).astype(BF)
    cut = pairs * query_rows
    xs = (dot(d_scores[:, :cut], xq) + dot(d_scores[:, cut:], xp)).astype(BF)
    xs_s[...] = xs
    d_query = (collapse_heads(dot(xs, wk[...])) * HEAD**-0.5).astype(BF)
    heads_rows = HEADS * seqs
    for k, out in enumerate(late):
        window = pl.ds(pl.multiple_of(places[k], LANES), 2 * LANES)
        out[0:heads_rows, :] = xs_s[:, window]
        for j in range(width // (2 * LANES)):
            base = heads_rows + j * seqs
            out[base : base + seqs, :] = d_query[:, j * 2 * LANES : (j + 1) * 2 * LANES]
    dp_out[0:heads_rows, :] = d_scores
    dp_out[heads_rows : 2 * heads_rows, :] = probs.astype(BF)
    shape = (seqs, dp_out.shape[1])
    seq = lax.broadcasted_iota(jnp.int32, shape, 0)
    first_row = jnp.where(seq < pairs, seq * query_rows, cut + (seq - pairs) * passage_rows)
    first_row = jnp.where(lax.broadcasted_iota(jnp.int32, shape, 1) == first_row, 1.0, 0.0).astype(BF)
    ab_out[0:heads_rows, :] = a_ref[...]
    ab_out[heads_rows : 2 * heads_rows, :] = bm
    at_start = dot_nt(d_query, wq[...]) + own_start
    for j, part in enumerate(split3(at_start)):
        rows_of = slice(2 * heads_rows + j * seqs, 2 * heads_rows + (j + 1) * seqs)
        ab_out[rows_of, :] = part
        dp_out[rows_of, :] = first_row
    for copy in sent:
        copy.wait()


def cls_backward(places, packet_a, packet_b, pack, bi, mats, query_tokens, passage_tokens, probs, a, planes, batch_count):
    pairs, _, width = query_tokens.shape
    seqs = 2 * pairs
    blocks = packet_a.shape[0]
    rows = 2 * blocks * seqs
    late_rows = seqs * (HEADS + width // (2 * LANES))
    factors = (2 * HEADS + 3) * seqs
    hidden = mats[4].shape[1]
    first_rows, hidden_rows = width // batch_count, hidden // batch_count
    slice_first = first_rows % 8 == 0

    def out(shape, kind):
        return jax.ShapeDtypeStruct(shape, kind)

    outs = [
        pltpu.HBM((hidden_rows, width), F32),
        pltpu.HBM((first_rows if slice_first else 2 * LANES, hidden), F32),
        out((8, width), F32),
        out((1, hidden), F32),
        out((planes * seqs, width), BF),
        out((planes * seqs, width), BF),
        pltpu.VMEM((factors, probs.shape[1]), BF),
        pltpu.VMEM((factors, width), BF),
    ] + [out((late_rows, 2 * LANES), BF)] * planes
    got = pl.pallas_call(
        functools.partial(back_kernel, planes, slice_first),
        in_specs=[smem()] + [vmem()] * 14,
        out_specs=[anywhere()] * 2 + [vmem()] * (len(outs) - 2),
        out_shape=outs,
        scratch_shapes=[
            pltpu.VMEM(outs[0].shape, F32),
            pltpu.VMEM(outs[1].shape, F32),
            pltpu.VMEM((blocks, 2) + packet_a.shape[1:], BF),
            pltpu.VMEM((rows, width), BF),
            pltpu.VMEM((planes, rows // (planes * seqs), seqs, width), BF),
            pltpu.VMEM((planes, rows // (planes * seqs), seqs, width), F32),
            pltpu.VMEM((planes * seqs, width), F32),
            pltpu.VMEM((HEADS * seqs, width), BF),
            pltpu.VMEM((2 * LANES, width), F32),
            pltpu.SemaphoreType.DMA((hidden // width + 1,)),
        ],
        compiler_params=params(22),
        cost_estimate=pl.CostEstimate(flops=16 * 10**9, bytes_accessed=25 * 10**6, transcendentals=0),
        name="cls_backward",
    )(
        places, packet_a, packet_b, pack, bi, *mats,
        query_tokens, passage_tokens, in_vmem(probs), in_vmem(a),
    )
    return got[:8], got[8:]


def plain_backward(places, packet_a, packet_b, pack, bi, mats, query_tokens, passage_tokens, probs, a, planes, batch_count):
    wq, wk, wv, wm, wi, wo = mats
    pairs, query_rows, width = query_tokens.shape
    seqs = 2 * pairs
    blocks = packet_a.shape[0]
    rows = 2 * blocks * seqs
    cut = pairs * query_rows
    hidden = wi.shape[1]

    def at(name):
        return places[2 * planes + PLACES.index(name)]

    core = at("core")
    packet = jnp.stack(
        [jnp.where(core == 0, packet_a, packet_b), jnp.where(core == 0, packet_b, packet_a)], 1
    )
    packet = packet.reshape(2 * blocks, seqs, -1)
    cls_query = packet[:, :pairs, :width].reshape(-1, width)
    cls_passage = packet[:, pairs:, :width].reshape(-1, width)
    packet = packet.reshape(rows, -1)
    tail = packet[:, 2 * width :].astype(F32)

    def sides(v):
        v = v.reshape(2 * blocks, seqs)
        return v[:, :pairs].reshape(-1), v[:, pairs:].reshape(-1)

    scale = 2.0 * width**-0.5
    scores = dot_nt(cls_query, cls_passage) * scale
    wanted = sides(tail[:, 6] * LANES + tail[:, 7])[0]
    query_cluster, passage_cluster = sides(tail[:, 8] * LANES + tail[:, 9])
    chosen = jnp.arange(scores.shape[1], dtype=F32)[None] == wanted[:, None]
    counted = (query_cluster[:, None] != passage_cluster[None]) | chosen
    masked = jnp.where(counted, scores, -1e30)
    log_total = jax.nn.logsumexp(masked, axis=1, keepdims=True)
    one = chosen.astype(F32)
    loss = jnp.sum(log_total - jnp.sum(one * scores, axis=1, keepdims=True))
    d_pair = (jnp.exp(masked - log_total) - one).astype(BF)
    d_cls = jnp.concatenate(
        [
            dot(d_pair, cls_passage).reshape(2 * blocks, pairs, width),
            dot_tn(d_pair, cls_query).reshape(2 * blocks, pairs, width),
        ],
        1,
    ).reshape(rows, width) * scale
    first = packet[:, width : 2 * width]
    nrm_two = (packet[:, :width].astype(F32) - row(pack, SHIFT_TWO)) / row(pack, GAIN_TWO)
    nrm_one = (first.astype(F32) - row(pack, SHIFT_ONE)) / row(pack, GAIN_ONE)
    d_second = norm_back(
        d_cls, nrm_two, jnp.sum(tail[:, 3:6], 1, keepdims=True), row(pack, GAIN_TWO)
    )
    d_outer = d_second.astype(BF)
    hidden_rows, first_rows = hidden // batch_count, width // batch_count
    hidden_at = at("hidden_off") + at("hidden_inside")
    first_at = at("first_off") + at("first_inside")
    wi_piece = lax.dynamic_slice_in_dim(wi, hidden_at, hidden_rows, 1)
    bi_piece = lax.dynamic_slice_in_dim(bi, hidden_at, hidden_rows, 1)

    def block(parts):
        first, d_outer = parts
        d_inner = (dot_nt(d_outer, wo) * gelu_slope(dot(first, wi) + bi)).astype(BF)
        return d_inner, dot_nt(d_inner, wi), gelu(dot(first, wi_piece) + bi_piece).astype(BF)

    size = rows // 8
    parts = first.reshape(-1, size, width), d_outer.reshape(-1, size, width)
    d_inner, more, hidden_piece = (v.reshape(rows, -1) for v in lax.map(block, parts))
    d_first = d_second + more
    first_piece = lax.dynamic_slice_in_dim(first, first_at, first_rows, 1)
    grad_wo, grad_wi = dot_tn(hidden_piece, d_outer), dot_tn(first_piece, d_inner)
    if first_rows % 8:
        grad_wi = lax.dynamic_update_slice_in_dim(
            jnp.zeros((2 * LANES, hidden), F32), grad_wi, at("first_inside"), 0
        )
    d_start = norm_back(
        d_first, nrm_one, jnp.sum(tail[:, 0:3], 1, keepdims=True), row(pack, GAIN_ONE)
    )
    d_attended = d_start.astype(BF)
    d_mixed = dot_nt(d_attended, wm).astype(BF)
    def line(v):
        v = v.reshape(planes, -1, seqs, width)
        return lax.dynamic_slice_in_dim(v, at("line"), 1, 1).reshape(planes * seqs, width)

    sums = (d_outer, d_cls * nrm_two, d_cls)
    sums += tuple(line(v) for v in (d_first * nrm_one, d_first, d_attended, d_mixed))
    vectors = [jnp.sum(v.astype(F32), 0) for v in sums] + [jnp.full((width,), loss * (2.0 / rows))]

    def own(v):
        return lax.dynamic_slice_in_dim(v, at("own"), seqs, 0)

    bm = dot_nt(expand_heads(own(d_mixed)), wv).astype(BF)
    xq = query_tokens.reshape(-1, width)
    xp = passage_tokens.reshape(-1, width)
    d_probs = jnp.concatenate([dot_nt(bm, xq), dot_nt(bm, xp)], 1)
    d_scores = (probs * (d_probs - jnp.sum(probs * d_probs, axis=-1, keepdims=True))).astype(BF)
    xs = (dot(d_scores[:, :cut], xq) + dot(d_scores[:, cut:], xp)).astype(BF)
    d_query = (collapse_heads(dot(xs, wk)) * HEAD**-0.5).astype(BF)
    blocks_of_query = [
        d_query[:, j : j + 2 * LANES] for j in range(0, width, 2 * LANES)
    ]
    late = [
        jnp.concatenate(
            [lax.dynamic_slice_in_dim(xs, places[k], 2 * LANES, 1)] + blocks_of_query
        )
        for k in range(planes)
    ]
    at_start = [lax.reduce_precision(dot_nt(d_query, wq) + own(d_start), 8, 23)]
    for _ in range(2):
        high = lax.reduce_precision(at_start[-1], 8, 7)
        at_start[-1:] = [high, at_start[-1] - high]
    seq = jnp.arange(seqs)
    first_row = jnp.where(seq < pairs, seq * query_rows, cut + (seq - pairs) * passage_tokens.shape[1])
    first_row = (jnp.arange(probs.shape[1])[None] == first_row[:, None]).astype(BF)
    dp = jnp.concatenate([d_scores, probs.astype(BF)] + [first_row] * 3)
    ab = jnp.concatenate([a, bm] + [v.astype(BF) for v in at_start])
    return (
        grad_wo, grad_wi, jnp.stack(vectors), jnp.sum(d_inner.astype(F32), 0, keepdims=True),
        line(d_attended), line(d_mixed), dp, ab,
    ), late


def tokens_kernel(first, moves, dp, ab, *refs):
    near, (out, *far), (stage, sems) = refs[:moves], refs[moves : 2 * moves + 1], refs[-2:]
    copies = [pltpu.make_async_copy(a, b, sems.at[i]) for i, (a, b) in enumerate(zip(near, far))]
    for c in copies:
        c.start()
    size = stage.shape[1]
    for n in range(stage.shape[0]):
        cols = slice(first + n * size, first + (n + 1) * size)
        stage[n] = dot_tn(dp[:, cols], ab[...])
        copy = pltpu.make_async_copy(
            stage.at[n], out.at[pl.ds(n * size, size)], sems.at[moves + n]
        )
        copy.start()
        copies.append(copy)
    for c in copies:
        c.wait()


def token_grads(dp, ab, first, rows, near):
    width = ab.shape[1]
    chunks = rows // (2 * LANES)
    moves = len(near)
    return pl.pallas_call(
        functools.partial(tokens_kernel, first, moves),
        in_specs=[vmem()] * 2 + [anywhere()] * moves,
        out_specs=[anywhere()] * (1 + moves),
        out_shape=[pltpu.HBM((rows, width), F32)] + [pltpu.HBM(v.shape, BF) for v in near],
        scratch_shapes=[
            pltpu.VMEM((chunks, 2 * LANES, width), F32),
            pltpu.SemaphoreType.DMA((moves + chunks,)),
        ],
        compiler_params=params(16),
        cost_estimate=pl.CostEstimate(
            flops=rows * 800 * width, bytes_accessed=rows * width * 6, transcendentals=0
        ),
        name="token_grads",
    )(in_vmem(dp), in_vmem(ab), *[in_vmem(v) for v in near])


def sums_kernel(places, vectors, line_att, line_mix, *rest):
    planes = (len(rest) - 3) // 2
    early, late = rest[:planes], rest[planes : 2 * planes]
    mine, other, win = rest[2 * planes :]
    width = line_att.shape[1]
    wide = 2 * LANES
    seqs = line_att.shape[0] // planes
    heads_rows = HEADS * seqs

    def unfold(ref, base):
        return jnp.concatenate(
            [ref[base + j * seqs : base + (j + 1) * seqs, :] for j in range(width // wide)], 1
        )

    xs, px, starts, mixed, q0, dq, dm, da = ([] for _ in range(8))
    for k in range(planes):
        e, l = early[k], late[k]
        at = pl.ds(pl.multiple_of(places[planes + k], seqs), seqs)
        px.append(e[0:heads_rows, :])
        starts.append(e[heads_rows : heads_rows + seqs, :])
        mixed.append(e[heads_rows + seqs : heads_rows + 2 * seqs, :])
        q0.append(expand_heads(unfold(e, heads_rows + 2 * seqs)))
        xs.append(l[0:heads_rows, :])
        dq.append(unfold(l, heads_rows))
        dm.append(expand_heads(line_mix[at, :]))
        da.append(line_att[at, :])
    cat = functools.partial(jnp.concatenate, axis=0)
    dq = cat(dq)
    found = (
        dot_tn(cat(starts), dq),
        dot_tn(cat(xs), cat(q0)) * HEAD**-0.5,
        dot_tn(cat(px), cat(dm)),
        dot_tn(cat(mixed), cat(da)),
    )
    bias = [jnp.sum(dq.astype(F32), axis=0, keepdims=True), vectors[3:7, :]]
    bias = jnp.concatenate(bias + [jnp.zeros((11, width), F32)], 0)
    slab = (mine.shape[0] - 16) // 4
    half = width // 2
    inside = pl.ds(pl.multiple_of(place_of(places, planes, "inside"), 8), slab)
    is_low = place_of(places, planes, "core") == 0
    for i in range(5):
        if i < 4:
            win[...] = found[i]
            v = win[inside, :]
        else:
            v = bias
        to = slice(i * slab, i * slab + v.shape[0])
        a, b = v[:, :half], v[:, half:]
        mine[to, :] = jnp.where(is_low, a, b)
        other[to, :] = jnp.where(is_low, b, a).astype(BF)


def partial_sums(places, vectors, line_att, line_mix, early, late, slab):
    width = line_att.shape[1]
    shape = (4 * slab + 16, width // 2)
    return pl.pallas_call(
        sums_kernel,
        in_specs=[smem()] + [vmem()] * (3 + 2 * len(early)),
        out_specs=[vmem()] * 2,
        out_shape=[jax.ShapeDtypeStruct(shape, F32), jax.ShapeDtypeStruct(shape, BF)],
        scratch_shapes=[pltpu.VMEM((2 * LANES, width), F32)],
        compiler_params=params(12),
        cost_estimate=pl.CostEstimate(flops=2 * 10**9, bytes_accessed=4 * 10**6, transcendentals=0),
        name="partial_sums",
    )(places, vectors, line_att, line_mix, *early, *late)


def fold_kernel(planes, places, mine, got, keep, send):
    total = mine[...] + got[...].astype(F32)
    slab = (mine.shape[0] - 16) // 4
    small = slab // 2
    is_low = place_of(places, planes, "y") == 0
    for i in range(5):
        base = i * slab
        if i < 4:
            a, b = total[base : base + small], total[base + small : base + slab]
            v, w = jnp.where(is_low, a, b), jnp.where(is_low, b, a)
        else:
            v = w = total[base : base + 16]
        to = slice(i * small, i * small + v.shape[0])
        keep[to, :] = v
        send[to, :] = w.astype(BF)


def fold(places, planes, mine, got):
    rows = (mine.shape[0] - 16) // 2 + 16
    shape = (rows, mine.shape[1])
    return pl.pallas_call(
        functools.partial(fold_kernel, planes),
        in_specs=[smem()] + [vmem()] * 2,
        out_specs=[vmem()] * 2,
        out_shape=[jax.ShapeDtypeStruct(shape, F32), jax.ShapeDtypeStruct(shape, BF)],
        compiler_params=params(8),
        name="fold",
    )(places, mine, got)


def add_kernel(a, b, out):
    out[...] = (a[...].astype(F32) + b[...].astype(F32)).astype(BF)


def add_low(a, b):
    return pl.pallas_call(
        add_kernel,
        in_specs=[vmem()] * 2,
        out_specs=vmem(),
        out_shape=jax.ShapeDtypeStruct(a.shape, BF),
        compiler_params=params(8),
        name="add_low",
    )(a, b)


def take_lanes(v, off, inside, size):
    wide = min(v.shape[1], window_size(size) if size % LANES == 0 else 2 * LANES)
    v = v[:, pl.ds(pl.multiple_of(off, LANES), wide)]
    if wide != size:
        v = pltpu.roll(v, jnp.where(inside == 0, 0, wide - inside), 1)
    return v[:, :size]


def final_kernel(planes, places, mine, got, sums, grad_bi, *rest):
    matrices, small_outs, (bi_out, loss, both) = rest[:4], rest[4:12], rest[12:]
    is_low = place_of(places, planes, "core") == 0
    a, b = mine[...].astype(F32), got[...].astype(F32)
    half = a.shape[1]
    both[:, :half] = jnp.where(is_low, a, b)
    both[:, half:] = jnp.where(is_low, b, a)
    small = matrices[0].shape[0]
    for i, out in enumerate(matrices):
        out[...] = both[i * small : (i + 1) * small]
    first = place_of(places, planes, "first_off"), place_of(places, planes, "first_inside")
    hidden = place_of(places, planes, "hidden_off"), place_of(places, planes, "hidden_inside")
    found = take_lanes(sums, *first, small)
    bias = take_lanes(both.at[4 * small : 4 * small + 8], *first, small)
    for i, out in enumerate(small_outs):
        at = 0 if i == 7 else i - 2
        v = found[i : i + 1] if i < 3 else bias[at : at + 1]
        out[...] = v.reshape(small)
    size = bi_out.shape[0]
    bi_out[...] = take_lanes(grad_bi, *hidden, size)[:1].reshape(size)
    loss[...] = sums[7:8, :LANES].reshape(LANES)


def finish(places, planes, mine, got, sums, grad_bi, hidden_rows):
    small = (mine.shape[0] - 16) // 4
    width = 2 * mine.shape[1]
    shapes = [jax.ShapeDtypeStruct((small, width), F32)] * 4
    shapes += [jax.ShapeDtypeStruct((small,), F32)] * 8
    shapes += [jax.ShapeDtypeStruct((hidden_rows,), F32), jax.ShapeDtypeStruct((LANES,), F32)]
    got = pl.pallas_call(
        functools.partial(final_kernel, planes),
        in_specs=[smem()] + [vmem()] * 4,
        out_specs=[vmem()] * len(shapes),
        out_shape=shapes,
        scratch_shapes=[pltpu.VMEM((mine.shape[0], width), F32)],
        compiler_params=params(8),
        name="finish",
    )(places, mine, got, sums, grad_bi)
    return got[:4], got[4:12], got[12], got[13][0]


def permute(v, count, move):
    return lax.ppermute(v, AXES, [(i, move(i)) for i in range(count)])


def from_planes(parts, count):
    return [parts[0]] + [
        permute(parts[k], count, lambda i: (i + 8 * k) % count) for k in range(1, len(parts))
    ]


def gather_pair(v, count, bit, mine):
    got = permute(v, count, lambda i: i ^ bit)
    out = jnp.zeros((2,) + v.shape, v.dtype)
    out = lax.dynamic_update_slice_in_dim(out, v[None], mine, 0)
    return lax.dynamic_update_slice_in_dim(out, got[None], 1 - mine, 0)


def after(v, *others):
    return lax.optimization_barrier((v,) + others)[0]


def body(
    query_tokens, passage_tokens, query_length, passage_length, clusters, positives,
    w_query, b_query, w_key, w_value, b_value, w_mix, b_mix, gain_one, shift_one,
    w_inner, b_inner, w_outer, b_outer, gain_two, shift_two,
):
    pairs, query_rows, width = query_tokens.shape
    passage_rows = passage_tokens.shape[1]
    seqs = 2 * pairs
    batch_count = lax.axis_size("batch")
    count = batch_count * lax.axis_size("rep")
    planes = count // 8
    slab = width // planes
    me = lax.axis_index(AXES)
    z, y, x, core = me // 8, me // 4 % 2, me // 2 % 2, me % 2
    mats = whole_mats = (w_query, w_key, w_value, w_mix, w_inner, w_outer)
    vectors = (b_query, b_value, b_mix, gain_one, shift_one, b_outer, gain_two, shift_two, b_inner)
    batch_index = lax.axis_index("batch")
    first_rows, hidden_rows = width // batch_count, w_inner.shape[1] // batch_count

    def window(at, total, size):
        return jnp.minimum(at // LANES * LANES, total - size)

    slot = jnp.arange(2 * planes + len(PLACES), dtype=jnp.int32)
    places = jnp.where(
        slot < planes,
        window((z + slot) % planes * slab, width, 2 * LANES),
        (z - slot) % planes * seqs,
    )
    first_at, hidden_at = batch_index * first_rows, batch_index * hidden_rows
    first_off = window(first_at, width, 2 * LANES)
    hidden_off = window(hidden_at, w_inner.shape[1], window_size(hidden_rows))
    found = dict(
        own=me * seqs, line=me % 8, core=core, y=y, x=x,
        inside=z * slab - window(z * slab, width, 2 * LANES),
        first_off=first_off, first_inside=first_at - first_off,
        hidden_off=hidden_off, hidden_inside=hidden_at - hidden_off, pair=me * pairs,
    )
    for i, name in enumerate(PLACES):
        places = jnp.where(slot == 2 * planes + i, found[name], places)
    places = places.astype(jnp.int32)

    (packet, probs, a, pack, bi), mats, (near_query, near_passage), early = cls_forward(
        places, query_length, passage_length, positives, clusters,
        query_tokens, passage_tokens, mats, vectors, planes,
    )
    done = [None]

    def run(start, size, wait_for=None):
        lengths = passage_length
        if wait_for is not None:
            lengths, wait_for = lax.optimization_barrier((lengths, wait_for))
        done[0] = forward(near_passage, lengths, pack, bi, mats, False, start, size, done[0])
        return wait_for

    def hold(v):
        v, done[0] = lax.optimization_barrier((v, done[0]))
        return v

    def backward(packet_a, packet_b):
        if 2 * packet_a.shape[0] * seqs <= KERNEL_ROWS:
            return cls_backward(
                places, packet_a, packet_b, pack, bi, mats, near_query, near_passage, probs, a, planes, batch_count
            )
        return plain_backward(
            places, packet_a, packet_b, pack, bi, whole_mats, query_tokens, passage_tokens, probs, a, planes, batch_count
        )

    parts = from_planes([packet] * planes, count)
    cuts = [pairs * i // 4 for i in (1, 2, 3)]
    run(0, cuts[0])
    parts[-1] = hold(parts[-1])
    packet = place_planes(places, parts)
    packet = run(cuts[0], cuts[1] - cuts[0], packet)
    early = list(early)
    early[0], packet = lax.optimization_barrier((early[0], packet))
    parts = [packet] + [
        permute(packet, count, lambda i: i ^ (4 * dy + 2 * dx)) for dy, dx in SQUARE[1:]
    ]
    early = from_planes(early, count)
    parts[-1] = hold(parts[-1])
    parts[-1], early[-1] = lax.optimization_barrier((parts[-1], early[-1]))
    packet = place_square(places, planes, parts)
    got = permute(packet, count, lambda i: i ^ 1)
    (
        (grad_w_outer, grad_w_inner, sums, grad_b_inner, line_att, line_mix, dp, ab),
        late,
    ) = backward(packet, got)
    if grad_w_inner.shape[0] != first_rows:
        grad_w_inner = lax.dynamic_slice_in_dim(
            grad_w_inner, first_at - first_off, first_rows, 0
        )

    late = list(late)
    late[0] = run(cuts[1], cuts[2] - cuts[1], late[0])
    late = from_planes(late, count)
    late[-1] = hold(late[-1])
    mine, other = partial_sums(places, sums, line_att, line_mix, early, late, slab)
    got = permute(other, count, lambda i: i ^ 1)
    ab, mine = lax.optimization_barrier((ab, mine))
    (query_grad,) = token_grads(dp, ab, 0, pairs * query_rows, [])
    got, query_grad = lax.optimization_barrier((got, query_grad))
    mine, other = fold(places, planes, mine, got)
    other = run(cuts[2], pairs - cuts[2], other)
    got = hold(permute(other, count, lambda i: i ^ 4))
    passage_out = done[0]
    mine = add_low(mine, got)
    lengths, mine = lax.optimization_barrier((query_length, mine))
    query_out, passage_out = forward(
        near_query, lengths, pack, bi, mats, True, 0, pairs, passage_out
    )
    got = permute(mine, count, lambda i: i ^ 2)
    got, query_out = lax.optimization_barrier((got, query_out))
    mine = add_low(mine, got)
    ab, mine = lax.optimization_barrier((ab, mine))
    passage_grad, query_out = token_grads(
        dp, ab, pairs * query_rows, pairs * passage_rows, [query_out]
    )
    got = permute(mine, count, lambda i: i ^ 1)
    matrices, small, grad_b_inner, loss = finish(
        places, planes, mine, got, sums, grad_b_inner, hidden_rows
    )
    grad_w_query, grad_w_key, grad_w_value, grad_w_mix = matrices
    b_outer, gain_two, shift_two, gain_one, shift_one, b_mix, b_value, b_query = small
    return (
        query_out, passage_out, loss,
        query_grad.reshape(query_tokens.shape), passage_grad.reshape(passage_tokens.shape),
        grad_w_query, b_query, grad_w_key, grad_w_value, b_value,
        grad_w_mix, b_mix, gain_one, shift_one, grad_w_inner, grad_b_inner,
        grad_w_outer, b_outer, gain_two, shift_two,
    )


def solution(mesh):
    rows = P(AXES, None, None)
    vector, matrix = P("batch"), P("batch", None)
    return jax.shard_map(
        body,
        mesh=mesh,
        in_specs=(rows, rows, P(AXES), P(AXES), P(), P(AXES)) + (P(),) * 15,
        out_specs=(
            rows, rows, P(), rows, rows,
            matrix, vector, matrix, matrix, vector,
            matrix, vector, vector, vector, matrix, vector,
            matrix, vector, vector, vector,
        ),
        check_vma=False,
    )
```

```python
import functools

import jax
import jax.numpy as jnp
from jax import lax
from jax.experimental import pallas as pl
from jax.experimental.pallas import tpu as pltpu
from jax.sharding import PartitionSpec as P

HEADS = 12
HEAD = 64
LANES = 128
AXES = ("batch", "rep")
BF = jnp.bfloat16
F32 = jnp.float32
MIB = 2**20
KERNEL_ROWS = 1024
B_QUERY, B_VALUE, B_MIX, GAIN_ONE, SHIFT_ONE, B_OUTER, GAIN_TWO, SHIFT_TWO = range(8)


def dot(a, b):
    return jnp.dot(a, b, preferred_element_type=F32)


def dot_nt(a, b):
    return lax.dot_general(a, b, (((1,), (1,)), ((), ())), preferred_element_type=F32)


def dot_tn(a, b):
    return lax.dot_general(a, b, (((0,), (0,)), ((), ())), preferred_element_type=F32)


def gelu(z):
    half = 0.5 * z
    return half + half * lax.erf(z * 0.5**0.5)


def gelu_slope(z):
    phi = jnp.exp(-0.5 * z * z) * 0.3989422804014327
    return 0.5 + 0.5 * lax.erf(z * 0.5**0.5) + z * phi


def center_scale(v):
    c = v - jnp.mean(v, axis=-1, keepdims=True)
    r = lax.rsqrt(jnp.mean(c * c, axis=-1, keepdims=True) + 1e-12)
    return c * r, r


def scores_of(qp, ka, own, sel):
    qa = jnp.concatenate([jnp.where(sel, qp, jnp.zeros_like(qp)), own], 1)
    return dot_nt(qa, ka)


def softened(scores):
    return jnp.exp(scores - jnp.max(scores, axis=-1, keepdims=True)).astype(BF)


def values_of(vp, key_low):
    zero, one = jnp.zeros_like(vp), jnp.ones_like(vp)
    top = jnp.concatenate([jnp.where(key_low, vp, zero), jnp.where(key_low, one, zero)], 1)
    low = jnp.concatenate([jnp.where(key_low, zero, vp), jnp.where(key_low, zero, one)], 1)
    return jnp.concatenate([top, low], 0)


def row(pack, index):
    return pack[index : index + 1, :]


def layer_rows(xs, own, biases, pack, bi, wq, wk, wv, wm, wi, wo, split):
    seqs = len(xs)
    rows, width = xs[0].shape
    x = jnp.concatenate(xs, 0)
    keys = biases[0].shape[0]
    wide = 2 * LANES
    groups = width // wide
    scale = HEAD**-0.5
    low = lax.broadcasted_iota(jnp.int32, (rows, LANES), 1) < HEAD
    key_low = lax.broadcasted_iota(jnp.int32, (keys, LANES), 1) < HEAD

    def projected(w, g, index=None, factor=None):
        cols = slice(g * wide, (g + 1) * wide)
        v = dot(x, w[:, cols])
        if index is not None:
            v = v + row(pack, index)[:, cols]
        if factor is not None:
            v = v * factor
        v = v.astype(BF)
        vs = [v[i * rows : (i + 1) * rows] for i in range(seqs)]
        if factor is not None or keys == rows:
            return vs
        return [jnp.concatenate([v, jnp.zeros((keys - rows, wide), BF)], 0) for v in vs]

    def pair_cols(p):
        return slice(p % 2 * LANES, (p % 2 + 1) * LANES)

    made = [(projected(wq, 0, B_QUERY, scale), projected(wk, 0), projected(wv, 0, B_VALUE))]

    def pair_scores(p):
        q, k, _ = made[p // 2]
        cols = pair_cols(p)
        out = []
        for i in range(seqs):
            ka = jnp.concatenate([k[i][:, cols], biases[i]], 1)
            out.append([scores_of(q[i][:, cols], ka, own, sel) for sel in (low, ~low)])
        return out

    ready = pair_scores(0)
    outs = [[] for _ in range(seqs)]
    for p in range(HEADS // 2):
        g = p // 2
        scores = ready
        if p % 2 == 0 and g + 1 < groups:
            part = projected(wq, g + 1, B_QUERY, scale), projected(wk, g + 1)
        if p % 2 == 1 and g + 1 < groups:
            made.append(part + (projected(wv, g + 1, B_VALUE),))
        if p + 1 < HEADS // 2:
            ready = pair_scores(p + 1)
        for i in range(seqs):
            e = jnp.concatenate([softened(v) for v in scores[i]], 1)
            o = dot(e, values_of(made[g][2][i][:, pair_cols(p)], key_low))
            outs[i].append((o[:, :LANES] / o[:, LANES:]).astype(BF))
    mixed = jnp.concatenate([jnp.concatenate(o, 1) for o in outs], 0)
    part = seqs * rows // split
    lows, accs = [], []
    for h in range(split):
        sl = slice(h * part, (h + 1) * part)
        nrm, _ = center_scale(x[sl].astype(F32) + dot(mixed[sl], wm[...]) + row(pack, B_MIX))
        first = nrm * row(pack, GAIN_ONE) + row(pack, SHIFT_ONE)
        lows.append(first.astype(BF))
        accs.append(first + row(pack, B_OUTER))
    hidden = [[] for _ in range(split)]
    for j in range(wi.shape[1] // width):
        cols = slice(j * width, (j + 1) * width)
        for h in range(split):
            v = gelu(dot(lows[h], wi[:, cols]) + bi[:, cols]).astype(BF)
            if split == 1:
                accs[h] = accs[h] + dot(v, wo[cols, :])
            hidden[h].append(v)
    if split > 1:
        accs = [acc + dot(jnp.concatenate(v, 1), wo[...]) for acc, v in zip(accs, hidden)]
    done = []
    for acc in accs:
        nrm, _ = center_scale(acc)
        done.append((nrm * row(pack, GAIN_TWO) + row(pack, SHIFT_TWO)).astype(BF))
    return jnp.concatenate(done, 0)


def forward_kernel(joint, group, start, len_ref, x_ref, pack, bi, wq, wk, wv, wm, wi, wo, *rest):
    out_ref = rest[1]
    seqs, seq_rows, _ = x_ref.shape
    weights = (pack, bi, wq, wk, wv, wm, wi, wo)
    if joint:
        part = seqs // 2
        rows = part * seq_rows
        x = x_ref[...].reshape(2, rows, x_ref.shape[2])
        at = lax.broadcasted_iota(jnp.int32, (rows, LANES), 0)
        lane = lax.broadcasted_iota(jnp.int32, (rows, LANES), 1)
        off = at - lane * seq_rows
        own = jnp.where((off >= 0) & (off < seq_rows), 1.0, 0.0).astype(BF)
        biases = []
        for b in range(2):
            length = jnp.zeros((rows, LANES), jnp.int32)
            for s in range(part):
                length = jnp.where(lane == s, len_ref[b * part + s], length)
            biases.append(jnp.where((off >= 0) & (off < length), 0.0, -1e30).astype(BF))
        near, _, far, sem = rest
        copy = pltpu.make_async_copy(near, far, sem.at[0])
        copy.start()
        out_ref[...] = layer_rows([x[0], x[1]], own, biases, *weights, 1).reshape(out_ref.shape)
        copy.wait()
        return
    biases = []
    for b in range(group):
        at_seq = start + pl.program_id(0) * group + b
        keys = -(-seq_rows // LANES) * LANES
        at = lax.broadcasted_iota(jnp.int32, (keys, LANES), 0)
        lane = lax.broadcasted_iota(jnp.int32, (keys, LANES), 1)
        biases.append(jnp.where((lane == 0) & (at >= len_ref[at_seq]), -1e30, 0.0).astype(BF))
    own = jnp.where(
        lax.broadcasted_iota(jnp.int32, (seq_rows, LANES), 1) == 0, 1.0, 0.0
    ).astype(BF)
    base = start + pl.program_id(0) * group

    v = layer_rows([x_ref[base + b] for b in range(group)], own, biases, *weights, group)
    for b in range(group):
        out_ref[base + b] = v[b * seq_rows : (b + 1) * seq_rows]


def forward(tokens, lengths, pack, bi, mats, joint, start, count, other):
    _, rows, width = tokens.shape
    total = count * rows
    weight_bytes = sum(m.size * 2 for m in mats)
    group = 2 if count % 2 == 0 else 1
    if other is None:
        other = tokens
    operands = [in_hbm(lengths), tokens, pack, bi, *mats, in_vmem(other)]
    fresh = not joint and other is tokens
    outs = [pltpu.VMEM(tokens.shape, BF)]
    if joint:
        outs.append(pltpu.HBM(other.shape, BF))
    got = pl.pallas_call(
        functools.partial(forward_kernel, joint, group, start),
        grid=(1 if joint else count // group,),
        in_specs=[smem()] + [vmem()] * 9 + [anywhere()],
        out_specs=[vmem()] + [anywhere()] * (len(outs) - 1),
        out_shape=outs,
        scratch_shapes=[pltpu.SemaphoreType.DMA((1,))] if joint else [],
        input_output_aliases={} if joint or fresh else {len(operands) - 1: 0},
        compiler_params=params(16),
        cost_estimate=pl.CostEstimate(
            flops=int(total * weight_bytes * 1.9),
            bytes_accessed=weight_bytes + total * width * 4,
            transcendentals=total * 4096,
        ),
        name="forward_rows",
    )(*operands)
    return got if joint else got[0]


def head_of_lane(shape):
    return lax.broadcasted_iota(jnp.int32, shape, 1) // HEAD


def expand_heads(v):
    head = head_of_lane(v.shape)
    zero = jnp.zeros_like(v)
    return jnp.concatenate([jnp.where(head == h, v, zero) for h in range(HEADS)], 0)


def collapse_heads(v):
    seqs = v.shape[0] // HEADS
    out = jnp.zeros((seqs, v.shape[1]), v.dtype)
    head = head_of_lane(out.shape)
    for h in range(HEADS):
        out = jnp.where(head == h, v[h * seqs : (h + 1) * seqs], out)
    return out


SQUARE = ((0, 0), (0, 1), (1, 0), (1, 1))
PLACES = ("own", "line", "core", "y", "x", "inside", "first_off", "first_inside", "hidden_off", "hidden_inside", "pair")


def place_of(places, planes, name):
    return places[2 * planes + PLACES.index(name)]


def window_size(size):
    return size if size % LANES == 0 else 2 * LANES


def split3(v):
    hi = v.astype(BF)
    mid = (v - hi.astype(F32)).astype(BF)
    lo = (v - hi.astype(F32) - mid.astype(F32)).astype(BF)
    return hi, mid, lo


def load(pairs, sems):
    copies = [pltpu.make_async_copy(a, b, sems.at[i]) for i, (a, b) in enumerate(pairs)]
    for c in copies:
        c.start()
    return copies


def cls_kernel(places, query_len, passage_len, target, clusters, qt_h, pt_h, wq_h, wk_h, wv_h, wm_h, wi_h, wo_h, *rest):
    planes = len(rest) - 34
    vectors_h, (packet, probs_out, a_out, pack, bi), rest = rest[:9], rest[9:14], rest[14:]
    wq, wk, wv, wm, wi, wo, qt, pt = rest[:8]
    early = rest[8 : 8 + planes]
    px_s, pair_s, *vectors, sems = rest[8 + planes :]
    copies = load(
        (*zip(vectors_h, vectors), (qt_h, qt), (pt_h, pt), (wq_h, wq), (wk_h, wk), (wv_h, wv), (wm_h, wm), (wi_h, wi), (wo_h, wo)),
        sems,
    )
    small, (q_copy, p_copy), copies = copies[:9], copies[9:11], copies[11:]
    for c in small:
        c.wait()
    for i, v in enumerate(vectors[:8]):
        pack[i : i + 1, :] = v[...].astype(F32).reshape(1, -1)
    bi[...] = vectors[8][...].astype(F32).reshape(1, -1)
    pairs, query_rows, width = qt.shape
    passage_rows = pt.shape[1]
    seqs = 2 * pairs
    at = lax.broadcasted_iota(jnp.int32, (seqs, width), 0)
    start = jnp.zeros((seqs, width), F32)
    q_copy.wait()
    p_copy.wait()
    for s in range(seqs):
        src = qt[s, 0:16, :] if s < pairs else pt[s - pairs, 0:16, :]
        start = jnp.where(at == s, src.astype(F32)[0:1, :], start)
    low_start = start.astype(BF)
    copies[0].wait()
    q0 = (dot(low_start, wq[...]) + row(pack, B_QUERY)).astype(BF)
    copies[1].wait()
    a = (dot_nt(expand_heads(q0), wk[...]) * HEAD**-0.5).astype(BF)
    a_out[...] = a
    xq = qt[...].reshape(pairs * query_rows, width)
    xp = pt[...].reshape(pairs * passage_rows, width)
    scores = jnp.concatenate([dot_nt(a, xq), dot_nt(a, xp)], 1)
    s_row = lax.broadcasted_iota(jnp.int32, (HEADS * seqs, 1), 0) % seqs
    lo = jnp.zeros((HEADS * seqs, 1), jnp.int32)
    hi = jnp.zeros((HEADS * seqs, 1), jnp.int32)
    for s in range(seqs):
        if s < pairs:
            first_at, length = s * query_rows, query_len[s]
        else:
            first_at = pairs * query_rows + (s - pairs) * passage_rows
            length = passage_len[s - pairs]
        lo = jnp.where(s_row == s, first_at, lo)
        hi = jnp.where(s_row == s, first_at + length, hi)
    column = lax.broadcasted_iota(jnp.int32, scores.shape, 1)
    scores = jnp.where((column >= lo) & (column < hi), scores, -1e30)
    e = jnp.exp(scores - jnp.max(scores, axis=-1, keepdims=True))
    probs = e / jnp.sum(e, axis=-1, keepdims=True)
    probs_out[...] = probs
    probs = probs.astype(BF)
    cut = pairs * query_rows
    px = (dot(probs[:, :cut], xq) + dot(probs[:, cut:], xp)).astype(BF)
    px_s[...] = px
    copies[2].wait()
    mixed = (collapse_heads(dot(px, wv[...])) + row(pack, B_VALUE)).astype(BF)
    pair_s[0:seqs, :] = low_start
    pair_s[seqs : 2 * seqs, :] = mixed
    heads_rows = HEADS * seqs
    for k, out in enumerate(early):
        window = pl.ds(pl.multiple_of(places[k], LANES), 2 * LANES)
        out[0:heads_rows, :] = px_s[:, window]
        out[heads_rows : heads_rows + 2 * seqs, :] = pair_s[:, window]
        for j in range(width // (2 * LANES)):
            base = heads_rows + (2 + j) * seqs
            out[base : base + seqs, :] = q0[:, j * 2 * LANES : (j + 1) * 2 * LANES]
    copies[3].wait()
    nrm, r_one = center_scale(start + dot(mixed, wm[...]) + row(pack, B_MIX))
    first = nrm * row(pack, GAIN_ONE) + row(pack, SHIFT_ONE)
    low = first.astype(BF)
    acc = first + row(pack, B_OUTER)
    copies[4].wait()
    hidden = gelu(dot(low, wi[...]) + bi[...]).astype(BF)
    copies[5].wait()
    acc = acc + dot(hidden, wo[...])
    nrm, r_two = center_scale(acc)
    packet[:, :width] = (nrm * row(pack, GAIN_TWO) + row(pack, SHIFT_TWO)).astype(BF)
    packet[:, width : 2 * width] = low
    lane = lax.broadcasted_iota(jnp.int32, (seqs, LANES), 1)
    at = lax.broadcasted_iota(jnp.int32, (seqs, LANES), 0)
    wanted = jnp.zeros((seqs, LANES), jnp.int32)
    cluster = jnp.zeros((seqs, LANES), jnp.int32)
    base = place_of(places, planes, "pair")
    for s in range(seqs):
        cluster = jnp.where(at == s, clusters[base + s % pairs], cluster)
        if s < pairs:
            wanted = jnp.where(at == s, target[s], wanted)
    extra = jnp.zeros((seqs, LANES), jnp.int32)
    for j, v in enumerate((wanted // LANES, wanted % LANES, cluster // LANES, cluster % LANES)):
        extra = jnp.where(lane == 6 + j, v, extra)
    extra = extra.astype(F32)
    for j, part in enumerate(split3(r_one) + split3(r_two)):
        extra = jnp.where(lane == j, part.astype(F32), extra)
    packet[:, 2 * width :] = extra.astype(BF)


def vmem():
    return pl.BlockSpec(memory_space=pltpu.VMEM)


def smem():
    return pl.BlockSpec(memory_space=pltpu.SMEM)


def anywhere():
    return pl.BlockSpec(memory_space=pl.ANY)


def params(mib):
    return pltpu.CompilerParams(vmem_limit_bytes=mib * MIB)


def in_hbm(v):
    return pltpu.with_memory_space_constraint(v, pltpu.HBM)


def in_vmem(v):
    return pltpu.with_memory_space_constraint(v, pltpu.VMEM)


def cls_forward(places, query_length, passage_length, positives, clusters, query_tokens, passage_tokens, mats, vectors, planes):
    pairs, query_rows, width = query_tokens.shape
    seqs = 2 * pairs
    tokens = pairs * (query_rows + passage_tokens.shape[1])
    early_rows = seqs * (HEADS + 2 + width // (2 * LANES))
    outs = [
        jax.ShapeDtypeStruct((seqs, 2 * width + LANES), BF),
        pltpu.VMEM((HEADS * seqs, tokens), F32),
        pltpu.VMEM((HEADS * seqs, width), BF),
        jax.ShapeDtypeStruct((8, width), F32),
        jax.ShapeDtypeStruct((1, mats[4].shape[1]), F32),
    ]
    outs += [pltpu.VMEM(v.shape, v.dtype) for v in (*mats, query_tokens, passage_tokens)]
    outs += [jax.ShapeDtypeStruct((early_rows, 2 * LANES), BF)] * planes
    got = pl.pallas_call(
        cls_kernel,
        in_specs=[smem()] * 5 + [anywhere()] * 17,
        out_specs=[vmem()] * len(outs),
        out_shape=outs,
        scratch_shapes=[
            pltpu.VMEM((HEADS * seqs, width), BF),
            pltpu.VMEM((2 * seqs, width), BF),
            *[pltpu.VMEM(v.shape, v.dtype) for v in vectors],
            pltpu.SemaphoreType.DMA((17,)),
        ],
        compiler_params=params(16),
        cost_estimate=pl.CostEstimate(flops=8 * 10**9, bytes_accessed=20 * 10**6, transcendentals=0),
        name="cls_forward",
    )(
        places, *[in_hbm(v) for v in (query_length, passage_length, positives, clusters)],
        in_hbm(query_tokens), in_hbm(passage_tokens), *[in_hbm(m) for m in mats], *[in_hbm(v) for v in vectors],
    )
    kept = [in_vmem(v) for v in got[5:13]]
    return got[:5], kept[:6], kept[6:], got[13:]


def place_planes_kernel(places, *refs):
    *parts, out = refs
    for k, part in enumerate(parts):
        at = places[len(parts) + k]
        out[pl.ds(at // part.shape[0], 1)] = part[...][None]


def place_planes(places, parts):
    shape = (len(parts),) + parts[0].shape
    return pl.pallas_call(
        place_planes_kernel,
        in_specs=[smem()] + [vmem()] * len(parts),
        out_specs=vmem(),
        out_shape=jax.ShapeDtypeStruct(shape, BF),
        compiler_params=params(8),
        name="place_planes",
    )(places, *parts)


def place_square_kernel(planes, places, *refs):
    *parts, out = refs
    y, x = place_of(places, planes, "y"), place_of(places, planes, "x")
    for (dy, dx), part in zip(SQUARE, parts):
        at_y, at_x = (1 - y if dy else y), (1 - x if dx else x)
        out[:, pl.ds(at_y * 2 + at_x, 1)] = part[...][:, None]


def place_square(places, planes, parts):
    v = parts[0]
    out = pl.pallas_call(
        functools.partial(place_square_kernel, planes),
        in_specs=[smem()] + [vmem()] * 4,
        out_specs=vmem(),
        out_shape=jax.ShapeDtypeStruct((planes, 4) + v.shape[1:], BF),
        compiler_params=params(8),
        name="place_square",
    )(places, *parts)
    return out.reshape((-1,) + v.shape[1:])


def norm_back(grad, nrm, r, gain):
    g = grad * gain
    return r * (
        g - jnp.mean(g, axis=-1, keepdims=True) - nrm * jnp.mean(g * nrm, axis=-1, keepdims=True)
    )


def back_kernel(
    planes, slice_first, places, packet_a, packet_b, pack, bi, wq, wk, wv, wm, wi, wo,
    qt, pt, probs_ref, a_ref, *rest,
):
    grad_wo_h, grad_wi_h, vectors, grad_bi, line_att, line_mix, dp_out, ab_out = rest[:8]
    late = rest[8 : 8 + planes]
    grad_wo, grad_wi, packet_s, mix_s, line_s, start_s, own_s, xs_s, win_s, sems = rest[8 + planes :]
    sent = []

    def send(a, b):
        copy = pltpu.make_async_copy(a, b, sems.at[len(sent)])
        copy.start()
        sent.append(copy)

    core = place_of(places, planes, "core")
    packet_s[:, pl.ds(core, 1)] = packet_a[...][:, None]
    packet_s[:, pl.ds(1 - core, 1)] = packet_b[...][:, None]
    pairs, query_rows, width = qt.shape
    passage_rows = pt.shape[1]
    seqs = 2 * pairs
    packet = packet_s[...].reshape(-1, packet_s.shape[-1])
    rows = packet.shape[0]
    scale = 2.0 * width**-0.5

    cls = packet[:, :width]
    tail = packet[:, 2 * width :].astype(F32)
    scores = dot_nt(cls, cls) * scale
    is_query = lax.broadcasted_iota(jnp.int32, (rows, 1), 0) % seqs < pairs
    is_passage = lax.broadcasted_iota(jnp.int32, (1, rows), 1) % seqs >= pairs
    wanted = (tail[:, 6:7] * LANES + tail[:, 7:8]).astype(jnp.int32)
    column = lax.broadcasted_iota(jnp.int32, (1, rows), 1)
    chosen = (column // seqs * pairs + column % pairs == wanted) & is_passage
    across = tail.T
    cluster_row = across[8:9, :] * LANES + across[9:10, :]
    cluster_col = tail[:, 8:9] * LANES + tail[:, 9:10]
    counted = ((cluster_row != cluster_col) | chosen) & is_passage
    masked = jnp.where(counted, scores, -1e30)
    peak = jnp.max(masked, axis=1, keepdims=True)
    log_total = peak + jnp.log(jnp.sum(jnp.exp(masked - peak), axis=1, keepdims=True))
    one = jnp.where(chosen, 1.0, 0.0)
    picked = jnp.sum(one * scores, axis=1, keepdims=True)
    loss = jnp.sum(jnp.where(is_query, log_total - picked, 0.0), axis=0, keepdims=True)
    d_pair = jnp.where(is_query, jnp.exp(masked - log_total) - one, 0.0).astype(BF)
    d_cls = (dot(d_pair, cls) + dot_tn(d_pair, cls)) * scale

    first = packet[:, width : 2 * width]
    nrm_two = (cls.astype(F32) - row(pack, SHIFT_TWO)) / row(pack, GAIN_TWO)
    r_two = tail[:, 3:4] + tail[:, 4:5] + tail[:, 5:6]
    d_second = norm_back(d_cls, nrm_two, r_two, row(pack, GAIN_TWO))
    d_outer = d_second.astype(BF)
    vectors[0:1, :] = jnp.sum(d_outer.astype(F32), axis=0, keepdims=True)
    vectors[1:2, :] = jnp.sum(d_cls * nrm_two, axis=0, keepdims=True)
    vectors[2:3, :] = jnp.sum(d_cls, axis=0, keepdims=True)
    piece = grad_wi.shape[0]
    first_window = pl.ds(
        pl.multiple_of(place_of(places, planes, "first_off"), LANES), 2 * LANES
    )
    mix_s[...] = first
    first_piece = mix_s[:, first_window]
    inside = pl.ds(pl.multiple_of(place_of(places, planes, "first_inside"), 8), piece)
    line = pl.ds(place_of(places, planes, "line"), 1)
    line_rows = planes * seqs
    by_line = (planes, rows // line_rows, seqs, width)
    start_s[...] = d_second.reshape(by_line)
    d_first = start_s[:, line].reshape(line_rows, width)
    for j in range(wi.shape[1] // width):
        cols = slice(j * width, (j + 1) * width)
        inner = dot(first, wi[:, cols]) + bi[:, cols]
        d_inner = (dot_nt(d_outer, wo[cols, :]) * gelu_slope(inner)).astype(BF)
        line_s[...] = d_inner.reshape(by_line)
        d_first = d_first + dot_nt(line_s[:, line].reshape(line_rows, width), wi[:, cols])
        found = dot_tn(first_piece, d_inner)
        if slice_first:
            win_s[: 2 * LANES, :] = found
            found = win_s[inside, :]
        grad_wi[:, cols] = found
        send(grad_wi.at[:, cols], grad_wi_h.at[:, cols])
        grad_bi[:, cols] = jnp.sum(d_inner.astype(F32), axis=0, keepdims=True)
    size = grad_wo.shape[0]
    off = pl.multiple_of(place_of(places, planes, "hidden_off"), LANES)
    window = pl.ds(off, window_size(size))
    hidden = gelu(dot(first, wi[:, window]) + bi[:, window]).astype(BF)
    found = dot_tn(hidden, d_outer)
    if size != window_size(size):
        win_s[: window_size(size), :] = found
        found = win_s[pl.ds(pl.multiple_of(place_of(places, planes, "hidden_inside"), 8), size), :]
    grad_wo[...] = found
    send(grad_wo, grad_wo_h)
    at_line = place_of(places, planes, "line")
    lined = jnp.concatenate(
        [
            packet_s[pl.ds(p * 4 + at_line // 2, 1), pl.ds(at_line % 2, 1)].reshape(seqs, -1)
            for p in range(planes)
        ],
        0,
    )
    nrm_one = (lined[:, width : 2 * width].astype(F32) - row(pack, SHIFT_ONE)) / row(pack, GAIN_ONE)
    tail = lined[:, 2 * width :].astype(F32)
    r_one = tail[:, 0:1] + tail[:, 1:2] + tail[:, 2:3]
    d_start = norm_back(d_first, nrm_one, r_one, row(pack, GAIN_ONE))
    vectors[3:4, :] = jnp.sum(d_first * nrm_one, axis=0, keepdims=True)
    vectors[4:5, :] = jnp.sum(d_first, axis=0, keepdims=True)
    d_attended = d_start.astype(BF)
    vectors[5:6, :] = jnp.sum(d_attended.astype(F32), axis=0, keepdims=True)
    d_mixed = dot_nt(d_attended, wm[...]).astype(BF)
    vectors[6:7, :] = jnp.sum(d_mixed.astype(F32), axis=0, keepdims=True)
    vectors[7:8, :] = jnp.broadcast_to(loss * (2.0 / rows), (1, width))
    line_att[...] = d_attended
    line_mix[...] = d_mixed

    own = pl.ds(pl.multiple_of(places[planes], seqs), seqs)
    own_s[...] = d_start
    own_start = own_s[own, :]
    own_mixed = line_mix[own, :]
    bm = dot_nt(expand_heads(own_mixed), wv[...]).astype(BF)
    xq = qt[...].reshape(pairs * query_rows, width)
    xp = pt[...].reshape(pairs * passage_rows, width)
    d_probs = jnp.concatenate([dot_nt(bm, xq), dot_nt(bm, xp)], 1)
    probs = probs_ref[...]
    d_scores = (probs * (d_probs - jnp.sum(probs * d_probs, axis=-1, keepdims=True))).astype(BF)
    cut = pairs * query_rows
    xs = (dot(d_scores[:, :cut], xq) + dot(d_scores[:, cut:], xp)).astype(BF)
    xs_s[...] = xs
    d_query = (collapse_heads(dot(xs, wk[...])) * HEAD**-0.5).astype(BF)
    heads_rows = HEADS * seqs
    for k, out in enumerate(late):
        window = pl.ds(pl.multiple_of(places[k], LANES), 2 * LANES)
        out[0:heads_rows, :] = xs_s[:, window]
        for j in range(width // (2 * LANES)):
            base = heads_rows + j * seqs
            out[base : base + seqs, :] = d_query[:, j * 2 * LANES : (j + 1) * 2 * LANES]
    dp_out[0:heads_rows, :] = d_scores
    dp_out[heads_rows : 2 * heads_rows, :] = probs.astype(BF)
    shape = (seqs, dp_out.shape[1])
    seq = lax.broadcasted_iota(jnp.int32, shape, 0)
    first_row = jnp.where(seq < pairs, seq * query_rows, cut + (seq - pairs) * passage_rows)
    first_row = jnp.where(lax.broadcasted_iota(jnp.int32, shape, 1) == first_row, 1.0, 0.0).astype(BF)
    ab_out[0:heads_rows, :] = a_ref[...]
    ab_out[heads_rows : 2 * heads_rows, :] = bm
    at_start = dot_nt(d_query, wq[...]) + own_start
    for j, part in enumerate(split3(at_start)):
        rows_of = slice(2 * heads_rows + j * seqs, 2 * heads_rows + (j + 1) * seqs)
        ab_out[rows_of, :] = part
        dp_out[rows_of, :] = first_row
    for copy in sent:
        copy.wait()


def cls_backward(places, packet_a, packet_b, pack, bi, mats, query_tokens, passage_tokens, probs, a, planes, batch_count):
    pairs, _, width = query_tokens.shape
    seqs = 2 * pairs
    blocks = packet_a.shape[0]
    rows = 2 * blocks * seqs
    late_rows = seqs * (HEADS + width // (2 * LANES))
    factors = (2 * HEADS + 3) * seqs
    hidden = mats[4].shape[1]
    first_rows, hidden_rows = width // batch_count, hidden // batch_count
    slice_first = first_rows % 8 == 0

    def out(shape, kind):
        return jax.ShapeDtypeStruct(shape, kind)

    outs = [
        pltpu.HBM((hidden_rows, width), F32),
        pltpu.HBM((first_rows if slice_first else 2 * LANES, hidden), F32),
        out((8, width), F32),
        out((1, hidden), F32),
        out((planes * seqs, width), BF),
        out((planes * seqs, width), BF),
        pltpu.VMEM((factors, probs.shape[1]), BF),
        pltpu.VMEM((factors, width), BF),
    ] + [out((late_rows, 2 * LANES), BF)] * planes
    got = pl.pallas_call(
        functools.partial(back_kernel, planes, slice_first),
        in_specs=[smem()] + [vmem()] * 14,
        out_specs=[anywhere()] * 2 + [vmem()] * (len(outs) - 2),
        out_shape=outs,
        scratch_shapes=[
            pltpu.VMEM(outs[0].shape, F32),
            pltpu.VMEM(outs[1].shape, F32),
            pltpu.VMEM((blocks, 2) + packet_a.shape[1:], BF),
            pltpu.VMEM((rows, width), BF),
            pltpu.VMEM((planes, rows // (planes * seqs), seqs, width), BF),
            pltpu.VMEM((planes, rows // (planes * seqs), seqs, width), F32),
            pltpu.VMEM((planes * seqs, width), F32),
            pltpu.VMEM((HEADS * seqs, width), BF),
            pltpu.VMEM((2 * LANES, width), F32),
            pltpu.SemaphoreType.DMA((hidden // width + 1,)),
        ],
        compiler_params=params(22),
        cost_estimate=pl.CostEstimate(flops=16 * 10**9, bytes_accessed=25 * 10**6, transcendentals=0),
        name="cls_backward",
    )(
        places, packet_a, packet_b, pack, bi, *mats,
        query_tokens, passage_tokens, in_vmem(probs), in_vmem(a),
    )
    return got[:8], got[8:]


def plain_backward(places, packet_a, packet_b, pack, bi, mats, query_tokens, passage_tokens, probs, a, planes, batch_count):
    wq, wk, wv, wm, wi, wo = mats
    pairs, query_rows, width = query_tokens.shape
    seqs = 2 * pairs
    blocks = packet_a.shape[0]
    rows = 2 * blocks * seqs
    cut = pairs * query_rows
    hidden = wi.shape[1]

    def at(name):
        return places[2 * planes + PLACES.index(name)]

    core = at("core")
    packet = jnp.stack(
        [jnp.where(core == 0, packet_a, packet_b), jnp.where(core == 0, packet_b, packet_a)], 1
    )
    packet = packet.reshape(2 * blocks, seqs, -1)
    cls_query = packet[:, :pairs, :width].reshape(-1, width)
    cls_passage = packet[:, pairs:, :width].reshape(-1, width)
    packet = packet.reshape(rows, -1)
    tail = packet[:, 2 * width :].astype(F32)

    def sides(v):
        v = v.reshape(2 * blocks, seqs)
        return v[:, :pairs].reshape(-1), v[:, pairs:].reshape(-1)

    scale = 2.0 * width**-0.5
    scores = dot_nt(cls_query, cls_passage) * scale
    wanted = sides(tail[:, 6] * LANES + tail[:, 7])[0]
    query_cluster, passage_cluster = sides(tail[:, 8] * LANES + tail[:, 9])
    chosen = jnp.arange(scores.shape[1], dtype=F32)[None] == wanted[:, None]
    counted = (query_cluster[:, None] != passage_cluster[None]) | chosen
    masked = jnp.where(counted, scores, -1e30)
    log_total = jax.nn.logsumexp(masked, axis=1, keepdims=True)
    one = chosen.astype(F32)
    loss = jnp.sum(log_total - jnp.sum(one * scores, axis=1, keepdims=True))
    d_pair = (jnp.exp(masked - log_total) - one).astype(BF)
    d_cls = jnp.concatenate(
        [
            dot(d_pair, cls_passage).reshape(2 * blocks, pairs, width),
            dot_tn(d_pair, cls_query).reshape(2 * blocks, pairs, width),
        ],
        1,
    ).reshape(rows, width) * scale
    first = packet[:, width : 2 * width]
    nrm_two = (packet[:, :width].astype(F32) - row(pack, SHIFT_TWO)) / row(pack, GAIN_TWO)
    nrm_one = (first.astype(F32) - row(pack, SHIFT_ONE)) / row(pack, GAIN_ONE)
    d_second = norm_back(
        d_cls, nrm_two, jnp.sum(tail[:, 3:6], 1, keepdims=True), row(pack, GAIN_TWO)
    )
    d_outer = d_second.astype(BF)
    hidden_rows, first_rows = hidden // batch_count, width // batch_count
    hidden_at = at("hidden_off") + at("hidden_inside")
    first_at = at("first_off") + at("first_inside")
    wi_piece = lax.dynamic_slice_in_dim(wi, hidden_at, hidden_rows, 1)
    bi_piece = lax.dynamic_slice_in_dim(bi, hidden_at, hidden_rows, 1)

    def block(parts):
        first, d_outer = parts
        d_inner = (dot_nt(d_outer, wo) * gelu_slope(dot(first, wi) + bi)).astype(BF)
        return d_inner, dot_nt(d_inner, wi), gelu(dot(first, wi_piece) + bi_piece).astype(BF)

    size = rows // 8
    parts = first.reshape(-1, size, width), d_outer.reshape(-1, size, width)
    d_inner, more, hidden_piece = (v.reshape(rows, -1) for v in lax.map(block, parts))
    d_first = d_second + more
    first_piece = lax.dynamic_slice_in_dim(first, first_at, first_rows, 1)
    grad_wo, grad_wi = dot_tn(hidden_piece, d_outer), dot_tn(first_piece, d_inner)
    if first_rows % 8:
        grad_wi = lax.dynamic_update_slice_in_dim(
            jnp.zeros((2 * LANES, hidden), F32), grad_wi, at("first_inside"), 0
        )
    d_start = norm_back(
        d_first, nrm_one, jnp.sum(tail[:, 0:3], 1, keepdims=True), row(pack, GAIN_ONE)
    )
    d_attended = d_start.astype(BF)
    d_mixed = dot_nt(d_attended, wm).astype(BF)
    def line(v):
        v = v.reshape(planes, -1, seqs, width)
        return lax.dynamic_slice_in_dim(v, at("line"), 1, 1).reshape(planes * seqs, width)

    sums = (d_outer, d_cls * nrm_two, d_cls)
    sums += tuple(line(v) for v in (d_first * nrm_one, d_first, d_attended, d_mixed))
    vectors = [jnp.sum(v.astype(F32), 0) for v in sums] + [jnp.full((width,), loss * (2.0 / rows))]

    def own(v):
        return lax.dynamic_slice_in_dim(v, at("own"), seqs, 0)

    bm = dot_nt(expand_heads(own(d_mixed)), wv).astype(BF)
    xq = query_tokens.reshape(-1, width)
    xp = passage_tokens.reshape(-1, width)
    d_probs = jnp.concatenate([dot_nt(bm, xq), dot_nt(bm, xp)], 1)
    d_scores = (probs * (d_probs - jnp.sum(probs * d_probs, axis=-1, keepdims=True))).astype(BF)
    xs = (dot(d_scores[:, :cut], xq) + dot(d_scores[:, cut:], xp)).astype(BF)
    d_query = (collapse_heads(dot(xs, wk)) * HEAD**-0.5).astype(BF)
    blocks_of_query = [
        d_query[:, j : j + 2 * LANES] for j in range(0, width, 2 * LANES)
    ]
    late = [
        jnp.concatenate(
            [lax.dynamic_slice_in_dim(xs, places[k], 2 * LANES, 1)] + blocks_of_query
        )
        for k in range(planes)
    ]
    at_start = [lax.reduce_precision(dot_nt(d_query, wq) + own(d_start), 8, 23)]
    for _ in range(2):
        high = lax.reduce_precision(at_start[-1], 8, 7)
        at_start[-1:] = [high, at_start[-1] - high]
    seq = jnp.arange(seqs)
    first_row = jnp.where(seq < pairs, seq * query_rows, cut + (seq - pairs) * passage_tokens.shape[1])
    first_row = (jnp.arange(probs.shape[1])[None] == first_row[:, None]).astype(BF)
    dp = jnp.concatenate([d_scores, probs.astype(BF)] + [first_row] * 3)
    ab = jnp.concatenate([a, bm] + [v.astype(BF) for v in at_start])
    return (
        grad_wo, grad_wi, jnp.stack(vectors), jnp.sum(d_inner.astype(F32), 0, keepdims=True),
        line(d_attended), line(d_mixed), dp, ab,
    ), late


def tokens_kernel(first, moves, dp, ab, *refs):
    near, (out, *far), (stage, sems) = refs[:moves], refs[moves : 2 * moves + 1], refs[-2:]
    copies = [pltpu.make_async_copy(a, b, sems.at[i]) for i, (a, b) in enumerate(zip(near, far))]
    for c in copies:
        c.start()
    size = stage.shape[1]
    for n in range(stage.shape[0]):
        cols = slice(first + n * size, first + (n + 1) * size)
        stage[n] = dot_tn(dp[:, cols], ab[...])
        copy = pltpu.make_async_copy(
            stage.at[n], out.at[pl.ds(n * size, size)], sems.at[moves + n]
        )
        copy.start()
        copies.append(copy)
    for c in copies:
        c.wait()


def token_grads(dp, ab, first, rows, near):
    width = ab.shape[1]
    chunks = rows // (2 * LANES)
    moves = len(near)
    return pl.pallas_call(
        functools.partial(tokens_kernel, first, moves),
        in_specs=[vmem()] * 2 + [anywhere()] * moves,
        out_specs=[anywhere()] * (1 + moves),
        out_shape=[pltpu.HBM((rows, width), F32)] + [pltpu.HBM(v.shape, BF) for v in near],
        scratch_shapes=[
            pltpu.VMEM((chunks, 2 * LANES, width), F32),
            pltpu.SemaphoreType.DMA((moves + chunks,)),
        ],
        compiler_params=params(16),
        cost_estimate=pl.CostEstimate(
            flops=rows * 800 * width, bytes_accessed=rows * width * 6, transcendentals=0
        ),
        name="token_grads",
    )(in_vmem(dp), in_vmem(ab), *[in_vmem(v) for v in near])


def sums_kernel(places, vectors, line_att, line_mix, *rest):
    planes = (len(rest) - 3) // 2
    early, late = rest[:planes], rest[planes : 2 * planes]
    mine, other, win = rest[2 * planes :]
    width = line_att.shape[1]
    wide = 2 * LANES
    seqs = line_att.shape[0] // planes
    heads_rows = HEADS * seqs

    def unfold(ref, base):
        return jnp.concatenate(
            [ref[base + j * seqs : base + (j + 1) * seqs, :] for j in range(width // wide)], 1
        )

    xs, px, starts, mixed, q0, dq, dm, da = ([] for _ in range(8))
    for k in range(planes):
        e, l = early[k], late[k]
        at = pl.ds(pl.multiple_of(places[planes + k], seqs), seqs)
        px.append(e[0:heads_rows, :])
        starts.append(e[heads_rows : heads_rows + seqs, :])
        mixed.append(e[heads_rows + seqs : heads_rows + 2 * seqs, :])
        q0.append(expand_heads(unfold(e, heads_rows + 2 * seqs)))
        xs.append(l[0:heads_rows, :])
        dq.append(unfold(l, heads_rows))
        dm.append(expand_heads(line_mix[at, :]))
        da.append(line_att[at, :])
    cat = functools.partial(jnp.concatenate, axis=0)
    dq = cat(dq)
    found = (
        dot_tn(cat(starts), dq),
        dot_tn(cat(xs), cat(q0)) * HEAD**-0.5,
        dot_tn(cat(px), cat(dm)),
        dot_tn(cat(mixed), cat(da)),
    )
    bias = [jnp.sum(dq.astype(F32), axis=0, keepdims=True), vectors[3:7, :]]
    bias = jnp.concatenate(bias + [jnp.zeros((11, width), F32)], 0)
    slab = (mine.shape[0] - 16) // 4
    half = width // 2
    inside = pl.ds(pl.multiple_of(place_of(places, planes, "inside"), 8), slab)
    is_low = place_of(places, planes, "core") == 0
    for i in range(5):
        if i < 4:
            win[...] = found[i]
            v = win[inside, :]
        else:
            v = bias
        to = slice(i * slab, i * slab + v.shape[0])
        a, b = v[:, :half], v[:, half:]
        mine[to, :] = jnp.where(is_low, a, b)
        other[to, :] = jnp.where(is_low, b, a).astype(BF)


def partial_sums(places, vectors, line_att, line_mix, early, late, slab):
    width = line_att.shape[1]
    shape = (4 * slab + 16, width // 2)
    return pl.pallas_call(
        sums_kernel,
        in_specs=[smem()] + [vmem()] * (3 + 2 * len(early)),
        out_specs=[vmem()] * 2,
        out_shape=[jax.ShapeDtypeStruct(shape, F32), jax.ShapeDtypeStruct(shape, BF)],
        scratch_shapes=[pltpu.VMEM((2 * LANES, width), F32)],
        compiler_params=params(12),
        cost_estimate=pl.CostEstimate(flops=2 * 10**9, bytes_accessed=4 * 10**6, transcendentals=0),
        name="partial_sums",
    )(places, vectors, line_att, line_mix, *early, *late)


def fold_kernel(planes, places, mine, got, keep, send):
    total = mine[...] + got[...].astype(F32)
    slab = (mine.shape[0] - 16) // 4
    small = slab // 2
    is_low = place_of(places, planes, "y") == 0
    for i in range(5):
        base = i * slab
        if i < 4:
            a, b = total[base : base + small], total[base + small : base + slab]
            v, w = jnp.where(is_low, a, b), jnp.where(is_low, b, a)
        else:
            v = w = total[base : base + 16]
        to = slice(i * small, i * small + v.shape[0])
        keep[to, :] = v
        send[to, :] = w.astype(BF)


def fold(places, planes, mine, got):
    rows = (mine.shape[0] - 16) // 2 + 16
    shape = (rows, mine.shape[1])
    return pl.pallas_call(
        functools.partial(fold_kernel, planes),
        in_specs=[smem()] + [vmem()] * 2,
        out_specs=[vmem()] * 2,
        out_shape=[jax.ShapeDtypeStruct(shape, F32), jax.ShapeDtypeStruct(shape, BF)],
        compiler_params=params(8),
        name="fold",
    )(places, mine, got)


def add_kernel(a, b, out):
    out[...] = (a[...].astype(F32) + b[...].astype(F32)).astype(BF)


def add_low(a, b):
    return pl.pallas_call(
        add_kernel,
        in_specs=[vmem()] * 2,
        out_specs=vmem(),
        out_shape=jax.ShapeDtypeStruct(a.shape, BF),
        compiler_params=params(8),
        name="add_low",
    )(a, b)


def take_lanes(v, off, inside, size):
    wide = min(v.shape[1], window_size(size) if size % LANES == 0 else 2 * LANES)
    v = v[:, pl.ds(pl.multiple_of(off, LANES), wide)]
    if wide != size:
        v = pltpu.roll(v, jnp.where(inside == 0, 0, wide - inside), 1)
    return v[:, :size]


def final_kernel(planes, places, mine, got, sums, grad_bi, *rest):
    matrices, small_outs, (bi_out, loss, both) = rest[:4], rest[4:12], rest[12:]
    is_low = place_of(places, planes, "core") == 0
    a, b = mine[...].astype(F32), got[...].astype(F32)
    half = a.shape[1]
    both[:, :half] = jnp.where(is_low, a, b)
    both[:, half:] = jnp.where(is_low, b, a)
    small = matrices[0].shape[0]
    for i, out in enumerate(matrices):
        out[...] = both[i * small : (i + 1) * small]
    first = place_of(places, planes, "first_off"), place_of(places, planes, "first_inside")
    hidden = place_of(places, planes, "hidden_off"), place_of(places, planes, "hidden_inside")
    found = take_lanes(sums, *first, small)
    bias = take_lanes(both.at[4 * small : 4 * small + 8], *first, small)
    for i, out in enumerate(small_outs):
        at = 0 if i == 7 else i - 2
        v = found[i : i + 1] if i < 3 else bias[at : at + 1]
        out[...] = v.reshape(small)
    size = bi_out.shape[0]
    bi_out[...] = take_lanes(grad_bi, *hidden, size)[:1].reshape(size)
    loss[...] = sums[7:8, :LANES].reshape(LANES)


def finish(places, planes, mine, got, sums, grad_bi, hidden_rows):
    small = (mine.shape[0] - 16) // 4
    width = 2 * mine.shape[1]
    shapes = [jax.ShapeDtypeStruct((small, width), F32)] * 4
    shapes += [jax.ShapeDtypeStruct((small,), F32)] * 8
    shapes += [jax.ShapeDtypeStruct((hidden_rows,), F32), jax.ShapeDtypeStruct((LANES,), F32)]
    got = pl.pallas_call(
        functools.partial(final_kernel, planes),
        in_specs=[smem()] + [vmem()] * 4,
        out_specs=[vmem()] * len(shapes),
        out_shape=shapes,
        scratch_shapes=[pltpu.VMEM((mine.shape[0], width), F32)],
        compiler_params=params(8),
        name="finish",
    )(places, mine, got, sums, grad_bi)
    return got[:4], got[4:12], got[12], got[13][0]


def permute(v, count, move):
    return lax.ppermute(v, AXES, [(i, move(i)) for i in range(count)])


def from_planes(parts, count):
    return [parts[0]] + [
        permute(parts[k], count, lambda i: (i + 8 * k) % count) for k in range(1, len(parts))
    ]


def gather_pair(v, count, bit, mine):
    got = permute(v, count, lambda i: i ^ bit)
    out = jnp.zeros((2,) + v.shape, v.dtype)
    out = lax.dynamic_update_slice_in_dim(out, v[None], mine, 0)
    return lax.dynamic_update_slice_in_dim(out, got[None], 1 - mine, 0)


def after(v, *others):
    return lax.optimization_barrier((v,) + others)[0]


def body(
    query_tokens, passage_tokens, query_length, passage_length, clusters, positives,
    w_query, b_query, w_key, w_value, b_value, w_mix, b_mix, gain_one, shift_one,
    w_inner, b_inner, w_outer, b_outer, gain_two, shift_two,
):
    pairs, query_rows, width = query_tokens.shape
    passage_rows = passage_tokens.shape[1]
    seqs = 2 * pairs
    batch_count = lax.axis_size("batch")
    count = batch_count * lax.axis_size("rep")
    planes = count // 8
    slab = width // planes
    me = lax.axis_index(AXES)
    z, y, x, core = me // 8, me // 4 % 2, me // 2 % 2, me % 2
    mats = whole_mats = (w_query, w_key, w_value, w_mix, w_inner, w_outer)
    vectors = (b_query, b_value, b_mix, gain_one, shift_one, b_outer, gain_two, shift_two, b_inner)
    batch_index = lax.axis_index("batch")
    first_rows, hidden_rows = width // batch_count, w_inner.shape[1] // batch_count

    def window(at, total, size):
        return jnp.minimum(at // LANES * LANES, total - size)

    slot = jnp.arange(2 * planes + len(PLACES), dtype=jnp.int32)
    places = jnp.where(
        slot < planes,
        window((z + slot) % planes * slab, width, 2 * LANES),
        (z - slot) % planes * seqs,
    )
    first_at, hidden_at = batch_index * first_rows, batch_index * hidden_rows
    first_off = window(first_at, width, 2 * LANES)
    hidden_off = window(hidden_at, w_inner.shape[1], window_size(hidden_rows))
    found = dict(
        own=me * seqs, line=me % 8, core=core, y=y, x=x,
        inside=z * slab - window(z * slab, width, 2 * LANES),
        first_off=first_off, first_inside=first_at - first_off,
        hidden_off=hidden_off, hidden_inside=hidden_at - hidden_off, pair=me * pairs,
    )
    for i, name in enumerate(PLACES):
        places = jnp.where(slot == 2 * planes + i, found[name], places)
    places = places.astype(jnp.int32)

    (packet, probs, a, pack, bi), mats, (near_query, near_passage), early = cls_forward(
        places, query_length, passage_length, positives, clusters,
        query_tokens, passage_tokens, mats, vectors, planes,
    )
    done = [None]

    def run(start, size, wait_for=None):
        lengths = passage_length
        if wait_for is not None:
            lengths, wait_for = lax.optimization_barrier((lengths, wait_for))
        done[0] = forward(near_passage, lengths, pack, bi, mats, False, start, size, done[0])
        return wait_for

    def hold(v):
        v, done[0] = lax.optimization_barrier((v, done[0]))
        return v

    def backward(packet_a, packet_b):
        if 2 * packet_a.shape[0] * seqs <= KERNEL_ROWS:
            return cls_backward(
                places, packet_a, packet_b, pack, bi, mats, near_query, near_passage, probs, a, planes, batch_count
            )
        return plain_backward(
            places, packet_a, packet_b, pack, bi, whole_mats, query_tokens, passage_tokens, probs, a, planes, batch_count
        )

    parts = from_planes([packet] * planes, count)
    cuts = [pairs * i // 4 for i in (1, 2, 3)]
    run(0, cuts[0])
    parts[-1] = hold(parts[-1])
    packet = place_planes(places, parts)
    packet = run(cuts[0], cuts[1] - cuts[0], packet)
    early = list(early)
    early[0], packet = lax.optimization_barrier((early[0], packet))
    parts = [packet] + [
        permute(packet, count, lambda i: i ^ (4 * dy + 2 * dx)) for dy, dx in SQUARE[1:]
    ]
    early = from_planes(early, count)
    parts[-1] = hold(parts[-1])
    parts[-1], early[-1] = lax.optimization_barrier((parts[-1], early[-1]))
    packet = place_square(places, planes, parts)
    got = permute(packet, count, lambda i: i ^ 1)
    (
        (grad_w_outer, grad_w_inner, sums, grad_b_inner, line_att, line_mix, dp, ab),
        late,
    ) = backward(packet, got)
    if grad_w_inner.shape[0] != first_rows:
        grad_w_inner = lax.dynamic_slice_in_dim(
            grad_w_inner, first_at - first_off, first_rows, 0
        )

    late = list(late)
    late[0] = run(cuts[1], cuts[2] - cuts[1], late[0])
    late = from_planes(late, count)
    late[-1] = hold(late[-1])
    mine, other = partial_sums(places, sums, line_att, line_mix, early, late, slab)
    got = permute(other, count, lambda i: i ^ 1)
    ab, mine = lax.optimization_barrier((ab, mine))
    (query_grad,) = token_grads(dp, ab, 0, pairs * query_rows, [])
    got, query_grad = lax.optimization_barrier((got, query_grad))
    mine, other = fold(places, planes, mine, got)
    other = run(cuts[2], pairs - cuts[2], other)
    got = hold(permute(other, count, lambda i: i ^ 4))
    passage_out = done[0]
    mine = add_low(mine, got)
    lengths, mine = lax.optimization_barrier((query_length, mine))
    query_out, passage_out = forward(
        near_query, lengths, pack, bi, mats, True, 0, pairs, passage_out
    )
    got = permute(mine, count, lambda i: i ^ 2)
    got, query_out = lax.optimization_barrier((got, query_out))
    mine = add_low(mine, got)
    ab, mine = lax.optimization_barrier((ab, mine))
    passage_grad, query_out = token_grads(
        dp, ab, pairs * query_rows, pairs * passage_rows, [query_out]
    )
    got = permute(mine, count, lambda i: i ^ 1)
    matrices, small, grad_b_inner, loss = finish(
        places, planes, mine, got, sums, grad_b_inner, hidden_rows
    )
    grad_w_query, grad_w_key, grad_w_value, grad_w_mix = matrices
    b_outer, gain_two, shift_two, gain_one, shift_one, b_mix, b_value, b_query = small
    return (
        query_out, passage_out, loss,
        query_grad.reshape(query_tokens.shape), passage_grad.reshape(passage_tokens.shape),
        grad_w_query, b_query, grad_w_key, grad_w_value, b_value,
        grad_w_mix, b_mix, gain_one, shift_one, grad_w_inner, grad_b_inner,
        grad_w_outer, b_outer, gain_two, shift_two,
    )


def solution(mesh):
    rows = P(AXES, None, None)
    vector, matrix = P("batch"), P("batch", None)
    return jax.shard_map(
        body,
        mesh=mesh,
        in_specs=(rows, rows, P(AXES), P(AXES), P(), P(AXES)) + (P(),) * 15,
        out_specs=(
            rows, rows, P(), rows, rows,
            matrix, vector, matrix, matrix, vector,
            matrix, vector, vector, vector, matrix, vector,
            matrix, vector, vector, vector,
        ),
        check_vma=False,
    )
```
